32 devices in a mesh: stream: 2 (over x), dp: 16 (over z, y, core).
Axes of the slice: x: 2, y: 2, z: 4, core: 2. Of those that a mesh axis runs over, the one named last changes fastest.
Arguments:
- short_tokens: bfloat16 [2, 128, 32, 512], P('stream', 'dp'), may hold values from -6 to 6
- long_tokens: bfloat16 [2, 128, 128, 512], P('stream', 'dp'), may hold values from -6 to 6
- short_len: int32 [2, 128], P('stream', 'dp'), may hold values from 2 to 32, as said below
- long_len: int32 [2, 128], P('stream', 'dp'), may hold values from 33 to 128, as said below
- pair_index: int32 [256], replicated, may hold values from 0 to 255, each once
- w_qkv: bfloat16 [2, 512, 1536], replicated, may hold values from -0.25 to 0.25
- b_qv: float32 [2, 1024], replicated, may hold values from -1.8 to 1.8
- w_out: bfloat16 [2, 512, 512], replicated, may hold values from -1 to 1
- b_resid: float32 [2, 1024], replicated, may hold values from -1.8 to 1.8
- norm_gain: float32 [2, 1024], replicated, may hold values from 0.5 to 1.5
- norm_bias: float32 [2, 1024], replicated, may hold values from -1.8 to 1.8
- w_in: bfloat16 [2, 512, 2048], replicated, may hold values from -0.25 to 0.25
- b_in: float32 [2, 2048], replicated, may hold values from -1.8 to 1.8
- w_back: bfloat16 [2, 2048, 512], replicated, may hold values from -0.125 to 0.125
Outputs:
- grad_w_qkv: float32 [2, 512, 1536], replicated
- grad_b_qv: float32 [2, 1024], replicated
- grad_w_out: float32 [2, 512, 512], replicated
- grad_b_resid: float32 [2, 1024], replicated
- grad_norm_gain: float32 [2, 1024], replicated
- grad_norm_bias: float32 [2, 1024], replicated
- grad_w_in: float32 [2, 512, 2048], replicated
- grad_b_in: float32 [2, 2048], replicated
- grad_w_back: float32 [2, 2048, 512], replicated
- grad_short: float32 [2, 128, 32, 512], P('stream', 'dp')
- grad_long: float32 [2, 128, 128, 512], P('stream', 'dp')
The draws below stay inside these ranges and needn't reach their ends.
Inputs may be any that keep to these rules, and one draw needn't show every extreme that they name: `short_len`: lengths in the short bucket; the first short sentence of every data device has all 32 tokens. `long_len`: lengths in the long bucket; on each side some long sentence has all 128 tokens. A permutation: source sentence i and target sentence pair_index[i] are translations; on either side sentences are numbered data device by data device, on each its 8 short ones and then its 8 long ones.
All inputs are finite; a program needn't handle non-finite values.
Results may differ from the reference program's by a relative error of at most 0.023.
Values may be sent and summed in bfloat16 or wider, within the bound.
No kernel may reach another device: no remote copies, remote signals or barrier semaphores. Data moves between devices by JAX's collectives and lax.ppermute only.
A program may use at most 192 MiB of HBM per device.

```python
import math
import jax
import jax.numpy as jnp
from jax import lax

D = 512
HEADS = 8
FF = 2048
LAYERS = 2
SHORT = 32
LONG = 128
SHORT_DEV = 8
LONG_DEV = 8
NSHORT = 128
NLONG = 128
NPAIRS = 256
N_DP = 16


def draw_short_len(key, part):
    key = jax.random.fold_in(key, 11)
    drawn = jax.random.randint(key, (2, NSHORT), 2, SHORT + 1)
    leading = jnp.arange(NSHORT) % SHORT_DEV == 0
    return jnp.where(leading[None, :], SHORT, drawn).astype(jnp.int32)


def draw_long_len(key, part):
    key = jax.random.fold_in(key, 23)
    length_key, place_key = jax.random.split(key)
    drawn = jax.random.randint(length_key, (2, NLONG), SHORT + 1, LONG + 1)
    chosen = jax.random.randint(place_key, (2, 1), 0, NLONG)
    leading = jnp.arange(NLONG)[None, :] == chosen
    return jnp.where(leading, LONG, drawn).astype(jnp.int32)


def block_scale(own_key, shape, cuts, smallest, largest):
    def one(position, parts):
        steps = jax.random.uniform(jax.random.fold_in(jax.random.fold_in(own_key, 6), position), (parts,), jnp.float32, smallest / len(cuts), largest / len(cuts))
        return jnp.repeat(jnp.exp(steps), shape[position] // parts).reshape((-1,) + (1,) * (len(shape) - position - 1))

    factor_of = one(*cuts[0])
    for cut in cuts[1:]:
        factor_of = factor_of * one(*cut)
    return factor_of


def gaussian(key, shape, scale, reach, cuts=(), held_as=jnp.bfloat16):
    gain = block_scale(key, shape, cuts, -0.22, 0.18) if cuts else 1.0
    values = jax.random.normal(key, shape, jnp.float32) * scale * gain
    return jnp.minimum(jnp.maximum(values, -reach), reach).astype(held_as)


def setup_inputs(seed: int = 0) -> dict:
    keys = jax.random.split(jax.random.key(seed), 15)
    short_tokens = gaussian(keys[0], (2, NSHORT, SHORT, D), 1.0, 6.0, ((0, 2), (1, 16)))
    long_tokens = gaussian(keys[1], (2, NLONG, LONG, D), 1.0, 6.0, ((0, 2), (1, 16)))
    short_len = draw_short_len(jax.random.fold_in(keys[14], 71), 0)
    long_len = draw_long_len(jax.random.fold_in(keys[14], 71), 0)
    pair_index = jax.random.permutation(keys[4], NPAIRS).astype(jnp.int32)
    w_qkv = gaussian(keys[5], (LAYERS, D, 3 * D), D ** -0.5, 0.25)
    b_qv = gaussian(keys[6], (LAYERS, 2 * D), 0.3, 1.8, (), jnp.float32)
    w_out = gaussian(keys[7], (LAYERS, D, D), (D // 16) ** -0.5, 1.0)
    b_resid = gaussian(keys[8], (LAYERS, 2 * D), 0.3, 1.8, (), jnp.float32)
    norm_gain = jnp.clip(1.0 + 0.1 * jax.random.normal(keys[9], (LAYERS, 2 * D), jnp.float32), 0.5, 1.5)
    norm_bias = gaussian(keys[10], (LAYERS, 2 * D), 0.3, 1.8, (), jnp.float32)
    w_in = gaussian(keys[11], (LAYERS, D, FF), D ** -0.5, 0.25)
    b_in = gaussian(keys[12], (LAYERS, FF), 0.3, 1.8, (), jnp.float32)
    w_back = gaussian(keys[13], (LAYERS, FF, D), FF ** -0.5, 0.125)
    return dict(short_tokens=short_tokens, long_tokens=long_tokens, short_len=short_len, long_len=long_len, pair_index=pair_index, w_qkv=w_qkv, b_qv=b_qv, w_out=w_out, b_resid=b_resid, norm_gain=norm_gain, norm_bias=norm_bias, w_in=w_in, b_in=b_in, w_back=w_back)


@jax.custom_vjp
def low(v):
    return lax.optimization_barrier(v.astype(jnp.bfloat16)).astype(jnp.float32)

@jax.custom_vjp
def low_back(v):
    return v

def low_keep(v):
    return (low(v), None)

def low_pass(kept, grad):
    return (grad,)

def back_keep(v):
    return (v, None)

def back_low(kept, grad):
    return (low(grad),)
low.defvjp(low_keep, low_pass)
low_back.defvjp(back_keep, back_low)
logit_scale = 40.0
margin = 0.3
norm_eps = 1e-12
unit_eps = 1e-06
highest = lax.Precision.HIGHEST

def matmul(left, right):
    return jnp.matmul(left, right, precision=highest)

def norm_rows(matrix, gain_row, bias_row):
    centre = matrix - lax.optimization_barrier(jnp.mean(matrix, -1, keepdims=True))
    spread = lax.optimization_barrier(jnp.mean(centre * centre, -1, keepdims=True))
    return centre * lax.rsqrt(spread + norm_eps) * gain_row + bias_row

def unit_rows(matrix):
    return matrix * lax.rsqrt(lax.optimization_barrier(jnp.sum(matrix * matrix, -1, keepdims=True)) + unit_eps)

def encoder_layer(inputs, lengths, params, number, is_last):
    w_qkv, b_qv, w_out, b_resid, norm_gain, norm_bias, w_in, b_in, w_back = params
    sent_count, sent_span, model_width = inputs.shape
    head_count = HEADS
    head_size = model_width // head_count
    lowered = low(inputs)
    weights = w_qkv[number]
    key_rows = low_back(low(matmul(lowered, weights[:, model_width:2 * model_width])))
    value_rows = low_back(low(matmul(lowered, weights[:, 2 * model_width:]) + b_qv[number, model_width:]))
    if is_last:
        query_in = lowered[:, :1]
        residual = inputs[:, :1]
    else:
        query_in = lowered
        residual = inputs
    query_rows = low_back(low(matmul(query_in, weights[:, :model_width]) + b_qv[number, :model_width]))
    query_count = query_rows.shape[1]
    query_heads = query_rows.reshape(sent_count, query_count, head_count, head_size)
    key_heads = key_rows.reshape(sent_count, sent_span, head_count, head_size)
    value_heads = value_rows.reshape(sent_count, sent_span, head_count, head_size)
    scores = low_back(jnp.einsum('nqhd,nkhd->nhqk', query_heads, key_heads, precision=highest))
    visible = (jnp.arange(sent_span)[None, :] < lengths[:, None])[:, None, None, :]
    logits = jnp.where(visible, scores * (1.0 / math.sqrt(head_size)), -jnp.inf)
    biggest = lax.optimization_barrier(jnp.max(logits, -1, keepdims=True))
    powers = jnp.exp(logits - biggest)
    attn_probs = low(powers / lax.optimization_barrier(jnp.sum(powers, -1, keepdims=True)))
    context = jnp.einsum('nhqk,nkhd->nqhd', attn_probs, value_heads, precision=highest)
    context = low_back(low(context.reshape(sent_count, query_count, model_width)))
    attended = residual + low_back(matmul(context, w_out[number])) + b_resid[number, :model_width]
    normed = norm_rows(attended, norm_gain[number, :model_width], norm_bias[number, :model_width])
    hidden = low_back(matmul(low(normed), w_in[number]) + b_in[number])
    activated = low(jax.nn.gelu(hidden, approximate=False))
    mixed_rows = normed + low_back(matmul(activated, w_back[number])) + b_resid[number, model_width:]
    return norm_rows(mixed_rows, norm_gain[number, model_width:], norm_bias[number, model_width:])

def encode_group(params, tokens, lengths):
    hidden_rows = tokens
    for number in range(LAYERS):
        hidden_rows = encoder_layer(hidden_rows, lengths, params, number, number == LAYERS - 1)
    return hidden_rows[:, 0]

def encode_bucket(params, tokens, lengths):
    sent_count, sent_span, model_width = tokens.shape
    group_size = math.gcd(sent_count, max(1, 4096 // sent_span))
    shaped = tokens.reshape(sent_count // group_size, group_size, sent_span, model_width)
    group_lens = lengths.reshape(sent_count // group_size, group_size)
    encode_step = jax.checkpoint(encode_group)
    pooled = lax.map(lambda slab_pair: encode_step(params, slab_pair[0], slab_pair[1]), (shaped, group_lens))
    return pooled.reshape(sent_count, model_width)

def direction_loss(scores, positive):
    logits = logit_scale * (scores - margin * positive)
    biggest = lax.optimization_barrier(jnp.max(logits, -1, keepdims=True))
    log_sums = biggest[:, 0] + jnp.log(lax.optimization_barrier(jnp.sum(jnp.exp(logits - biggest), -1)))
    return jnp.sum(log_sums - lax.optimization_barrier(jnp.sum(logits * positive, -1)))

def objective(params, short_x, long_x, short_len, long_len, pair_index):
    short_cls = encode_bucket(params, short_x.reshape(2 * NSHORT, SHORT, D), short_len.reshape(-1))
    long_cls = encode_bucket(params, long_x.reshape(2 * NLONG, LONG, D), long_len.reshape(-1))
    short_cls = short_cls.reshape(2, N_DP, SHORT_DEV, D)
    long_cls = long_cls.reshape(2, N_DP, LONG_DEV, D)
    pooled = jnp.concatenate([short_cls, long_cls], 2).reshape(2, NPAIRS, D)
    unit_vecs = low(unit_rows(pooled))
    source = unit_vecs[0]
    target = unit_vecs[1]
    positive = (pair_index[:, None] == jnp.arange(NPAIRS)[None, :]).astype(jnp.float32)
    forward_scores = low_back(matmul(source, target.T))
    backward_scores = low_back(matmul(target, source.T))
    total_loss = direction_loss(forward_scores, positive) + direction_loss(backward_scores, positive.T)
    return 0.5 * total_loss

def reference(short_tokens, long_tokens, short_len, long_len, pair_index, w_qkv, b_qv, w_out, b_resid, norm_gain, norm_bias, w_in, b_in, w_back):
    params = tuple((item.astype(jnp.float32) for item in (w_qkv, b_qv, w_out, b_resid, norm_gain, norm_bias, w_in, b_in, w_back)))
    short_x = short_tokens.astype(jnp.float32)
    long_x = long_tokens.astype(jnp.float32)
    objective_value, back_fn = jax.vjp(lambda params_in, short_in, long_in: objective(params_in, short_in, long_in, short_len, long_len, pair_index), params, short_x, long_x)
    gradients, grad_short, grad_long = back_fn(jnp.ones_like(objective_value))
    return (gradients[0], gradients[1], gradients[2], gradients[3], gradients[4], gradients[5], gradients[6], gradients[7], gradients[8], grad_short, grad_long)
```

```python
import math

import jax
import jax.numpy as jnp
from jax import lax
from jax.sharding import PartitionSpec as P

HEADS = 8
BF = jnp.bfloat16
F32 = jnp.float32
AXES = ("stream", "dp")
logit_scale = 40.0
margin = 0.3
norm_eps = 1e-12
unit_eps = 1e-06


def mm(a, b):
    return jnp.dot(a, b, preferred_element_type=F32)


def mm_nt(a, b):
    return lax.dot_general(a, b, (((1,), (1,)), ((), ())), preferred_element_type=F32)


def mm_tn(a, b):
    return lax.dot_general(a, b, (((0,), (0,)), ((), ())), preferred_element_type=F32)


def ln_stats(v):
    centre = v - jnp.mean(v, -1, keepdims=True)
    rstd = lax.rsqrt(jnp.mean(centre * centre, -1, keepdims=True) + norm_eps)
    return centre * rstd, rstd


def ln_back(dy, vhat, rstd, gain):
    dhat = dy * gain
    return (dhat - jnp.mean(dhat, -1, keepdims=True) - vhat * jnp.mean(dhat * vhat, -1, keepdims=True)) * rstd


def gelu_pair(v):
    cdf = 0.5 * (1.0 + lax.erf(v * (1.0 / math.sqrt(2.0))))
    pdf = jnp.exp(-0.5 * v * v) * (1.0 / math.sqrt(2.0 * math.pi))
    return v * cdf, cdf + v * pdf


def routes(n):
    rest = [1 << k for k in range(2, n.bit_length() - 2)]
    for k in range(1, len(rest)):
        rest[k] ^= rest[k - 1]
    top, y = n >> 1, 2
    first = [top, y] + rest
    second = [y, top] + rest
    return [(1, 1)] + list(zip(first, second))


def coordinate(index, n, bits):
    if bits == 1 or bits == 2 or bits == n >> 1:
        return (index // bits) % 2
    high = 1 << (bits.bit_length() - 1)
    value = (index // high) % 2
    probe = high * 2
    while probe < n >> 1:
        value = value ^ ((index // probe) % 2)
        probe *= 2
    return value


def swap(value, n, hop):
    return lax.ppermute(value, AXES, [(i, i ^ (hop[1] if i & 1 else hop[0])) for i in range(n)])


def my_bits(n):
    index = lax.axis_index("stream") * lax.axis_size("dp") + lax.axis_index("dp")
    core = index % 2
    return [
        jnp.where(core == 0, coordinate(index, n, hop[0]), coordinate(index, n, hop[1]))
        for hop in routes(n)
    ]


def reduce_scatter(bucket, n, bits):
    cur = bucket
    for hop, bit in zip(routes(n), bits):
        half = cur.shape[0] // 2
        theirs = lax.dynamic_slice_in_dim(cur, (1 - bit) * half, half, 0)
        mine = lax.dynamic_slice_in_dim(cur, bit * half, half, 0)
        got = swap(theirs, n, hop)
        cur = (mine.astype(F32) + got.astype(F32)).astype(BF)
    return cur


def all_gather(shard, n, bits):
    cur = shard
    for hop, bit in reversed(list(zip(routes(n), bits))):
        got = swap(cur, n, hop)
        low = jnp.where(bit == 0, cur, got)
        high = jnp.where(bit == 0, got, cur)
        cur = jnp.concatenate([low, high], 0)
    return cur


def gather_rows(rows, n):
    index = lax.axis_index("stream") * lax.axis_size("dp") + lax.axis_index("dp")
    cur = rows[None]
    order = [1 << k for k in range(1, n.bit_length() - 1)] + [1]
    for flip in order:
        got = swap(cur, n, (flip, flip))
        bit = (index // flip) % 2
        low = jnp.where(bit == 0, cur, got)
        high = jnp.where(bit == 0, got, cur)
        cur = jnp.stack([low, high], 1).reshape((2 * cur.shape[0],) + cur.shape[1:])
    k = len(order)
    cur = cur.reshape((2,) * k + rows.shape)
    places = [f.bit_length() - 1 for f in order]
    perm = [places.index(b) for b in reversed(range(k))]
    cur = cur.transpose(perm + [k, k + 1])
    return cur.reshape(n * rows.shape[0], rows.shape[1])


def layer0_forward(x, mask, weights):
    w_qkv, b_qv, w_out, b_resid, gain, shift, w_in, b_in, w_back = weights
    rows, width = x.shape
    blocks = mask.shape[0]
    head = width // HEADS
    bias = jnp.concatenate([b_qv[:width], jnp.zeros((width,), F32), b_qv[width:]])
    qkv = (mm(x, w_qkv) + bias).astype(BF)
    heads = qkv.reshape(blocks, rows // blocks, 3, HEADS, head)
    q, k, v = heads[:, :, 0], heads[:, :, 1], heads[:, :, 2]
    scores = jnp.einsum("bqhd,bkhd->bhqk", q, k, preferred_element_type=F32)
    logits = jnp.where(mask[:, None], scores * (1.0 / math.sqrt(head)), -jnp.inf)
    powers = jnp.exp(logits - jnp.max(logits, -1, keepdims=True))
    prob = (powers / jnp.sum(powers, -1, keepdims=True)).astype(BF)
    context = jnp.einsum("bhqk,bkhd->bqhd", prob, v, preferred_element_type=F32)
    context = context.reshape(rows, width).astype(BF)
    attended = x.astype(F32) + mm(context, w_out) + b_resid[:width]
    hat1, rstd1 = ln_stats(attended)
    normed = hat1 * gain[:width] + shift[:width]
    normed_low = normed.astype(BF)
    activ, slope = gelu_pair(mm(normed_low, w_in) + b_in)
    activ = activ.astype(BF)
    hat2, rstd2 = ln_stats(normed + mm(activ, w_back) + b_resid[width:])
    y = (hat2 * gain[width:] + shift[width:]).astype(BF)
    saved = (qkv, prob, context, hat1.astype(BF), rstd1, normed_low, activ, slope.astype(BF), hat2.astype(BF), rstd2)
    return y, saved


def colsum(v):
    return jnp.sum(v.astype(F32), 0)


def layer0_backward(dy, x, saved, weights):
    w_qkv, b_qv, w_out, b_resid, gain, shift, w_in, b_in, w_back = weights
    qkv, prob, context, hat1, rstd1, normed_low, activ, slope, hat2, rstd2 = saved
    rows, width = x.shape
    blocks = prob.shape[0]
    head = width // HEADS
    hat1, hat2 = hat1.astype(F32), hat2.astype(F32)
    dg2, dc2 = colsum(dy * hat2), colsum(dy)
    dmixed = ln_back(dy, hat2, rstd2, gain[width:])
    dmixed_low = dmixed.astype(BF)
    g_back = mm_tn(activ, dmixed_low)
    dhidden = (mm_nt(dmixed_low, w_back) * slope.astype(F32)).astype(BF)
    g_in = mm_tn(normed_low, dhidden)
    dnormed = dmixed + mm_nt(dhidden, w_in)
    dg1, dc1 = colsum(dnormed * hat1), colsum(dnormed)
    datt = ln_back(dnormed, hat1, rstd1, gain[:width])
    datt_low = datt.astype(BF)
    g_out = mm_tn(context, datt_low)
    dctx = mm_nt(datt_low, w_out).astype(BF).reshape(blocks, rows // blocks, HEADS, head)
    heads = qkv.reshape(blocks, rows // blocks, 3, HEADS, head)
    q, k, v = heads[:, :, 0], heads[:, :, 1], heads[:, :, 2]
    dprob = jnp.einsum("bqhd,bkhd->bhqk", dctx, v, preferred_element_type=F32)
    p32 = prob.astype(F32)
    dlogit = p32 * (dprob - jnp.sum(p32 * dprob, -1, keepdims=True))
    dscore = (dlogit * (1.0 / math.sqrt(head))).astype(BF)
    dq = jnp.einsum("bhqk,bkhd->bqhd", dscore, k, preferred_element_type=F32)
    dk = jnp.einsum("bhqk,bqhd->bkhd", dscore, q, preferred_element_type=F32)
    dv = jnp.einsum("bhqk,bqhd->bkhd", prob, dctx, preferred_element_type=F32)
    dqkv = jnp.stack([dq, dk, dv], 2).reshape(rows, 3 * width).astype(BF)
    g_qkv = mm_tn(x, dqkv)
    db_qkv = colsum(dqkv)
    dx = datt + mm_nt(dqkv, w_qkv)
    vectors = dict(
        b_qv=jnp.concatenate([db_qkv[:width], db_qkv[2 * width :]]),
        b_resid=jnp.concatenate([colsum(datt), colsum(dmixed)]),
        gain=jnp.concatenate([dg1, dg2]),
        shift=jnp.concatenate([dc1, dc2]),
        b_in=colsum(dhidden),
    )
    return dx, (g_qkv, g_out, g_in, g_back), vectors


def top_attention(y, valid, own, weights):
    w_qkv, b_qv = weights[0], weights[1]
    width = y.shape[1]
    sents = own.shape[0]
    head = width // HEADS
    cls = top_cls(y, sents)
    q = (mm(cls, w_qkv[:, :width]) + b_qv[:width]).astype(BF)
    pick = (jnp.arange(width)[None, :] // head == jnp.arange(HEADS)[:, None]).astype(BF)
    q_wide = (q[:, None, :] * pick[None]).reshape(sents * HEADS, width)
    q_key = mm_nt(q_wide, w_qkv[:, width : 2 * width]).astype(BF)
    seen = jnp.repeat(own & valid[None, :], HEADS, axis=0)
    logits = jnp.where(seen, mm_nt(q_key, y) * (1.0 / math.sqrt(head)), -jnp.inf)
    powers = jnp.exp(logits - jnp.max(logits, -1, keepdims=True))
    prob = powers / jnp.sum(powers, -1, keepdims=True)
    prob_low = prob.astype(BF)
    mixed = mm(prob_low, y).astype(BF)
    picked = mm(mixed, w_qkv[:, 2 * width :]).reshape(sents, HEADS, width) * pick[None].astype(F32)
    context = (jnp.sum(picked, 1) + b_qv[width:]).astype(BF)
    return context, cls, (q_wide, q_key, prob_low, mixed, pick)


def top_cls(y, sents):
    half = sents // 2
    return jnp.concatenate([y[: half * SPANS[0] : SPANS[0]], y[half * SPANS[0] :: SPANS[1]]], 0)


SPANS = (32, 128)


def top_attention_back(dctx, datt, y, cls, kept, weights):
    w_qkv = weights[0]
    q_wide, q_key, prob_low, mixed, pick = kept
    sents, width = dctx.shape
    head = width // HEADS
    d_wide = (dctx[:, None, :] * pick[None]).reshape(sents * HEADS, width)
    d_value = mm_nt(d_wide, w_qkv[:, 2 * width :]).astype(BF)
    dprob = mm_nt(d_value, y)
    prob = prob_low.astype(F32)
    dlogit = prob * (dprob - jnp.sum(prob * dprob, -1, keepdims=True))
    dscore = (dlogit * (1.0 / math.sqrt(head))).astype(BF)
    pulled = mm(dscore, y).astype(BF)
    dq = mm(pulled, w_qkv[:, width : 2 * width]).reshape(sents, HEADS, width) * pick[None].astype(F32)
    dq = jnp.sum(dq, 1).astype(BF)
    g_qkv = jnp.concatenate([mm_tn(cls, dq), mm_tn(pulled, q_wide), mm_tn(mixed, d_wide)], 1)
    dy = mm_tn(jnp.concatenate([dscore, prob_low], 0), jnp.concatenate([q_key, d_value], 0))
    dcls = mm_nt(dq, w_qkv[:, :width]) + datt
    half = sents // 2
    cut = half * SPANS[0]
    dy = jnp.concatenate(
        [
            dy[:cut].reshape(half, SPANS[0], width).at[:, 0].add(dcls[:half]).reshape(cut, width),
            dy[cut:].reshape(half, SPANS[1], width).at[:, 0].add(dcls[half:]).reshape(half * SPANS[1], width),
        ],
        0,
    )
    return dy, g_qkv, colsum(dq)


def top_rows(context, resid, pair_index, weights):
    w_qkv, b_qv, w_out, b_resid, gain, shift, w_in, b_in, w_back = weights
    rows, width = context.shape
    pairs = rows // 2
    hat1, rstd1 = ln_stats(resid.astype(F32) + mm(context, w_out) + b_resid[:width])
    normed = hat1 * gain[:width] + shift[:width]
    normed_low = normed.astype(BF)
    activ, slope = gelu_pair(mm(normed_low, w_in) + b_in)
    activ = activ.astype(BF)
    hat2, rstd2 = ln_stats(normed + mm(activ, w_back) + b_resid[width:])
    pooled = hat2 * gain[width:] + shift[width:]
    radius = lax.rsqrt(jnp.sum(pooled * pooled, -1, keepdims=True) + unit_eps)
    unit = pooled * radius
    unit_low = unit.astype(BF)
    src, tgt = unit_low[:pairs], unit_low[pairs:]
    positive = (pair_index[:, None] == jnp.arange(pairs)[None, :]).astype(F32)
    logits = logit_scale * (mm_nt(src, tgt) - margin * positive)

    def soft(axis):
        powers = jnp.exp(logits - jnp.max(logits, axis, keepdims=True))
        return powers / jnp.sum(powers, axis, keepdims=True)

    dscore = (0.5 * logit_scale * (soft(1) + soft(0) - 2.0 * positive)).astype(BF)
    dunit = jnp.concatenate([mm(dscore, tgt), mm_tn(dscore, src)], 0)
    dy = radius * (dunit - unit * jnp.sum(dunit * unit, -1, keepdims=True))
    dg2, dc2 = colsum(dy * hat2), colsum(dy)
    dmixed = ln_back(dy, hat2, rstd2, gain[width:])
    dmixed_low = dmixed.astype(BF)
    dhidden = (mm_nt(dmixed_low, w_back) * slope).astype(BF)
    dnormed = dmixed + mm_nt(dhidden, w_in)
    dg1, dc1 = colsum(dnormed * hat1), colsum(dnormed)
    datt = ln_back(dnormed, hat1, rstd1, gain[:width])
    datt_low = datt.astype(BF)
    dctx = mm_nt(datt_low, w_out).astype(BF)
    grads = (mm_tn(context, datt_low), mm_tn(normed_low, dhidden), mm_tn(activ, dmixed_low))
    vectors = dict(
        bv=colsum(dctx),
        b_resid=jnp.concatenate([colsum(datt), colsum(dmixed)]),
        gain=jnp.concatenate([dg1, dg2]),
        shift=jnp.concatenate([dc1, dc2]),
        b_in=colsum(dhidden),
    )
    return datt, dctx, grads, vectors


def per_device(short_tokens, long_tokens, short_len, long_len, pair_index, *params):
    n = lax.axis_size("stream") * lax.axis_size("dp")
    index = lax.axis_index("stream") * lax.axis_size("dp") + lax.axis_index("dp")
    width = short_tokens.shape[-1]
    spans = (short_tokens.shape[2], long_tokens.shape[2])
    counts = (short_tokens.shape[1], long_tokens.shape[1])
    sents = sum(counts)
    block = spans[1]
    lower = tuple(p[0] for p in params)
    upper = tuple(p[1] for p in params)
    x = jnp.concatenate([short_tokens.reshape(-1, width), long_tokens.reshape(-1, width)], 0)
    rows = x.shape[0]
    lens = jnp.concatenate([short_len.reshape(-1), long_len.reshape(-1)])
    sent_of = jnp.concatenate(
        [jnp.arange(counts[0] * spans[0]) // spans[0], counts[0] + jnp.arange(counts[1] * spans[1]) // spans[1]]
    )
    place = jnp.concatenate([jnp.arange(counts[0] * spans[0]) % spans[0], jnp.arange(counts[1] * spans[1]) % spans[1]])
    own = sent_of[None, :] == jnp.arange(sents)[:, None]
    valid = place < jnp.sum(jnp.where(own, lens[:, None], 0), 0)
    by_block = sent_of.reshape(-1, block)
    mask = (by_block[:, :, None] == by_block[:, None, :]) & valid.reshape(-1, 1, block)

    y, saved = layer0_forward(x, mask, lower)
    context, cls, kept = top_attention(y, valid, own, upper)
    every = gather_rows(jnp.concatenate([context, cls], 1), n)
    datt, dctx, top_grads, top_vec = top_rows(every[:, :width], every[:, width:], pair_index, upper)
    own_datt = lax.dynamic_slice_in_dim(datt, index * sents, sents, 0)
    own_dctx = lax.dynamic_slice_in_dim(dctx, index * sents, sents, 0)
    dy, g_qkv1, dbq1 = top_attention_back(own_dctx, own_datt, y, cls, kept, upper)
    dx, (g_qkv, g_out, g_in, g_back), vec = layer0_backward(dy, x, saved, lower)

    def as_rows(v):
        return v.reshape(-1, width).astype(BF)

    pad = jnp.zeros((n - 13, width), BF)
    pieces = [
        [as_rows(g_qkv1), as_rows(g_back)],
        [as_rows(g_in), as_rows(g_out)],
        [as_rows(g_qkv)] + [as_rows(v) for v in (vec["b_qv"], vec["b_resid"], vec["gain"], vec["shift"], vec["b_in"], dbq1)] + [pad],
    ]
    bits = my_bits(n)
    whole = []
    for piece in pieces:
        bucket = jnp.concatenate(piece, 0)
        whole.append(all_gather(reduce_scatter(bucket, n, bits), n, bits).astype(F32))
    cut = 3 * width
    w_qkv1, w_back0 = whole[0][:cut].reshape(width, cut), whole[0][cut:]
    cut = width * HEADS // 2
    w_in0, w_out0 = whole[1][:cut].reshape(width, cut), whole[1][cut:]
    cut = 3 * width
    w_qkv0 = whole[2][:cut].reshape(width, cut)
    small = whole[2][cut:].reshape(-1)
    wide = 2 * width
    bq1 = small[6 * wide : 6 * wide + width]
    outs = (
        jnp.stack([w_qkv0, w_qkv1]),
        jnp.stack([small[:wide], jnp.concatenate([bq1, top_vec["bv"]])]),
        jnp.stack([w_out0, top_grads[0]]),
        jnp.stack([small[wide : 2 * wide], top_vec["b_resid"]]),
        jnp.stack([small[2 * wide : 3 * wide], top_vec["gain"]]),
        jnp.stack([small[3 * wide : 4 * wide], top_vec["shift"]]),
        jnp.stack([w_in0, top_grads[1]]),
        jnp.stack([small[4 * wide : 6 * wide], top_vec["b_in"]]),
        jnp.stack([w_back0, top_grads[2]]),
    )
    cut = counts[0] * spans[0]
    return outs + (dx[:cut].reshape((1, counts[0], spans[0], width)), dx[cut:].reshape((1, counts[1], spans[1], width)))


def solution(mesh):
    split = P("stream", "dp", None, None)
    in_specs = (split, split, P("stream", "dp"), P("stream", "dp")) + (P(),) * 10
    out_specs = (P(),) * 9 + (split, split)
    return jax.shard_map(per_device, mesh=mesh, in_specs=in_specs, out_specs=out_specs, check_vma=False)
```

```python
import functools
import math

import jax
import jax.numpy as jnp
from jax import lax
from jax.experimental import pallas as pl
from jax.experimental.pallas import tpu as pltpu
from jax.sharding import PartitionSpec as P

HEADS = 8
BF = jnp.bfloat16
F32 = jnp.float32
AXES = ("stream", "dp")
logit_scale = 40.0
margin = 0.3
norm_eps = 1e-12
unit_eps = 1e-06
BLOCK = 128
STEP = 256
VMEM = 56 * 1024 * 1024


def mm(a, b):
    return jnp.dot(a, b, preferred_element_type=F32)


def mm_nt(a, b):
    return lax.dot_general(a, b, (((1,), (1,)), ((), ())), preferred_element_type=F32)


def mm_tn(a, b):
    return lax.dot_general(a, b, (((0,), (0,)), ((), ())), preferred_element_type=F32)


def ln_stats(v):
    centre = v - jnp.mean(v, -1, keepdims=True)
    rstd = lax.rsqrt(jnp.mean(centre * centre, -1, keepdims=True) + norm_eps)
    return centre * rstd, rstd


def ln_back(dy, vhat, rstd, gain):
    dhat = dy * gain
    return (dhat - jnp.mean(dhat, -1, keepdims=True) - vhat * jnp.mean(dhat * vhat, -1, keepdims=True)) * rstd


def gelu_pair(v):
    cdf = 0.5 * (1.0 + lax.erf(v * (1.0 / math.sqrt(2.0))))
    pdf = jnp.exp(-0.5 * v * v) * (1.0 / math.sqrt(2.0 * math.pi))
    return v * cdf, cdf + v * pdf


def colsum(v):
    return jnp.sum(v.astype(F32), 0)


def rowsum(v):
    return jnp.sum(v.astype(F32), 0, keepdims=True)


SMEM = pl.BlockSpec(memory_space=pltpu.SMEM)
ANY = pl.BlockSpec(memory_space=pl.ANY)


def whole(a):
    return pl.BlockSpec(a.shape, lambda i: (0,) * len(a.shape))


def shape(dims, dtype):
    return jax.ShapeDtypeStruct(dims, dtype)


def layer_of(a, level, rows=None, cols=None, at=lambda i: (0, 0)):
    rows, cols = rows or a.shape[1], cols or a.shape[2]
    return a, pl.BlockSpec((None, rows, cols), lambda i: (level, *at(i)))


def kernel_call(body, name, grid, ins, outs, flops, scratch=(), aliases=None):
    size = sum(a.size * a.dtype.itemsize for a, _ in ins) + sum(
        math.prod(s.shape) * s.dtype.itemsize for s, _ in outs
    )
    return pl.pallas_call(
        body,
        grid=grid,
        in_specs=[s for _, s in ins],
        out_specs=[s for _, s in outs],
        out_shape=[s for s, _ in outs],
        scratch_shapes=list(scratch),
        input_output_aliases=aliases or {},
        compiler_params=pltpu.CompilerParams(vmem_limit_bytes=VMEM),
        cost_estimate=pl.CostEstimate(flops=int(flops), bytes_accessed=int(size), transcendentals=0),
        name=name,
    )(*[a for a, _ in ins])


def routes(n):
    top, y = n >> 1, 2
    rest = [1 << k for k in range(2, n.bit_length() - 2)]
    for k in range(1, len(rest)):
        rest[k] |= rest[k - 1]
    halved = [(1, 1), (top, y), (y, top)]
    added = list(zip(rest, rest[::-1]))
    return halved, added


def swap(value, n, hop):
    return lax.ppermute(value, AXES, [(i, i ^ (hop[1] if i & 1 else hop[0])) for i in range(n)])


def device_index():
    return lax.axis_index("stream") * lax.axis_size("dp") + lax.axis_index("dp")


def my_bits(n):
    index = device_index()
    core = index % 2
    return [jnp.where(core == 0, (index // a) % 2, (index // b) % 2) for a, b in routes(n)[0]]


def sum_steps(bucket, n, bits):
    halved, added = routes(n)
    rows = bucket.shape[1]
    cur = bucket.reshape(2 * rows, -1)
    for hop, bit in zip(halved, bits):
        half = cur.shape[0] // 2
        theirs = lax.dynamic_slice_in_dim(cur, (1 - bit) * half, half, 0)
        mine = lax.dynamic_slice_in_dim(cur, bit * half, half, 0)
        got = yield theirs, hop
        cur = (mine.astype(F32) + got.astype(F32)).astype(BF)
    for hop in added:
        got = yield cur, hop
        cur = (cur.astype(F32) + got.astype(F32)).astype(BF)
    for hop, bit in reversed(list(zip(halved, bits))[1:]):
        got = yield cur, hop
        low = jnp.where(bit == 0, cur, got)
        high = jnp.where(bit == 0, got, cur)
        cur = jnp.concatenate([low, high], 0)
    got = yield cur, halved[0]
    return cur, got


class Lane:
    def __init__(self, bucket, n, bits):
        self.n, self.steps, self.result = n, sum_steps(bucket, n, bits), None
        self.ask = next(self.steps)

    def feed(self, got):
        try:
            self.ask = self.steps.send(got)
        except StopIteration as end:
            self.result = end.value


def stage(lanes, work=None, args=()):
    lanes = [lane for lane in lanes if lane.result is None]
    asked, args = lax.optimization_barrier(([lane.ask[0] for lane in lanes], args))
    got = [swap(value, lane.n, lane.ask[1]) for value, lane in zip(asked, lanes)]
    out = work(*args) if work else ()
    got, out = lax.optimization_barrier((got, out))
    for lane, value in zip(lanes, got):
        lane.feed(value)
    return out


def gather_rows(rows, n):
    index = device_index()
    cur = rows[None]
    order = [1 << k for k in range(1, n.bit_length() - 1)] + [1]
    for flip in order:
        got = swap(cur, n, (flip, flip))
        bit = (index // flip) % 2
        low = jnp.where(bit == 0, cur, got)
        high = jnp.where(bit == 0, got, cur)
        cur = jnp.stack([low, high], 1).reshape((2 * cur.shape[0],) + cur.shape[1:])
    k = len(order)
    cur = cur.reshape((2,) * k + rows.shape)
    places = [f.bit_length() - 1 for f in order]
    perm = [places.index(b) for b in reversed(range(k))]
    cur = cur.transpose(perm + [k, k + 1])
    return cur.reshape(n * rows.shape[0], rows.shape[1])


def halves(v, first):
    zero = jnp.zeros_like(v)
    return jnp.concatenate([jnp.where(first, v, zero), jnp.where(first, zero, v)], 0)


def join_halves(v, first):
    return jnp.where(first, v[: v.shape[0] // 2], v[v.shape[0] // 2 :])


def first_head(width):
    return lax.broadcasted_iota(jnp.int32, (1, 2 * width // HEADS), 1) < width // HEADS


def key_bias(lens_ref, block, span_short, count_short):
    key = lax.broadcasted_iota(jnp.int32, (BLOCK, 1), 0)
    query = lax.broadcasted_iota(jnp.int32, (1, BLOCK), 1)
    per = BLOCK // span_short
    blocks_short = count_short // per
    is_short = block < blocks_short
    at = jnp.where(is_short, block * per, count_short + block - blocks_short)
    limit = jnp.zeros((BLOCK, 1), jnp.int32)
    for s in range(per):
        inside = key // span_short == s
        limit = jnp.where(inside, jnp.where(is_short, lens_ref[at + jnp.where(is_short, s, 0)] + s * span_short, 0), limit)
    limit = jnp.where(is_short, limit, lens_ref[at])
    same = (key // span_short == query // span_short) | jnp.logical_not(is_short)
    return jnp.where((key < limit) & same, 0.0, -jnp.inf).astype(F32)


def vectors(level, width, bqv_ref, bresid_ref, gain_ref, shift_ref):
    row = slice(level, level + 1)
    low, high = slice(0, width), slice(width, 2 * width)
    return [ref[row, part] for ref in (bqv_ref, bresid_ref, gain_ref, shift_ref) for part in (low, high)]


def forward_body(
    span, count, lens_ref, short_ref, long_ref, wqkv_ref, wout_ref, win_ref, wback_ref, bin_ref, bqv_ref, bresid_ref, gain_ref, shift_ref,
    y_ref, qkv_ref, prob_ref, ctx_ref, hat1_ref, rstd1_ref, low_ref, act_ref, slope_ref, hat2_ref, rstd2_ref,
):
    step = pl.program_id(0)
    x = jnp.where(step == 0, short_ref[...], long_ref[...])
    rows, width = x.shape
    bq, bv, bo, bb, g1, g2, c1, c2 = vectors(0, width, bqv_ref, bresid_ref, gain_ref, shift_ref)
    pair = 2 * width // HEADS
    first = first_head(width)
    scale = 1.0 / math.sqrt(width // HEADS)
    bias = jnp.concatenate([bq, jnp.zeros_like(bq), bv], 1)
    qkv = (mm(x, wqkv_ref[...]) + bias).astype(BF)
    qkv_ref[...] = qkv
    blocks = []
    for b in range(rows // BLOCK):
        r = slice(b * BLOCK, (b + 1) * BLOCK)
        hide = key_bias(lens_ref, step * (rows // BLOCK) + b, span, count)
        hide = jnp.concatenate([hide, hide], 1)
        cols = []
        for p in range(HEADS // 2):
            q, k, v = (qkv[r, m * width + p * pair : m * width + (p + 1) * pair] for m in range(3))
            logit = mm_nt(k, halves(q, first)) * scale + hide
            power = jnp.exp(logit - jnp.max(logit, 0, keepdims=True))
            prob = (power * (1.0 / jnp.sum(power, 0, keepdims=True))).astype(BF)
            prob_ref[b, p] = prob
            cols.append(join_halves(mm_tn(prob, v), first))
        blocks.append(jnp.concatenate(cols, 1).astype(BF))
    ctx = jnp.concatenate(blocks, 0)
    ctx_ref[...] = ctx
    hat1, rstd1 = ln_stats(x.astype(F32) + mm(ctx, wout_ref[...]) + bo)
    normed = hat1 * g1 + c1
    low = normed.astype(BF)
    hat1_ref[...] = hat1.astype(BF)
    rstd1_ref[...] = jnp.broadcast_to(rstd1, rstd1_ref.shape)
    low_ref[...] = low
    act, slope = gelu_pair(mm(low, win_ref[...]) + bin_ref[0:1])
    act = act.astype(BF)
    act_ref[...] = act
    slope_ref[...] = slope.astype(BF)
    hat2, rstd2 = ln_stats(normed + mm(act, wback_ref[...]) + bb)
    hat2_ref[...] = hat2.astype(BF)
    rstd2_ref[...] = jnp.broadcast_to(rstd2, rstd2_ref.shape)
    y_ref[...] = (hat2 * g2 + c2).astype(BF)


def by_rows(cols):
    return pl.BlockSpec((STEP, cols), lambda i: (i, 0))


def from_buckets(short, long):
    width = short.shape[1]
    return [
        (short, pl.BlockSpec((STEP, width), lambda i: (0, 0))),
        (long, pl.BlockSpec((STEP, width), lambda i: (jnp.maximum(i - 1, 0), 0))),
    ]


def small_ins(w):
    return [(w[k], whole(w[k])) for k in ("b_qv", "b_resid", "gain", "shift")]


def forward(short, long, lens, w, span, count):
    rows, width = short.shape[0] + long.shape[0], short.shape[1]
    ff = w["in"].shape[2]
    per = STEP // BLOCK
    prob = pl.BlockSpec((per, HEADS // 2, BLOCK, 2 * BLOCK), lambda i: (i, 0, 0, 0))
    ins = [(lens, SMEM)] + from_buckets(short, long)
    ins += [layer_of(w[name], 0) for name in ("qkv", "out", "in", "back")] + [(w["b_in"], whole(w["b_in"]))] + small_ins(w)
    cols = [(width, BF), (3 * width, BF), None, (width, BF), (width, BF), (128, F32), (width, BF), (ff, BF), (ff, BF), (width, BF), (128, F32)]
    outs = [(shape((rows, c[0]), c[1]), by_rows(c[0])) if c else (shape((rows // BLOCK, HEADS // 2, BLOCK, 2 * BLOCK), BF), prob) for c in cols]
    body = functools.partial(forward_body, span, count)
    return kernel_call(body, "layer0_forward", (rows // STEP,), ins, outs, 2 * rows * width * (4 * width + 2 * ff))


def starts(sents, spans, rows):
    s = lax.broadcasted_iota(jnp.int32, (sents, rows), 0)
    r = lax.broadcasted_iota(jnp.int32, (sents, rows), 1)
    half = sents // 2
    at = jnp.where(s < half, s * spans[0], half * spans[0] + (s - half) * spans[1])
    return (r == at).astype(BF)


def spread(sents):
    a = lax.broadcasted_iota(jnp.int32, (sents * HEADS, sents), 0) // HEADS
    return (a == lax.broadcasted_iota(jnp.int32, (sents * HEADS, sents), 1)).astype(BF)


def own_head(sents, width):
    a = lax.broadcasted_iota(jnp.int32, (sents * HEADS, width), 0) % HEADS
    return a == lax.broadcasted_iota(jnp.int32, (sents * HEADS, width), 1) // (width // HEADS)


def sum_heads(v, keep, sents):
    return jnp.sum(jnp.where(keep, v, 0.0).reshape(sents, HEADS, v.shape[1]), 1)


def ask_body(spans, y_ref, lens_ref, wqkv_ref, bqv_ref, out_ref, wide_ref, key_ref, prob_ref, mixed_ref):
    y = y_ref[...]
    rows, width = y.shape
    sents = out_ref.shape[0]
    keep = own_head(sents, width)
    cls = mm(starts(sents, spans, rows), y).astype(BF)
    q = (mm(cls, wqkv_ref[:, :width]) + bqv_ref[1:2, :width]).astype(BF)
    wide = jnp.where(keep, mm(spread(sents), q), 0.0).astype(BF)
    key = mm_nt(wide, wqkv_ref[:, width : 2 * width]).astype(BF)
    half = sents // 2
    sent = lax.broadcasted_iota(jnp.int32, (sents * HEADS, 1), 0) // HEADS
    begin = jnp.where(sent < half, sent * spans[0], half * spans[0] + (sent - half) * spans[1])
    place = lax.broadcasted_iota(jnp.int32, (sents * HEADS, rows), 1) - begin
    seen = (place >= 0) & (place < lens_ref[...])
    logit = jnp.where(seen, mm_nt(key, y) * (1.0 / math.sqrt(width // HEADS)), -jnp.inf)
    power = jnp.exp(logit - jnp.max(logit, 1, keepdims=True))
    prob = (power * (1.0 / jnp.sum(power, 1, keepdims=True))).astype(BF)
    mixed = mm(prob, y).astype(BF)
    picked = sum_heads(mm(mixed, wqkv_ref[:, 2 * width :]), keep, sents)
    out_ref[:, :width] = (picked + bqv_ref[1:2, width:]).astype(BF)
    out_ref[:, width:] = cls
    wide_ref[...] = wide
    key_ref[...] = key
    prob_ref[...] = prob
    mixed_ref[...] = mixed


def ask(y, lens, w, spans, sents):
    rows, width = y.shape
    wide = sents * HEADS
    ins = [(y, whole(y)), (lens, whole(lens)), layer_of(w["qkv"], 1), (w["b_qv"], whole(w["b_qv"]))]
    outs = [(s, whole(s)) for s in (shape((sents, 2 * width), BF), shape((wide, width), BF), shape((wide, width), BF), shape((wide, rows), BF), shape((wide, width), BF))]
    return kernel_call(functools.partial(ask_body, spans), "layer1_ask", (1,), ins, outs, 2 * wide * width * (2 * rows + 3 * width))


def top_forward(ctx, cls, wout_ref, win_ref, bin_ref, bo, g1, c1):
    hat1, rstd1 = ln_stats(cls.astype(F32) + mm(ctx, wout_ref[...]) + bo)
    normed = hat1 * g1 + c1
    low = normed.astype(BF)
    return hat1, rstd1, normed, low, mm(low, win_ref[...]) + bin_ref[1:2]


def gelu(v):
    return v * (0.5 * (1.0 + lax.erf(v * (1.0 / math.sqrt(2.0)))))


def top_body(index_ref, every_ref, pair_ref, wout_ref, win_ref, wback_ref, bin_ref, bqv_ref, bresid_ref, gain_ref, shift_ref,
             datt_ref, dctx_ref, dy_ref, hid_s, hat1_s, rstd1_s, hat2_s, rstd2_s):
    width = dy_ref.shape[1]
    pairs = pair_ref.shape[0]
    sents = datt_ref.shape[0]
    _, _, bo, bb, g1, g2, c1, c2 = vectors(1, width, bqv_ref, bresid_ref, gain_ref, shift_ref)
    hat1, rstd1, normed, low, hid = top_forward(every_ref[:, :width], every_ref[:, width:], wout_ref, win_ref, bin_ref, bo, g1, c1)
    hid_s[...] = hid
    hat1_s[...] = hat1
    rstd1_s[...] = jnp.broadcast_to(rstd1, rstd1_s.shape)
    hat2, rstd2 = ln_stats(normed + mm(gelu(hid).astype(BF), wback_ref[...]) + bb)
    hat2_s[...] = hat2
    rstd2_s[...] = jnp.broadcast_to(rstd2, rstd2_s.shape)
    pooled = hat2 * g2 + c2
    radius = lax.rsqrt(jnp.sum(pooled * pooled, -1, keepdims=True) + unit_eps)
    unit = pooled * radius
    src, tgt = unit[:pairs].astype(BF), unit[pairs:].astype(BF)
    positive = (pair_ref[...] == lax.broadcasted_iota(jnp.int32, (pairs, pairs), 1)).astype(F32)
    logits = logit_scale * (mm_nt(src, tgt) - margin * positive)

    def soft(axis):
        powers = jnp.exp(logits - jnp.max(logits, axis, keepdims=True))
        return powers / jnp.sum(powers, axis, keepdims=True)

    dscore = (0.5 * logit_scale * (soft(1) + soft(0) - 2.0 * positive)).astype(BF)
    dunit = jnp.concatenate([mm(dscore, tgt), mm_tn(dscore, src)], 0)
    dy_ref[...] = radius * (dunit - unit * jnp.sum(dunit * unit, -1, keepdims=True))
    mine = pl.ds(pl.multiple_of(index_ref[0] * sents, sents), sents)
    dmixed = ln_back(dy_ref[mine], hat2_s[mine], rstd2_s[mine, 0:1], g2)
    dhidden = (mm_nt(dmixed.astype(BF), wback_ref[...]) * gelu_pair(hid_s[mine])[1]).astype(BF)
    dnormed = dmixed + mm_nt(dhidden, win_ref[...])
    datt = ln_back(dnormed, hat1_s[mine], rstd1_s[mine, 0:1], g1)
    datt_ref[...] = datt
    dctx_ref[...] = mm_nt(datt.astype(BF), wout_ref[...]).astype(BF)


def top_ins(w):
    return [layer_of(w[k], 1) for k in ("out", "in", "back")] + [(w["b_in"], whole(w["b_in"]))] + small_ins(w)


def top(index, every, pair, w, sents):
    rows, width = every.shape[0], every.shape[1] // 2
    ff = w["in"].shape[2]
    ins = [(index, SMEM), (every, whole(every)), (pair, whole(pair))] + top_ins(w)
    outs = [(s, whole(s)) for s in (shape((sents, width), F32), shape((sents, width), BF), shape((rows, width), F32))]
    scratch = [pltpu.VMEM((rows, c), F32) for c in (ff, width, 128, width, 128)]
    return kernel_call(top_body, "top", (1,), ins, outs, 2 * rows * width * (width + 2 * ff), scratch)


def top_grads_body(every_ref, dy_ref, wout_ref, win_ref, wback_ref, bin_ref, bqv_ref, bresid_ref, gain_ref, shift_ref,
                   gout_ref, gin_ref, gback_ref, sums_ref, sumin_ref):
    width = dy_ref.shape[1]
    _, _, bo, bb, g1, g2, c1, c2 = vectors(1, width, bqv_ref, bresid_ref, gain_ref, shift_ref)
    ctx = every_ref[:, :width]
    hat1, rstd1, normed, low, hid = top_forward(ctx, every_ref[:, width:], wout_ref, win_ref, bin_ref, bo, g1, c1)
    act, slope = gelu_pair(hid)
    act = act.astype(BF)
    hat2, rstd2 = ln_stats(normed + mm(act, wback_ref[...]) + bb)
    dy = dy_ref[...]
    dmixed = ln_back(dy, hat2, rstd2, g2)
    dmixed_low = dmixed.astype(BF)
    gback_ref[...] = mm_tn(act, dmixed_low)
    dhidden = (mm_nt(dmixed_low, wback_ref[...]) * slope).astype(BF)
    gin_ref[...] = mm_tn(low, dhidden)
    dnormed = dmixed + mm_nt(dhidden, win_ref[...])
    datt = ln_back(dnormed, hat1, rstd1, g1)
    datt_low = datt.astype(BF)
    gout_ref[...] = mm_tn(ctx, datt_low)
    sumin_ref[...] = rowsum(dhidden)
    parts = (datt, dmixed, dnormed * hat1, dy * hat2, dnormed, dy, mm_nt(datt_low, wout_ref[...]).astype(BF))
    for k, part in enumerate(parts):
        sums_ref[k : k + 1] = rowsum(part)
    sums_ref[7:8] = jnp.zeros((1, width), F32)


def top_grads(every, dy, w):
    width = dy.shape[1]
    ff = w["in"].shape[2]
    rows = every.shape[0]
    ins = [(every, whole(every)), (dy, whole(dy))] + top_ins(w)

    def upper(a, b):
        return shape((2, a, b), F32), pl.BlockSpec((None, a, b), lambda i: (1, 0, 0))

    sums, sumin = shape((8, width), F32), shape((1, ff), F32)
    outs = [upper(width, width), upper(width, ff), upper(ff, width), (sums, whole(sums)), (sumin, whole(sumin))]
    return kernel_call(top_grads_body, "top_grads", (1,), ins, outs, 6 * rows * width * (width + 2 * ff))


def ask_back_body(spans, y_ref, wide_ref, key_ref, prob_ref, mixed_ref, wqkv_ref, dctx_ref, datt_ref,
                  hat2_ref, rstd2_ref, gain_ref, act_ref, bucket_ref, dmixed_ref, low_ref, sums_ref):
    step = pl.program_id(0)
    rows, width = y_ref.shape
    ff = pl.num_programs(0) * width

    @pl.when(step == 0)
    def _():
        y = y_ref[...]
        sents = dctx_ref.shape[0]
        keep = own_head(sents, width)
        first = starts(sents, spans, rows)
        prob_low = prob_ref[...]
        wide = wide_ref[...]
        d_wide = jnp.where(keep, mm(spread(sents), dctx_ref[...]), 0.0).astype(BF)
        d_value = mm_nt(d_wide, wqkv_ref[:, 2 * width :]).astype(BF)
        dprob = mm_nt(d_value, y)
        prob = prob_low.astype(F32)
        dlogit = prob * (dprob - jnp.sum(prob * dprob, 1, keepdims=True))
        dscore = (dlogit * (1.0 / math.sqrt(width // HEADS))).astype(BF)
        pulled = mm(dscore, y).astype(BF)
        dq = sum_heads(mm(pulled, wqkv_ref[:, width : 2 * width]), keep, sents).astype(BF)
        dcls = mm_nt(dq, wqkv_ref[:, :width]) + datt_ref[...]
        high = dcls.astype(BF)
        left = jnp.concatenate([dscore, prob_low, first, first], 0)
        right = jnp.concatenate([key_ref[...], d_value, high, (dcls - high.astype(F32)).astype(BF)], 0)
        dy = mm_tn(left, right)
        hat2 = hat2_ref[...].astype(F32)
        dmixed = ln_back(dy, hat2, rstd2_ref[:, 0:1], gain_ref[0:1, width:])
        low_ref[...] = dmixed.astype(BF)
        dmixed_ref[...] = dmixed
        cls = mm(first, y).astype(BF)
        bucket_ref[ff : ff + width] = mm_tn(cls, dq).astype(BF)
        bucket_ref[ff + width : ff + 2 * width] = mm_tn(pulled, wide).astype(BF)
        bucket_ref[ff + 2 * width :] = mm_tn(mixed_ref[...], d_wide).astype(BF)
        sums_ref[0:1] = rowsum(dmixed)
        sums_ref[1:2] = rowsum(dy * hat2)
        sums_ref[2:3] = rowsum(dy)
        sums_ref[3:4] = rowsum(dq)
        sums_ref[4:8] = jnp.zeros((4, width), F32)

    bucket_ref[pl.ds(pl.multiple_of(step * width, width), width)] = mm_tn(act_ref[...], low_ref[...]).astype(BF)


def ask_back(y, kept, w, dctx, datt, hat2, rstd2, act, spans):
    rows, width = y.shape
    ff = act.shape[1]
    ins = [(a, whole(a)) for a in (y, *kept)] + [layer_of(w["qkv"], 1)]
    ins += [(a, whole(a)) for a in (dctx, datt, hat2, rstd2, w["gain"])] + [(act, pl.BlockSpec((rows, width), lambda i: (0, i)))]
    outs = [(s, whole(s)) for s in (shape((ff + 3 * width, width), BF), shape((rows, width), F32), shape((rows, width), BF), shape((8, width), F32))]
    return kernel_call(functools.partial(ask_back_body, spans), "layer1_ask_back", (ff // width,), ins, outs, 2 * rows * width * ff + 2 * rows * width * 512)


VECTOR_ROWS = 64


def hidden_back_body(low_ref, slope_ref, wback_ref, nlow_ref, bucket_ref, dhidden_ref, sumin_ref):
    dhidden = (mm_nt(low_ref[...], wback_ref[...]) * slope_ref[...].astype(F32)).astype(BF)
    dhidden_ref[...] = dhidden
    bucket_ref[...] = mm_tn(nlow_ref[...], dhidden).astype(BF)
    sumin_ref[0] = rowsum(dhidden)


def hidden_back(low, slope, nlow, w):
    rows, width = low.shape
    ff = slope.shape[1]
    cols = pl.BlockSpec((rows, width), lambda i: (0, i))
    ins = [(low, whole(low)), (slope, cols), layer_of(w["back"], 0, width, width, lambda i: (i, 0)), (nlow, whole(nlow))]
    outs = [(shape((2, ff + VECTOR_ROWS, width), BF), pl.BlockSpec((None, width, width), lambda i: (0, i, 0)))]
    outs += [(shape((rows, ff), BF), cols), (shape((ff // width, 1, width), F32), pl.BlockSpec((1, 1, width), lambda i: (i, 0, 0)))]
    return kernel_call(hidden_back_body, "layer0_hidden_back", (ff // width,), ins, outs, 4 * rows * width * ff)


def normed_back_body(dhidden_ref, dmixed_ref, win_ref, hat1_ref, rstd1_ref, gain_ref, ctx_ref, wout_ref, _, bucket_ref, datt_ref, dctx_ref, sums_ref, acc):
    step = pl.program_id(0)
    width = dmixed_ref.shape[1]

    @pl.when(step == 0)
    def _():
        acc[...] = jnp.zeros_like(acc)
        sums_ref[...] = jnp.zeros_like(sums_ref)

    dnormed = dmixed_ref[...] + mm_nt(dhidden_ref[...], win_ref[...])
    hat1 = hat1_ref[...].astype(F32)
    datt = ln_back(dnormed, hat1, rstd1_ref[:, 0:1], gain_ref[0:1, :width])
    low = datt.astype(BF)
    datt_ref[...] = datt
    dctx_ref[...] = mm_nt(low, wout_ref[...]).astype(BF)
    acc[...] += mm_tn(ctx_ref[...], low)
    sums_ref[0:1] += rowsum(datt)
    sums_ref[1:2] += rowsum(dnormed * hat1)
    sums_ref[2:3] += rowsum(dnormed)

    @pl.when(step == pl.num_programs(0) - 1)
    def _():
        bucket_ref[...] = acc[...].astype(BF)


def normed_back(dhidden, dmixed, hat1, rstd1, ctx, bucket, w):
    rows, width = dmixed.shape
    ff = dhidden.shape[1]
    ins = [(dhidden, by_rows(ff)), (dmixed, by_rows(width)), layer_of(w["in"], 0), (hat1, by_rows(width)), (rstd1, by_rows(128)), (w["gain"], whole(w["gain"]))]
    ins += [(ctx, by_rows(width)), layer_of(w["out"], 0), (bucket, ANY)]
    sums = shape((8, width), F32)
    outs = [(shape(bucket.shape, BF), pl.BlockSpec((None, width, width), lambda i: (1, 0, 0)))]
    outs += [(shape((rows, width), F32), by_rows(width)), (shape((rows, width), BF), by_rows(width)), (sums, whole(sums))]
    return kernel_call(normed_back_body, "layer0_normed_back", (rows // STEP,), ins, outs, 2 * rows * width * (ff + 2 * width), [pltpu.VMEM((width, width), F32)], {8: 0})


def attention_back_body(qkv_ref, prob_ref, dctx_ref, short_ref, long_ref, sums1_ref, sums2_ref, sumin_ref, _, dqkv_ref, bucket_ref, acc, sums, thirds, vec, done):
    step = pl.program_id(0)
    x = jnp.where(step == 0, short_ref[...], long_ref[...])
    rows, width = x.shape
    pair = 2 * width // HEADS
    first = first_head(width)
    scale = 1.0 / math.sqrt(width // HEADS)

    @pl.when(step == 0)
    def _():
        acc[...] = jnp.zeros_like(acc)
        sums[...] = jnp.zeros_like(sums)

    for b in range(rows // BLOCK):
        r = slice(b * BLOCK, (b + 1) * BLOCK)
        for p in range(HEADS // 2):
            c = [slice(m * width + p * pair, m * width + (p + 1) * pair) for m in range(3)]
            q, k, v = (qkv_ref[r, s] for s in c)
            dd = halves(dctx_ref[r, c[0]], first)
            low = prob_ref[b, p]
            prob = low.astype(F32)
            dprob = mm_nt(v, dd)
            dlogit = prob * (dprob - jnp.sum(prob * dprob, 0, keepdims=True))
            dscore = (dlogit * scale).astype(BF)
            dqkv_ref[r, c[0]] = join_halves(mm_tn(dscore, k), first).astype(BF)
            dqkv_ref[r, c[1]] = mm(dscore, halves(q, first)).astype(BF)
            dqkv_ref[r, c[2]] = mm(low, dd).astype(BF)
    dqkv = dqkv_ref[...]
    acc[...] += mm_tn(x, dqkv)
    sums[0:1] += rowsum(dqkv)

    @pl.when(step == pl.num_programs(0) - 1)
    def _():
        for m in range(3):
            thirds[m * width : (m + 1) * width] = acc[:, m * width : (m + 1) * width].astype(BF)
        rows_of = [sums[0:1, :width], sums[0:1, 2 * width :]]
        for k in range(3):
            rows_of += [sums1_ref[k : k + 1], sums2_ref[k : k + 1]]
        rows_of += [sumin_ref[k] for k in range(sumin_ref.shape[0])]
        rows_of += [sums2_ref[3:4], jnp.zeros((3, width), F32)]
        vec[...] = jnp.zeros_like(vec)
        vec[0:16] = jnp.concatenate(rows_of, 0).astype(BF)
        size = bucket_ref.shape[1]
        copies = [
            pltpu.make_async_copy(thirds, bucket_ref.at[1, width : 4 * width], done.at[0]),
            pltpu.make_async_copy(vec, bucket_ref.at[0, size - VECTOR_ROWS : size], done.at[1]),
        ]
        for copy in copies:
            copy.start()
        for copy in copies:
            copy.wait()


def attention_back(qkv, prob, dctx, sums1, bucket, sums2, sumin, short, long):
    rows, width = dctx.shape
    per = STEP // BLOCK
    ins = [(qkv, by_rows(3 * width)), (prob, pl.BlockSpec((per,) + prob.shape[1:], lambda i: (i, 0, 0, 0))), (dctx, by_rows(width))]
    ins += from_buckets(short, long) + [(a, whole(a)) for a in (sums1, sums2, sumin)]
    ins += [(bucket, ANY)]
    outs = [(shape((rows, 3 * width), BF), by_rows(3 * width)), (shape(bucket.shape, BF), ANY)]
    scratch = [pltpu.VMEM((width, 3 * width), F32), pltpu.VMEM((8, 3 * width), F32)]
    scratch += [pltpu.VMEM((3 * width, width), BF), pltpu.VMEM((VECTOR_ROWS, width), BF), pltpu.SemaphoreType.DMA((2,))]
    flops = 2 * rows * width * (3 * width + 10 * BLOCK)
    return kernel_call(attention_back_body, "layer0_attention_back", (rows // STEP,), ins, outs, flops, scratch, {8: 1})


def input_back_body(dqkv_ref, datt_ref, wqkv_ref, short_ref, long_ref):
    dx = datt_ref[...] + mm_nt(dqkv_ref[...], wqkv_ref[...])

    @pl.when(pl.program_id(0) == 0)
    def _():
        short_ref[...] = dx

    @pl.when(pl.program_id(0) > 0)
    def _():
        long_ref[...] = dx


def input_back(dqkv, datt, w, cut):
    rows, width = datt.shape
    ins = [(dqkv, by_rows(3 * width)), (datt, by_rows(width)), layer_of(w["qkv"], 0)]
    outs = [
        (shape((cut, width), F32), pl.BlockSpec((STEP, width), lambda i: (0, 0))),
        (shape((rows - cut, width), F32), pl.BlockSpec((STEP, width), lambda i: (jnp.maximum(i - 1, 0), 0))),
    ]
    return kernel_call(input_back_body, "layer0_input_back", (rows // STEP,), ins, outs, 2 * rows * width * 3 * width)


def unpack_call(body, name, bit, grid, ins, outs, aliases, size):
    return pl.pallas_call(
        body,
        grid_spec=pltpu.PrefetchScalarGridSpec(
            num_scalar_prefetch=1,
            grid=grid,
            in_specs=[s for _, s in ins],
            out_specs=[s for _, s in outs],
        ),
        out_shape=[s for s, _ in outs],
        input_output_aliases=aliases,
        compiler_params=pltpu.CompilerParams(vmem_limit_bytes=VMEM),
        cost_estimate=pl.CostEstimate(flops=0, bytes_accessed=size, transcendentals=0),
        name=name,
    )(bit, *[a for a, _ in ins])


def in_order(bit_ref, mine_ref, theirs_ref):
    mine, theirs = mine_ref[...].astype(F32), theirs_ref[...].astype(F32)
    low = bit_ref[0] == 0
    return jnp.where(low, mine, theirs), jnp.where(low, theirs, mine)


def unpack_first(bit, pair, back):
    _, ff, width = back.shape
    rows = width // 2
    steps = pair[0].shape[0] // rows
    block = pl.BlockSpec((rows, width), lambda j, bit: (j, 0))

    def at_qkv(j, bit):
        j = jnp.maximum(j - 1, 0)
        return 1, j % 2, j // 2

    def body(bit_ref, mine_ref, theirs_ref, _, qkv_ref, back_ref):
        step = pl.program_id(0)
        low, high = in_order(bit_ref, mine_ref, theirs_ref)
        back_ref[pl.ds(pl.multiple_of(step * rows, rows), rows)] = low

        @pl.when(step == 0)
        def _():
            back_ref[steps * rows :] = high

        @pl.when(step > 0)
        def _():
            qkv_ref[...] = high

    outs = [
        (shape((2, width, 3 * width), F32), pl.BlockSpec((None, rows, width), at_qkv)),
        (shape(back.shape, F32), pl.BlockSpec((None, ff, width), lambda j, bit: (0, 0, 0))),
    ]
    ins = [(pair[0], block), (pair[1], block), (back, ANY)]
    return unpack_call(body, "unpack_first", bit, (steps,), ins, outs, {3: 1}, 12 * steps * rows * width)


def unpack_second(bit, pair, gin, gout, qkv, sums, sumin):
    _, width, ff = gin.shape
    steps = ff // width
    block = pl.BlockSpec((width, width), lambda j, bit: (j, 0))
    tail = pl.BlockSpec((VECTOR_ROWS, width), lambda j, bit: (ff // VECTOR_ROWS, 0))

    def fixed(a):
        return pl.BlockSpec(a.shape, lambda j, bit: (0,) * len(a.shape))

    def body(bit_ref, mine_ref, theirs_ref, mine_v, theirs_v, sums_ref, sumin_ref, _, __, ___,
             in_ref, out_ref, qkv_ref, bqv_ref, bresid_ref, gain_ref, shift_ref, bin_ref):
        step = pl.program_id(0)
        low, high = in_order(bit_ref, mine_ref, theirs_ref)
        in_ref[...] = low

        @pl.when(step > 0)
        def _():
            qkv_ref[...] = high

        @pl.when(step == 0)
        def _():
            out_ref[...] = high
            value, _ = in_order(bit_ref, mine_v, theirs_v)
            for ref, lower, upper in (
                (bqv_ref, (value[0:1], value[1:2]), (value[12:13], sums_ref[6:7])),
                (bresid_ref, (value[2:3], value[3:4]), (sums_ref[0:1], sums_ref[1:2])),
                (gain_ref, (value[4:5], value[5:6]), (sums_ref[2:3], sums_ref[3:4])),
                (shift_ref, (value[6:7], value[7:8]), (sums_ref[4:5], sums_ref[5:6])),
            ):
                for level, both in enumerate((lower, upper)):
                    for k in range(2):
                        ref[level : level + 1, k * width : (k + 1) * width] = both[k]
            for k in range(ff // width):
                bin_ref[0:1, k * width : (k + 1) * width] = value[8 + k : 9 + k]
            bin_ref[1:2, :] = sumin_ref[...]

    outs = [
        (shape(gin.shape, F32), pl.BlockSpec((None, width, width), lambda j, bit: (0, 0, j))),
        (shape(gout.shape, F32), pl.BlockSpec((None, width, width), lambda j, bit: (0, 0, 0))),
        (shape(qkv.shape, F32), pl.BlockSpec((None, width, width), lambda j, bit: (0, 0, jnp.maximum(j - 1, 0)))),
    ]
    outs += [(s, fixed(s)) for s in [shape((2, 2 * width), F32)] * 4 + [shape((2, ff), F32)]]
    ins = [(pair[0], block), (pair[1], block), (pair[0], tail), (pair[1], tail), (sums, fixed(sums)), (sumin, fixed(sumin))]
    ins += [(gin, ANY), (gout, ANY), (qkv, ANY)]
    return unpack_call(body, "unpack_second", bit, (steps,), ins, outs, {7: 0, 8: 1, 9: 2}, 12 * steps * width * width)


def top_rows(context, resid, pair_index, weights):
    w_qkv, b_qv, w_out, b_resid, gain, shift, w_in, b_in, w_back = weights
    rows, width = context.shape
    pairs = rows // 2
    hat1, rstd1 = ln_stats(resid.astype(F32) + mm(context, w_out) + b_resid[:width])
    normed = hat1 * gain[:width] + shift[:width]
    normed_low = normed.astype(BF)
    activ, slope = gelu_pair(mm(normed_low, w_in) + b_in)
    activ = activ.astype(BF)
    hat2, rstd2 = ln_stats(normed + mm(activ, w_back) + b_resid[width:])
    pooled = hat2 * gain[width:] + shift[width:]
    radius = lax.rsqrt(jnp.sum(pooled * pooled, -1, keepdims=True) + unit_eps)
    unit = pooled * radius
    unit_low = unit.astype(BF)
    src, tgt = unit_low[:pairs], unit_low[pairs:]
    positive = (pair_index[:, None] == jnp.arange(pairs)[None, :]).astype(F32)
    logits = logit_scale * (mm_nt(src, tgt) - margin * positive)

    def soft(axis):
        powers = jnp.exp(logits - jnp.max(logits, axis, keepdims=True))
        return powers / jnp.sum(powers, axis, keepdims=True)

    dscore = (0.5 * logit_scale * (soft(1) + soft(0) - 2.0 * positive)).astype(BF)
    dunit = jnp.concatenate([mm(dscore, tgt), mm_tn(dscore, src)], 0)
    dy = radius * (dunit - unit * jnp.sum(dunit * unit, -1, keepdims=True))
    dg2, dc2 = colsum(dy * hat2), colsum(dy)
    dmixed = ln_back(dy, hat2, rstd2, gain[width:])
    dmixed_low = dmixed.astype(BF)
    dhidden = (mm_nt(dmixed_low, w_back) * slope).astype(BF)
    dnormed = dmixed + mm_nt(dhidden, w_in)
    dg1, dc1 = colsum(dnormed * hat1), colsum(dnormed)
    datt = ln_back(dnormed, hat1, rstd1, gain[:width])
    datt_low = datt.astype(BF)
    dctx = mm_nt(datt_low, w_out).astype(BF)
    grads = (mm_tn(context, datt_low), mm_tn(normed_low, dhidden), mm_tn(activ, dmixed_low))
    vectors = dict(
        bv=colsum(dctx),
        b_resid=jnp.concatenate([colsum(datt), colsum(dmixed)]),
        gain=jnp.concatenate([dg1, dg2]),
        shift=jnp.concatenate([dc1, dc2]),
        b_in=colsum(dhidden),
    )
    return datt, dctx, grads, vectors


def per_device(short_tokens, long_tokens, short_len, long_len, pair_index, *params):
    n = lax.axis_size("stream") * lax.axis_size("dp")
    index = lax.axis_index("stream") * lax.axis_size("dp") + lax.axis_index("dp")
    width = short_tokens.shape[-1]
    spans = (short_tokens.shape[2], long_tokens.shape[2])
    counts = (short_tokens.shape[1], long_tokens.shape[1])
    sents = sum(counts)
    w_qkv, b_qv, w_out, b_resid, gain, shift, w_in, b_in, w_back = params
    w = dict(qkv=w_qkv, b_qv=b_qv, out=w_out, b_resid=b_resid, gain=gain, shift=shift, b_in=b_in, back=w_back) | {"in": w_in}
    short, long = short_tokens.reshape(-1, width), long_tokens.reshape(-1, width)
    lens = jnp.concatenate([short_len.reshape(-1), long_len.reshape(-1)])
    lens_wide = jnp.repeat(lens, HEADS)[:, None]

    y, qkv, prob, ctx, hat1, rstd1, nlow, act, slope, hat2, rstd2 = forward(short, long, lens, w, spans[0], counts[0])
    sent, *kept = ask(y, lens_wide, w, spans, sents)
    every = gather_rows(sent, n)
    one_kernel = n * sents <= 512
    if one_kernel:
        own_datt, own_dctx, dy_top = top(index.reshape(1).astype(jnp.int32), every, pair_index[:, None], w, sents)
    else:
        datt, dctx, top_g, top_vec = top_rows(every[:, :width], every[:, width:], pair_index, tuple(p[1] for p in params))
        own_datt = lax.dynamic_slice_in_dim(datt, index * sents, sents, 0)
        own_dctx = lax.dynamic_slice_in_dim(dctx, index * sents, sents, 0)
    bits = my_bits(n)
    bit = bits[0].reshape(1).astype(jnp.int32)

    bucket1, dmixed, dmixed_low, sums2 = ask_back(y, kept, w, own_dctx, own_datt, hat2, rstd2, act, spans)
    first = Lane(bucket1.reshape(2, -1, width), n, bits)
    bucket2, dhidden, sumin = stage([first], lambda *a: hidden_back(*a, w), (dmixed_low, slope, nlow))
    bucket2, datt0, dctx0, sums1 = stage([first], lambda *a: normed_back(*a, w), (dhidden, dmixed, hat1, rstd1, ctx, bucket2))
    dqkv, bucket2 = stage([first], lambda *a: attention_back(*a, sums2, sumin, short, long), (qkv, prob, dctx0, sums1, bucket2))
    second = Lane(bucket2, n, bits)
    both = [first, second]
    dshort, dlong = stage(both, lambda *a: input_back(*a, w, counts[0] * spans[0]), (dqkv, datt0))
    if one_kernel:
        gout1, gin1, gback1, top_sums, top_sumin = stage(both, lambda *a: top_grads(*a, w), (every, dy_top))
    else:
        gout1, gin1, gback1 = (jnp.stack([g, g]) for g in top_g)
        rows_of = [top_vec[k].reshape(2, width) for k in ("b_resid", "gain", "shift")]
        top_sums = jnp.concatenate(rows_of + [top_vec["bv"][None], jnp.zeros((1, width), F32)], 0)
        top_sumin = top_vec["b_in"][None]
    while first.result is None:
        stage(both)
    g_qkv, g_back = stage([second], lambda *a: unpack_first(bit, *a), (first.result, gback1))
    while second.result is None:
        stage(both)
    g_in, g_out, g_qkv, g_bqv, g_bresid, g_gain, g_shift, g_bin = unpack_second(bit, second.result, gin1, gout1, g_qkv, top_sums, top_sumin)
    outs = (g_qkv, g_bqv, g_out, g_bresid, g_gain, g_shift, g_in, g_bin, g_back)
    return outs + (dshort.reshape((1, counts[0], spans[0], width)), dlong.reshape((1, counts[1], spans[1], width)))


def solution(mesh):
    split = P("stream", "dp", None, None)
    in_specs = (split, split, P("stream", "dp"), P("stream", "dp")) + (P(),) * 10
    out_specs = (P(),) * 9 + (split, split)
    return jax.shard_map(per_device, mesh=mesh, in_specs=in_specs, out_specs=out_specs, check_vma=False)
```

```python
import functools
import math

import jax
import jax.numpy as jnp
from jax import lax
from jax.experimental import pallas as pl
from jax.experimental.pallas import tpu as pltpu
from jax.sharding import PartitionSpec as P

HEADS = 8
BF = jnp.bfloat16
F32 = jnp.float32
AXES = ("stream", "dp")
logit_scale = 40.0
margin = 0.3
norm_eps = 1e-12
unit_eps = 1e-06
BLOCK = 128
STEP = 256
VMEM = 30 * 1024 * 1024


def mm(a, b):
    return jnp.dot(a, b, preferred_element_type=F32)


def mm_nt(a, b):
    return lax.dot_general(a, b, (((1,), (1,)), ((), ())), preferred_element_type=F32)


def mm_tn(a, b):
    return lax.dot_general(a, b, (((0,), (0,)), ((), ())), preferred_element_type=F32)


def ln_stats(v):
    centre = v - jnp.mean(v, -1, keepdims=True)
    rstd = lax.rsqrt(jnp.mean(centre * centre, -1, keepdims=True) + norm_eps)
    return centre * rstd, rstd


def ln_back(dy, vhat, rstd, gain):
    dhat = dy * gain
    return (dhat - jnp.mean(dhat, -1, keepdims=True) - vhat * jnp.mean(dhat * vhat, -1, keepdims=True)) * rstd


def gelu_pair(v):
    cdf = 0.5 * (1.0 + lax.erf(v * (1.0 / math.sqrt(2.0))))
    pdf = jnp.exp(-0.5 * v * v) * (1.0 / math.sqrt(2.0 * math.pi))
    return v * cdf, cdf + v * pdf


def colsum(v):
    return jnp.sum(v.astype(F32), 0)


def rowsum(v):
    return jnp.sum(v.astype(F32), 0, keepdims=True)


SMEM = pl.BlockSpec(memory_space=pltpu.SMEM)
ANY = pl.BlockSpec(memory_space=pl.ANY)


def hbm(a):
    return pltpu.with_memory_space_constraint(a, memory_space=pltpu.HBM)


def hbm_shape(dims, dtype):
    return pltpu.HBM(dims, dtype)


def whole(a):
    return pl.BlockSpec(a.shape, lambda i: (0,) * len(a.shape))


def shape(dims, dtype):
    return jax.ShapeDtypeStruct(dims, dtype)


def layer_of(a, level, rows=None, cols=None, at=lambda i: (0, 0)):
    rows, cols = rows or a.shape[1], cols or a.shape[2]
    return a, pl.BlockSpec((None, rows, cols), lambda i: (level, *at(i)))


def kernel_call(body, name, grid, ins, outs, flops, scratch=(), aliases=None, vmem=VMEM):
    size = sum(a.size * a.dtype.itemsize for a, _ in ins) + sum(
        math.prod(s.shape) * jnp.dtype(s.dtype).itemsize for s, _ in outs
    )
    return pl.pallas_call(
        body,
        grid=grid,
        in_specs=[s for _, s in ins],
        out_specs=[s for _, s in outs],
        out_shape=[s for s, _ in outs],
        scratch_shapes=list(scratch),
        input_output_aliases=aliases or {},
        compiler_params=pltpu.CompilerParams(vmem_limit_bytes=vmem),
        cost_estimate=pl.CostEstimate(flops=int(flops), bytes_accessed=int(size), transcendentals=0),
        name=name,
    )(*[hbm(a) if s is ANY else a for a, s in ins])


def routes(n):
    top, y = n >> 1, 2
    rest = [1 << k for k in range(2, n.bit_length() - 2)]
    for k in range(1, len(rest)):
        rest[k] |= rest[k - 1]
    halved = [(1, 1), (top, y), (y, top)]
    added = list(zip(rest, rest[::-1]))
    return halved, added


def swap(value, n, hop):
    return lax.ppermute(value, AXES, [(i, i ^ (hop[1] if i & 1 else hop[0])) for i in range(n)])


def device_index():
    return lax.axis_index("stream") * lax.axis_size("dp") + lax.axis_index("dp")


def coordinate(index, hop, n):
    value = (index // (1 << (hop.bit_length() - 1))) % 2
    if hop in (1, 2, n >> 1) or 2 * hop >= n >> 1:
        return value
    above = (index // (1 << hop.bit_length())) % 2
    return value + above - 2 * value * above


def my_bits(n):
    index = device_index()
    core = index % 2
    halved, _ = routes(n)
    return [jnp.where(core == 0, coordinate(index, a, n), coordinate(index, b, n)) for a, b in halved]


def split_body(bit_ref, mine_a, got_a, mine_b, got_b, keep_ref, send_ref):
    keep_ref[...] = (mine_a[...].astype(F32) + got_a[...].astype(F32)).astype(BF)
    send_ref[...] = (mine_b[...].astype(F32) + got_b[...].astype(F32)).astype(BF)


def add_and_split(mine, got, bit):
    rows, width = mine.shape[0] // 2, mine.shape[1]
    steps = 2 if rows % 32 == 0 and rows >= 256 else 1
    block = rows // steps
    kept = pl.BlockSpec((block, width), lambda j, bit: (bit[0] * steps + j, 0))
    sent = pl.BlockSpec((block, width), lambda j, bit: ((1 - bit[0]) * steps + j, 0))
    out = pl.BlockSpec((block, width), lambda j, bit: (j, 0))
    ins = [(mine, kept), (got, kept), (mine, sent), (got, sent)]
    outs = [(shape((rows, width), BF), out)] * 2
    return unpack_call(split_body, "add_and_split", bit.reshape(1).astype(jnp.int32), (steps,), ins, outs, {}, 12 * rows * width)


def sum_steps(keep, send, n, bits):
    halved, added = routes(n)
    for k, hop in enumerate(halved[:-1]):
        got = yield send, hop
        keep, send = add_and_split(keep, got, bits[k + 1])
    got = yield send, halved[-1]
    cur = (keep.astype(F32) + got.astype(F32)).astype(BF)
    for hop in added:
        got = yield cur, hop
        cur = (cur.astype(F32) + got.astype(F32)).astype(BF)
    for hop, bit in reversed(list(zip(halved, bits))[1:]):
        got = yield cur, hop
        low = jnp.where(bit == 0, cur, got)
        high = jnp.where(bit == 0, got, cur)
        cur = jnp.concatenate([low, high], 0)
    got = yield cur, halved[0]
    return cur, got


class Lane:
    def __init__(self, steps, n):
        self.n, self.steps, self.result = n, steps, None
        self.ask = next(self.steps)

    def feed(self, got):
        try:
            self.ask = self.steps.send(got)
        except StopIteration as end:
            self.result = end.value


def stage(lanes, work=None, args=()):
    lanes = [lane for lane in lanes if lane.result is None]
    asked, args = lax.optimization_barrier(([lane.ask[0] for lane in lanes], args))
    got = [swap(value, lane.n, lane.ask[1]) for value, lane in zip(asked, lanes)]
    out = work(*args) if work else ()
    got, out = lax.optimization_barrier((got, out))
    for lane, value in zip(lanes, got):
        lane.feed(value)
    return out


def gather_rows(rows, n):
    index = device_index()
    cur = rows[None]
    for flip in [1 << k for k in range(1, n.bit_length() - 1)] + [1]:
        got = swap(cur, n, (flip, flip))
        bit = (index // flip) % 2
        low, high = jnp.where(bit == 0, cur, got), jnp.where(bit == 0, got, cur)
        cur = jnp.stack([low, high], 1 if flip == 1 else 0).reshape((2 * cur.shape[0],) + rows.shape)
    return cur.reshape(n * rows.shape[0], rows.shape[1])


def stream_in(pairs, sems):
    loads = [pltpu.make_async_copy(a, b, sems.at[k]) for k, (a, b) in enumerate(pairs)]
    for load in loads:
        load.start()
    return loads


class Halves:
    def __init__(self, keep, send, block, sems):
        self.keep, self.send, self.block, self.sems = keep, send, block, sems
        self.low_is_kept = lax.axis_index("dp") % 2 == 0
        self.pieces = 0
        self.waits = []

    def put(self, at, value):
        self.block[at : at + value.shape[0]] = value
        half = self.keep.shape[0]
        end = at + value.shape[0]
        for lower, a, b in ((True, at, min(end, half)), (False, max(at, half), end)):
            if a >= b:
                continue
            base = 0 if lower else half
            sem = self.sems.at[self.pieces]
            self.pieces += 1
            copies = [
                pltpu.make_async_copy(self.block.at[a:b], ref.at[a - base : b - base], sem) for ref in (self.keep, self.send)
            ]
            kept = self.low_is_kept if lower else jnp.logical_not(self.low_is_kept)

            @pl.when(kept)
            def _(copy=copies[0]):
                copy.start()

            @pl.when(jnp.logical_not(kept))
            def _(copy=copies[1]):
                copy.start()

            self.waits.append(copies[0])

    def finish(self):
        for copy in self.waits:
            copy.wait()


def halves(v, first):
    zero = jnp.zeros_like(v)
    return jnp.concatenate([jnp.where(first, v, zero), jnp.where(first, zero, v)], 0)


def join_halves(v, first):
    return jnp.where(first, v[: v.shape[0] // 2], v[v.shape[0] // 2 :])


def first_head(width):
    return lax.broadcasted_iota(jnp.int32, (1, 2 * width // HEADS), 1) < width // HEADS


def key_bias(lens_ref, block, span_short, count_short):
    key = lax.broadcasted_iota(jnp.int32, (BLOCK, 1), 0)
    query = lax.broadcasted_iota(jnp.int32, (1, BLOCK), 1)
    per = BLOCK // span_short
    blocks_short = count_short // per
    is_short = block < blocks_short
    at = jnp.where(is_short, block * per, count_short + block - blocks_short)
    limit = jnp.zeros((BLOCK, 1), jnp.int32)
    for s in range(per):
        inside = key // span_short == s
        limit = jnp.where(inside, jnp.where(is_short, lens_ref[at + jnp.where(is_short, s, 0)] + s * span_short, 0), limit)
    limit = jnp.where(is_short, limit, lens_ref[at])
    same = (key // span_short == query // span_short) | jnp.logical_not(is_short)
    return jnp.where((key < limit) & same, 0.0, -jnp.inf).astype(F32)


def vectors(level, width, bqv_ref, bresid_ref, gain_ref, shift_ref):
    row = slice(level, level + 1)
    low, high = slice(0, width), slice(width, 2 * width)
    return [ref[row, part] for ref in (bqv_ref, bresid_ref, gain_ref, shift_ref) for part in (low, high)]


def forward_body(
    span, count, lens_ref, short_ref, long_ref, wqkv_ref, wout_ref, win_ref, wback_ref, bin_ref, bqv_ref, bresid_ref, gain_ref, shift_ref,
    y_ref, qkv_ref, prob_ref, ctx_ref, hat1_ref, rstd1_ref, act_ref, slope_ref, hat2_ref, rstd2_ref,
):
    step = pl.program_id(0)
    x = jnp.where(step == 0, short_ref[...], long_ref[...])
    rows, width = x.shape
    bq, bv, bo, bb, g1, g2, c1, c2 = vectors(0, width, bqv_ref, bresid_ref, gain_ref, shift_ref)
    pair = 2 * width // HEADS
    first = first_head(width)
    scale = 1.0 / math.sqrt(width // HEADS)
    bias = jnp.concatenate([bq, jnp.zeros_like(bq), bv], 1)
    qkv = (mm(x, wqkv_ref[...]) + bias).astype(BF)
    qkv_ref[...] = qkv
    blocks = []
    for b in range(rows // BLOCK):
        r = slice(b * BLOCK, (b + 1) * BLOCK)
        hide = key_bias(lens_ref, step * (rows // BLOCK) + b, span, count)
        hide = jnp.concatenate([hide, hide], 1)
        cols = []
        for p in range(HEADS // 2):
            q, k, v = (qkv[r, m * width + p * pair : m * width + (p + 1) * pair] for m in range(3))
            logit = mm_nt(k, halves(q, first)) * scale + hide
            power = jnp.exp(logit - jnp.max(logit, 0, keepdims=True))
            prob = (power * (1.0 / jnp.sum(power, 0, keepdims=True))).astype(BF)
            prob_ref[b, p] = prob
            cols.append(join_halves(mm_tn(prob, v), first))
        blocks.append(jnp.concatenate(cols, 1).astype(BF))
    ctx = jnp.concatenate(blocks, 0)
    ctx_ref[...] = ctx
    hat1, rstd1 = ln_stats(x.astype(F32) + mm(ctx, wout_ref[...]) + bo)
    normed = hat1 * g1 + c1
    low = normed.astype(BF)
    hat1_ref[...] = hat1.astype(BF)
    rstd1_ref[...] = jnp.broadcast_to(rstd1, rstd1_ref.shape)
    act, slope = gelu_pair(mm(low, win_ref[...]) + bin_ref[0:1])
    act = act.astype(BF)
    act_ref[...] = act
    slope_ref[...] = slope.astype(BF)
    hat2, rstd2 = ln_stats(normed + mm(act, wback_ref[...]) + bb)
    hat2_ref[...] = hat2.astype(BF)
    rstd2_ref[...] = jnp.broadcast_to(rstd2, rstd2_ref.shape)
    y_ref[...] = (hat2 * g2 + c2).astype(BF)


def by_rows(cols):
    return pl.BlockSpec((STEP, cols), lambda i: (i, 0))


def from_buckets(short, long):
    width = short.shape[1]
    return [
        (short, pl.BlockSpec((STEP, width), lambda i: (0, 0))),
        (long, pl.BlockSpec((STEP, width), lambda i: (jnp.maximum(i - 1, 0), 0))),
    ]


def small_ins(w):
    return [(w[k], whole(w[k])) for k in ("b_qv", "b_resid", "gain", "shift")]


def forward(short, long, lens, w, span, count):
    rows, width = short.shape[0] + long.shape[0], short.shape[1]
    ff = w["in"].shape[2]
    per = STEP // BLOCK
    prob = pl.BlockSpec((per, HEADS // 2, BLOCK, 2 * BLOCK), lambda i: (i, 0, 0, 0))
    ins = [(lens, SMEM)] + from_buckets(short, long)
    ins += [layer_of(w[name], 0) for name in ("qkv", "out", "in", "back")] + [(w["b_in"], whole(w["b_in"]))] + small_ins(w)
    far = [False] + [True] * 9
    cols = [(width, BF), (3 * width, BF), None, (width, BF), (width, BF), (128, F32), (ff, BF), (ff, BF), (width, BF), (128, F32)]
    outs = [((hbm_shape if f else shape)((rows, c[0]), c[1]), by_rows(c[0])) if c else (hbm_shape((rows // BLOCK, HEADS // 2, BLOCK, 2 * BLOCK), BF), prob) for c, f in zip(cols, far)]
    body = functools.partial(forward_body, span, count)
    return kernel_call(body, "layer0_forward", (rows // STEP,), ins, outs, 2 * rows * width * (4 * width + 2 * ff))


def starts(sents, spans, rows):
    s = lax.broadcasted_iota(jnp.int32, (sents, rows), 0)
    r = lax.broadcasted_iota(jnp.int32, (sents, rows), 1)
    half = sents // 2
    at = jnp.where(s < half, s * spans[0], half * spans[0] + (s - half) * spans[1])
    return (r == at).astype(BF)


def spread(sents):
    a = lax.broadcasted_iota(jnp.int32, (sents * HEADS, sents), 0) // HEADS
    return (a == lax.broadcasted_iota(jnp.int32, (sents * HEADS, sents), 1)).astype(BF)


def own_head(sents, width):
    a = lax.broadcasted_iota(jnp.int32, (sents * HEADS, width), 0) % HEADS
    return a == lax.broadcasted_iota(jnp.int32, (sents * HEADS, width), 1) // (width // HEADS)


def sum_heads(v, keep, sents):
    return jnp.sum(jnp.where(keep, v, 0.0).reshape(sents, HEADS, v.shape[1]), 1)


def ask_body(spans, y_ref, lens_ref, wqkv_ref, bqv_ref, wout_ref, bresid_ref, out_ref, ctx_ref, wide_ref, key_ref, prob_ref, mixed_ref):
    y = y_ref[...]
    rows, width = y.shape
    sents = out_ref.shape[0]
    keep = own_head(sents, width)
    cls = mm(starts(sents, spans, rows), y).astype(BF)
    q = (mm(cls, wqkv_ref[:, :width]) + bqv_ref[1:2, :width]).astype(BF)
    wide = jnp.where(keep, mm(spread(sents), q), 0.0).astype(BF)
    key = mm_nt(wide, wqkv_ref[:, width : 2 * width]).astype(BF)
    half = sents // 2
    sent = lax.broadcasted_iota(jnp.int32, (sents * HEADS, 1), 0) // HEADS
    begin = jnp.where(sent < half, sent * spans[0], half * spans[0] + (sent - half) * spans[1])
    place = lax.broadcasted_iota(jnp.int32, (sents * HEADS, rows), 1) - begin
    seen = (place >= 0) & (place < lens_ref[...])
    logit = jnp.where(seen, mm_nt(key, y) * (1.0 / math.sqrt(width // HEADS)), -jnp.inf)
    power = jnp.exp(logit - jnp.max(logit, 1, keepdims=True))
    prob = (power * (1.0 / jnp.sum(power, 1, keepdims=True))).astype(BF)
    mixed = mm(prob, y).astype(BF)
    picked = sum_heads(mm(mixed, wqkv_ref[:, 2 * width :]), keep, sents)
    ctx = (picked + bqv_ref[1:2, width:]).astype(BF)
    ctx_ref[...] = ctx
    out_ref[...] = (cls.astype(F32) + mm(ctx, wout_ref[...]) + bresid_ref[1:2, :width]).astype(BF)
    wide_ref[...] = wide
    key_ref[...] = key
    prob_ref[...] = prob
    mixed_ref[...] = mixed


def ask(y, lens, w, spans, sents):
    rows, width = y.shape
    wide = sents * HEADS
    ins = [(y, whole(y)), (lens, whole(lens)), layer_of(w["qkv"], 1), (w["b_qv"], whole(w["b_qv"])), layer_of(w["out"], 1), (w["b_resid"], whole(w["b_resid"]))]
    outs = [(s, whole(s)) for s in [shape((sents, width), BF)] + [hbm_shape(d, BF) for d in ((sents, width), (wide, width), (wide, width), (wide, rows), (wide, width))]]
    return kernel_call(functools.partial(ask_body, spans), "layer1_ask", (1,), ins, outs, 2 * wide * width * (2 * rows + 3 * width))


def top_forward(attended, win_ref, bin_ref, g1, c1):
    hat1, rstd1 = ln_stats(attended.astype(F32))
    normed = hat1 * g1 + c1
    low = normed.astype(BF)
    return hat1, rstd1, normed, low, mm(low, win_ref[...]) + bin_ref[1:2]


def gelu(v):
    return v * (0.5 * (1.0 + lax.erf(v * (1.0 / math.sqrt(2.0)))))


def top_part(index_ref, every_ref, pair_ref, dy_ref, hat2_s, rstd2_s, low_vectors, bin_ref, win, wback, wout_ref, sents):
    pairs = pair_ref.shape[1]
    _, _, _, bb, g1, g2, c1, c2 = low_vectors
    hat1, _ = ln_stats(every_ref[...].astype(F32))
    normed = hat1 * g1 + c1
    win_ref = win()
    act = gelu(mm(normed.astype(BF), win_ref[...]) + bin_ref[1:2]).astype(BF)
    wback_ref = wback()
    hat2, rstd2 = ln_stats(normed + mm(act, wback_ref[...]) + bb)
    hat2_s[...] = hat2
    rstd2_s[...] = jnp.broadcast_to(rstd2, rstd2_s.shape)
    pooled = hat2 * g2 + c2
    radius = lax.rsqrt(jnp.sum(pooled * pooled, -1, keepdims=True) + unit_eps)
    unit = pooled * radius
    src, tgt = unit[:pairs].astype(BF), unit[pairs:].astype(BF)
    positive = (pair_ref[...] == lax.broadcasted_iota(jnp.int32, (pairs, pairs), 0)).astype(F32)
    logits = logit_scale * (mm_nt(tgt, src) - margin * positive)

    def soft(axis):
        powers = jnp.exp(logits - jnp.max(logits, axis, keepdims=True))
        return powers * (1.0 / jnp.sum(powers, axis, keepdims=True))

    dscore = (0.5 * logit_scale * (soft(1) + soft(0) - 2.0 * positive)).astype(BF)
    dunit = jnp.concatenate([mm_tn(dscore, tgt), mm(dscore, src)], 0)
    dy_ref[...] = radius * (dunit - unit * jnp.sum(dunit * unit, -1, keepdims=True))
    mine = pl.ds(pl.multiple_of(index_ref[0] * sents, sents), sents)
    own_hat1, own_rstd1, _, _, own_hid = top_forward(every_ref[mine], win_ref, bin_ref, g1, c1)
    dmixed = ln_back(dy_ref[mine], hat2_s[mine], rstd2_s[mine, 0:1], g2)
    dhidden = (mm_nt(dmixed.astype(BF), wback_ref[...]) * gelu_pair(own_hid)[1]).astype(BF)
    dnormed = dmixed + mm_nt(dhidden, win_ref[...])
    datt = ln_back(dnormed, own_hat1, own_rstd1, g1)
    return datt, mm_nt(datt.astype(BF), wout_ref[...]).astype(BF)


def top_grads_body(every_ref, dy_ref, wout_ref, win_ref, wback_ref, bin_ref, bqv_ref, bresid_ref, gain_ref, shift_ref,
                   gin_ref, gback_ref, sums_ref, sumin_ref):
    width = dy_ref.shape[1]
    _, _, _, bb, g1, g2, c1, c2 = vectors(1, width, bqv_ref, bresid_ref, gain_ref, shift_ref)
    hat1, rstd1, normed, low, hid = top_forward(every_ref[...], win_ref, bin_ref, g1, c1)
    act, slope = gelu_pair(hid)
    act = act.astype(BF)
    hat2, rstd2 = ln_stats(normed + mm(act, wback_ref[...]) + bb)
    dy = dy_ref[...]
    dmixed = ln_back(dy, hat2, rstd2, g2)
    dmixed_low = dmixed.astype(BF)
    gback_ref[...] = mm_tn(act, dmixed_low)
    dhidden = (mm_nt(dmixed_low, wback_ref[...]) * slope).astype(BF)
    gin_ref[...] = mm_tn(low, dhidden)
    dnormed = dmixed + mm_nt(dhidden, win_ref[...])
    datt = ln_back(dnormed, hat1, rstd1, g1)
    sumin_ref[...] = rowsum(dhidden)
    parts = (datt, dmixed, dnormed * hat1, dy * hat2, dnormed, dy, mm_nt(datt.astype(BF), wout_ref[...]).astype(BF))
    for k, part in enumerate(parts):
        sums_ref[k : k + 1] = rowsum(part)
    sums_ref[7:8] = jnp.zeros((1, width), F32)


def top_grads(every, dy, w):
    width = dy.shape[1]
    ff = w["in"].shape[2]
    rows = every.shape[0]
    ins = [(every, whole(every)), (dy, whole(dy))] + [layer_of(w[k], 1) for k in ("out", "in", "back")]
    ins += [(w["b_in"], whole(w["b_in"]))] + small_ins(w)

    def upper(a, b):
        return hbm_shape((2, a, b), F32), pl.BlockSpec((None, a, b), lambda i: (1, 0, 0))

    sums, sumin = shape((8, width), F32), shape((1, ff), F32)
    outs = [upper(width, ff), upper(ff, width), (sums, whole(sums)), (sumin, whole(sumin))]
    return kernel_call(top_grads_body, "top_grads", (1,), ins, outs, 6 * rows * width * (width + 2 * ff))


def turn_body(spans, sents, with_top, *refs):
    refs = list(refs)

    def take(count):
        out, refs[:count] = refs[:count], []
        return out

    wide_ref, key_ref, prob_ref, mixed_ref, ctx_ref, gain_ref = take(6)
    wqkv_hbm, y_hbm, hat2_hbm, rstd2_hbm, act_hbm = take(5)
    if with_top:
        index_ref, every_ref, pair_ref, wout_ref, bin_ref, bqv_ref, bresid_ref, shift_ref, win_hbm, wback_hbm = take(10)
    else:
        datt_ref, dctx_ref = take(2)
    keep_hbm, send_hbm, low_ref, sums_ref = take(4)
    if with_top:
        (dy_ref,) = take(1)
    wqkv_ref, y_ref, hat2_ref, rstd2_ref, act_ref, block, got, sent = take(8)
    loads = [(wqkv_hbm.at[1], wqkv_ref), (y_hbm, y_ref), (hat2_hbm, hat2_ref), (rstd2_hbm, rstd2_ref), (act_hbm, act_ref)]
    if with_top:
        win_ref, wback_ref, top_hat2, top_rstd2 = take(4)
        loads = [(win_hbm.at[1], win_ref), (wback_hbm.at[1], wback_ref)] + loads
    loads = [pltpu.make_async_copy(a, b, got.at[k]) for k, (a, b) in enumerate(loads)]
    for load in loads:
        load.start()
    rows, width = y_ref.shape
    if with_top:

        def arrived(load, ref):
            def wait():
                load.wait()
                return ref

            return wait

        values = vectors(1, width, bqv_ref, bresid_ref, gain_ref, shift_ref)
        win, wback = arrived(loads[0], win_ref), arrived(loads[1], wback_ref)
        datt, dctx = top_part(index_ref, every_ref, pair_ref, dy_ref, top_hat2, top_rstd2, values, bin_ref, win, wback, wout_ref, sents)
        loads = loads[2:]
    else:
        datt, dctx = datt_ref[...], dctx_ref[...]
    keep = own_head(sents, width)
    first = starts(sents, spans, rows)
    prob_low = prob_ref[...]
    d_wide = jnp.where(keep, mm(spread(sents), dctx), 0.0).astype(BF)
    loads[0].wait()
    d_value = mm_nt(d_wide, wqkv_ref[:, 2 * width :]).astype(BF)
    loads[1].wait()
    y = y_ref[...]
    dprob = mm_nt(d_value, y)
    prob = prob_low.astype(F32)
    dlogit = prob * (dprob - jnp.sum(prob * dprob, 1, keepdims=True))
    dscore = (dlogit * (1.0 / math.sqrt(width // HEADS))).astype(BF)
    pulled = mm(dscore, y).astype(BF)
    dq = sum_heads(mm(pulled, wqkv_ref[:, width : 2 * width]), keep, sents).astype(BF)
    dcls = mm_nt(dq, wqkv_ref[:, :width]) + datt
    high = dcls.astype(BF)
    left = jnp.concatenate([dscore, prob_low, first, first], 0)
    right = jnp.concatenate([key_ref[...], d_value, high, (dcls - high.astype(F32)).astype(BF)], 0)
    dy = mm_tn(left, right)
    loads[2].wait()
    loads[3].wait()
    hat2 = hat2_ref[...].astype(F32)
    dmixed = ln_back(dy, hat2, rstd2_ref[:, 0:1], gain_ref[0:1, width:])
    low_ref[...] = dmixed.astype(BF)
    sums_ref[0:1] = rowsum(dmixed)
    sums_ref[1:2] = rowsum(dy * hat2)
    sums_ref[2:3] = rowsum(dy)
    sums_ref[3:4] = rowsum(dq)
    sums_ref[4:8] = jnp.zeros((4, width), F32)
    place = Halves(keep_hbm, send_hbm, block, sent)
    ff = act_ref.shape[1]
    tiles = ff // width
    cls = mm(first, y).astype(BF)
    tail = ((cls, dq), (pulled, wide_ref[...]), (mixed_ref[...], d_wide), (ctx_ref[...], datt.astype(BF)))
    for k, (a, b) in enumerate(tail):
        place.put((tiles + k) * width, mm_tn(a, b).astype(BF))
    loads[4].wait()
    for k in range(tiles):
        place.put(k * width, mm_tn(act_ref[:, k * width : (k + 1) * width], low_ref[...]).astype(BF))
    place.finish()


def turn(top_args, y, kept, w, hat2, rstd2, act, spans, sents):
    rows, width = y.shape
    ff = act.shape[1]
    ctx, wide, key, prob, mixed = kept
    with_top = len(top_args) == 3
    ins = [(a, whole(a)) for a in (wide, key, prob, mixed, ctx, w["gain"])]
    ins += [(a, ANY) for a in (w["qkv"], y, hat2, rstd2, act)]
    blocks = ff // width + 4
    outs = [(hbm_shape((blocks * width // 2, width), BF), ANY)] * 2
    outs += [(s, whole(s)) for s in (shape((rows, width), BF), shape((8, width), F32))]
    scratch = [pltpu.VMEM(d, t) for d, t in (((width, 3 * width), BF), ((rows, width), BF), ((rows, width), BF), ((rows, 128), F32), ((rows, ff), BF), ((blocks * width, width), BF))]
    scratch += [pltpu.SemaphoreType.DMA((7,)), pltpu.SemaphoreType.DMA((blocks,))]
    flops = 2 * rows * width * (ff + 512)
    if with_top:
        index, every, pair = top_args
        ins += [(index, SMEM), (every, whole(every)), (pair, whole(pair)), layer_of(w["out"], 1)]
        ins += [(w[k], whole(w[k])) for k in ("b_in", "b_qv", "b_resid", "shift")] + [(w["in"], ANY), (w["back"], ANY)]
        outs += [(hbm_shape(every.shape, F32), whole(every))]
        scratch += [pltpu.VMEM((width, ff), BF), pltpu.VMEM((ff, width), BF), pltpu.VMEM(every.shape, F32), pltpu.VMEM((every.shape[0], 128), F32)]
        flops += 4 * every.shape[0] * width * ff
    else:
        ins += [(a, whole(a)) for a in top_args]
    return kernel_call(functools.partial(turn_body, spans, sents, with_top), "turn", (1,), ins, outs, flops, scratch, vmem=VMEM + VMEM // 4)


VECTOR_ROWS = 128


def ff_back_body(low_ref, gain_ref, shift_ref, hat1_hbm, rstd1_hbm, wback_hbm, slope_hbm, win_hbm, wout_hbm, ctx_hbm,
                 keep_hbm, send_hbm, datt_ref, dctx_ref, sums_ref, sumin_ref,
                 hat1_ref, rstd1_ref, wback_ref, slope_ref, win_ref, wout_ref, ctx_ref, nlow_ref, dhidden_ref, block, got, sent):
    rows, width = low_ref.shape
    ff = slope_ref.shape[1]
    tiles = ff // width
    loads = [(hat1_hbm, hat1_ref)]
    for t in range(tiles):
        part = slice(t * width, (t + 1) * width)
        loads += [(wback_hbm.at[0, part], wback_ref.at[part]), (slope_hbm.at[:, part], slope_ref.at[:, part])]
    loads += [(win_hbm.at[0], win_ref), (rstd1_hbm, rstd1_ref), (wout_hbm.at[0], wout_ref), (ctx_hbm, ctx_ref)]
    loads = stream_in(loads, got)
    place = Halves(keep_hbm, send_hbm, block, sent)
    gain, shift = gain_ref[0:1, :width], shift_ref[0:1, :width]
    loads[0].wait()
    nlow_ref[...] = (hat1_ref[...].astype(F32) * gain + shift).astype(BF)
    for t in range(tiles):
        part = slice(t * width, (t + 1) * width)
        loads[1 + 2 * t].wait()
        loads[2 + 2 * t].wait()
        dhidden = (mm_nt(low_ref[...], wback_ref[part]) * slope_ref[:, part].astype(F32)).astype(BF)
        dhidden_ref[:, part] = dhidden
        sumin_ref[:, part] = rowsum(dhidden)
        place.put(t * width, mm_tn(nlow_ref[...], dhidden).astype(BF))
    for load in loads[1 + 2 * tiles :]:
        load.wait()
    sums_ref[...] = jnp.zeros_like(sums_ref)
    for r in range(0, rows, STEP):
        r = slice(r, r + STEP)
        dnormed = low_ref[r].astype(F32) + mm_nt(dhidden_ref[r], win_ref[...])
        hat1 = hat1_ref[r].astype(F32)
        datt = ln_back(dnormed, hat1, rstd1_ref[r, 0:1], gain)
        low = datt.astype(BF)
        datt_ref[r] = low
        dctx_ref[r] = mm_nt(low, wout_ref[...]).astype(BF)
        sums_ref[0:1] += rowsum(datt)
        sums_ref[1:2] += rowsum(dnormed * hat1)
        sums_ref[2:3] += rowsum(dnormed)
    place.put(ff, mm_tn(ctx_ref[...], datt_ref[...]).astype(BF))
    place.finish()


def ff_back(low, hat1, rstd1, slope, ctx, w):
    rows, width = low.shape
    ff = slope.shape[1]
    ins = [(low, whole(low)), (w["gain"], whole(w["gain"])), (w["shift"], whole(w["shift"]))]
    ins += [(a, ANY) for a in (hat1, rstd1, w["back"], slope, w["in"], w["out"], ctx)]
    half = (ff + width) // 2
    outs = [(hbm_shape((half, width), BF), ANY)] * 2
    outs += [(s, whole(s)) for s in (shape((rows, width), BF), shape((rows, width), BF), shape((8, width), F32), shape((1, ff), F32))]
    scratch = [((rows, width), BF), ((rows, 128), F32), ((ff, width), BF), ((rows, ff), BF), ((width, ff), BF), ((width, width), BF), ((rows, width), BF)]
    scratch += [((rows, width), BF), ((rows, ff), BF), ((ff + width, width), BF)]
    scratch = [pltpu.VMEM(d, t) for d, t in scratch]
    scratch += [pltpu.SemaphoreType.DMA((5 + 2 * (ff // width),)), pltpu.SemaphoreType.DMA((8,))]
    return kernel_call(ff_back_body, "layer0_ff_back", (1,), ins, outs, 2 * rows * width * (3 * ff + 2 * width), scratch)


def attention_back_body(qkv_ref, prob_ref, dctx_ref, short_ref, long_ref, sums1_ref, sums2_ref, sumin_ref, dqkv_ref, keep_hbm, send_hbm, acc, sums, block, sent):
    step = pl.program_id(0)
    x = jnp.where(step == 0, short_ref[...], long_ref[...])
    rows, width = x.shape
    pair = 2 * width // HEADS
    first = first_head(width)
    scale = 1.0 / math.sqrt(width // HEADS)

    @pl.when(step == 0)
    def _():
        acc[...] = jnp.zeros_like(acc)
        sums[...] = jnp.zeros_like(sums)

    pairs = range(HEADS // 2)
    c = [[slice(m * width + p * pair, m * width + (p + 1) * pair) for m in range(3)] for p in pairs]
    for b in range(rows // BLOCK):
        r = slice(b * BLOCK, (b + 1) * BLOCK)
        dd = [halves(dctx_ref[r, c[p][0]], first) for p in pairs]
        dprob = [mm_nt(qkv_ref[r, c[p][2]], dd[p]) for p in pairs]
        dscore = []
        for p in pairs:
            prob = prob_ref[b, p].astype(F32)
            dscore.append((prob * (dprob[p] - jnp.sum(prob * dprob[p], 0, keepdims=True)) * scale).astype(BF))
        dv = [mm(prob_ref[b, p], dd[p]).astype(BF) for p in pairs]
        dk = [mm(dscore[p], halves(qkv_ref[r, c[p][0]], first)).astype(BF) for p in pairs]
        dq = [join_halves(mm_tn(dscore[p], qkv_ref[r, c[p][1]]), first).astype(BF) for p in pairs]
        dqkv_ref[r] = jnp.concatenate(dq + dk + dv, 1)
    dqkv = dqkv_ref[...]
    acc[...] += mm_tn(x, dqkv)
    sums[0:1] += rowsum(dqkv)

    @pl.when(step == pl.num_programs(0) - 1)
    def _():
        place = Halves(keep_hbm, send_hbm, block, sent)
        for m in range(3):
            place.put(m * width, acc[:, m * width : (m + 1) * width].astype(BF))
        rows_of = [sums[0:1, :width], sums[0:1, 2 * width :]]
        for k in range(3):
            rows_of += [sums1_ref[k : k + 1], sums2_ref[k : k + 1]]
        rows_of += [sumin_ref[:, k * width : (k + 1) * width] for k in range(sumin_ref.shape[1] // width)]
        rows_of += [sums2_ref[3:4], jnp.zeros((3, width), F32)]
        rows_of += [jnp.zeros((VECTOR_ROWS - 16, width), F32)]
        place.put(3 * width, jnp.concatenate(rows_of, 0).astype(BF))
        place.finish()


def attention_back(qkv, prob, dctx, sums1, sums2, sumin, short, long):
    rows, width = dctx.shape
    per = STEP // BLOCK
    ins = [(qkv, by_rows(3 * width)), (prob, pl.BlockSpec((per,) + prob.shape[1:], lambda i: (i, 0, 0, 0))), (dctx, by_rows(width))]
    ins += from_buckets(short, long) + [(a, whole(a)) for a in (sums1, sums2, sumin)]
    total = 3 * width + VECTOR_ROWS
    outs = [(hbm_shape((rows, 3 * width), BF), by_rows(3 * width))] + [(hbm_shape((total // 2, width), BF), ANY)] * 2
    scratch = [pltpu.VMEM((width, 3 * width), F32), pltpu.VMEM((8, 3 * width), F32), pltpu.VMEM((total, width), BF), pltpu.SemaphoreType.DMA((8,))]
    flops = 2 * rows * width * (3 * width + 10 * BLOCK)
    return kernel_call(attention_back_body, "layer0_attention_back", (rows // STEP,), ins, outs, flops, scratch)


def input_back_body(dqkv_ref, datt_ref, wqkv_ref, short_ref, long_ref):
    dx = datt_ref[...].astype(F32) + mm_nt(dqkv_ref[...], wqkv_ref[...])

    @pl.when(pl.program_id(0) == 0)
    def _():
        short_ref[...] = dx

    @pl.when(pl.program_id(0) > 0)
    def _():
        long_ref[...] = dx


def input_back(dqkv, datt, w, cut):
    rows, width = datt.shape
    ins = [(dqkv, by_rows(3 * width)), (datt, by_rows(width)), layer_of(w["qkv"], 0)]
    outs = [
        (shape((cut, width), F32), pl.BlockSpec((STEP, width), lambda i: (0, 0))),
        (shape((rows - cut, width), F32), pl.BlockSpec((STEP, width), lambda i: (jnp.maximum(i - 1, 0), 0))),
    ]
    return kernel_call(input_back_body, "layer0_input_back", (rows // STEP,), ins, outs, 2 * rows * width * 3 * width)


def unpack_call(body, name, bit, grid, ins, outs, aliases, size):
    return pl.pallas_call(
        body,
        grid_spec=pltpu.PrefetchScalarGridSpec(
            num_scalar_prefetch=1,
            grid=grid,
            in_specs=[s for _, s in ins],
            out_specs=[s for _, s in outs],
        ),
        out_shape=[s for s, _ in outs],
        input_output_aliases=aliases,
        compiler_params=pltpu.CompilerParams(vmem_limit_bytes=VMEM),
        cost_estimate=pl.CostEstimate(flops=0, bytes_accessed=size, transcendentals=0),
        name=name,
    )(bit, *[hbm(a) if s is ANY else a for a, s in ins])


def in_order(bit_ref, mine_ref, theirs_ref):
    mine, theirs = mine_ref[...].astype(F32), theirs_ref[...].astype(F32)
    low = bit_ref[0] == 0
    return jnp.where(low, mine, theirs), jnp.where(low, theirs, mine)


def unpack_first(bit, pair, back):
    _, ff, width = back.shape
    steps = ff // width
    block = pl.BlockSpec((width, width), lambda j, bit: (j, 0))

    def body(bit_ref, mine_ref, theirs_ref, _, qkv_ref, out_ref, back_ref):
        low, high = in_order(bit_ref, mine_ref, theirs_ref)
        back_ref[...] = low
        step = pl.program_id(0)

        @pl.when(step < steps - 1)
        def _():
            qkv_ref[...] = high

        @pl.when(step == steps - 1)
        def _():
            out_ref[...] = high

    outs = [
        (shape((2, width, 3 * width), F32), pl.BlockSpec((None, width, width), lambda j, bit: (1, 0, jnp.minimum(j, 2)))),
        (shape((2, width, width), F32), pl.BlockSpec((None, width, width), lambda j, bit: (1, 0, 0))),
        (shape(back.shape, F32), pl.BlockSpec((None, width, width), lambda j, bit: (0, j, 0))),
    ]
    ins = [(pair[0], block), (pair[1], block), (back, ANY)]
    return unpack_call(body, "unpack_first", bit, (steps,), ins, outs, {3: 2}, 12 * steps * width * width)


def unpack_second(bit, pair, gin, gout):
    _, width, ff = gin.shape
    rows = width // 2
    half = pair[0].shape[0] // rows
    count = 2 * ff // width
    block = [pl.BlockSpec((rows, width), lambda j, bit, low=low: (jnp.where((bit[0] == 0) == low, jnp.minimum(j, half - 1), jnp.maximum(j - half, 0)), 0)) for low in (True, False)]

    def body(bit_ref, mine_ref, theirs_ref, _, __, in_ref, out_ref):
        step = pl.program_id(0)
        mine = (step < half) == (bit_ref[0] == 0)
        value = jnp.where(mine, mine_ref[...], theirs_ref[...]).astype(F32)

        @pl.when(step < count)
        def _():
            in_ref[...] = value

        @pl.when(step >= count)
        def _():
            out_ref[...] = value

    def at_in(j, bit):
        j = jnp.minimum(j, count - 1)
        return 0, j % 2, j // 2

    outs = [
        (shape(gin.shape, F32), pl.BlockSpec((None, rows, width), at_in)),
        (shape(gout.shape, F32), pl.BlockSpec((None, rows, width), lambda j, bit: (0, jnp.maximum(j - count, 0), 0))),
    ]
    ins = [(pair[0], block[0]), (pair[1], block[1]), (gin, ANY), (gout, ANY)]
    return unpack_call(body, "unpack_second", bit, (2 * half,), ins, outs, {3: 0, 4: 1}, 12 * half * rows * width)


def unpack_third(bit, pair, qkv, sums, sumin):
    _, width, _ = qkv.shape
    ff = sumin.shape[1]
    total = 3 * width + VECTOR_ROWS

    def fixed(a):
        return pl.BlockSpec(a.shape, lambda j, bit: (0,) * len(a.shape))

    def body(bit_ref, mine_ref, theirs_ref, _, sums_ref, sumin_ref, qkv_ref, bqv_ref, bresid_ref, gain_ref, shift_ref, bin_ref):
        low, high = in_order(bit_ref, mine_ref, theirs_ref)
        value = jnp.concatenate([low, high], 0)
        for m in range(3):
            qkv_ref[:, m * width : (m + 1) * width] = value[m * width : (m + 1) * width]
        value = value[3 * width :]
        for ref, lower, upper in (
            (bqv_ref, (value[0:1], value[1:2]), (value[12:13], sums_ref[6:7])),
            (bresid_ref, (value[2:3], value[3:4]), (sums_ref[0:1], sums_ref[1:2])),
            (gain_ref, (value[4:5], value[5:6]), (sums_ref[2:3], sums_ref[3:4])),
            (shift_ref, (value[6:7], value[7:8]), (sums_ref[4:5], sums_ref[5:6])),
        ):
            for level, both in enumerate((lower, upper)):
                for k in range(2):
                    ref[level : level + 1, k * width : (k + 1) * width] = both[k]
        for k in range(ff // width):
            bin_ref[0:1, k * width : (k + 1) * width] = value[8 + k : 9 + k]
        bin_ref[1:2, :] = sumin_ref[...]

    outs = [(shape(qkv.shape, F32), pl.BlockSpec((None, width, 3 * width), lambda j, bit: (0, 0, 0)))]
    outs += [(s, fixed(s)) for s in [shape((2, 2 * width), F32)] * 4 + [shape((2, ff), F32)]]
    ins = [(pair[0], fixed(pair[0])), (pair[1], fixed(pair[1])), (qkv, ANY), (sums, fixed(sums)), (sumin, fixed(sumin))]
    return unpack_call(body, "unpack_third", bit, (1,), ins, outs, {3: 0}, 6 * total * width)


def top_rows(attended, pair_index, weights):
    w_qkv, b_qv, w_out, b_resid, gain, shift, w_in, b_in, w_back = weights
    rows, width = attended.shape
    pairs = rows // 2
    hat1, rstd1 = ln_stats(attended.astype(F32))
    normed = hat1 * gain[:width] + shift[:width]
    normed_low = normed.astype(BF)
    activ, slope = gelu_pair(mm(normed_low, w_in) + b_in)
    activ = activ.astype(BF)
    hat2, rstd2 = ln_stats(normed + mm(activ, w_back) + b_resid[width:])
    pooled = hat2 * gain[width:] + shift[width:]
    radius = lax.rsqrt(jnp.sum(pooled * pooled, -1, keepdims=True) + unit_eps)
    unit = pooled * radius
    unit_low = unit.astype(BF)
    src, tgt = unit_low[:pairs], unit_low[pairs:]
    positive = (pair_index[:, None] == jnp.arange(pairs)[None, :]).astype(F32)
    logits = logit_scale * (mm_nt(src, tgt) - margin * positive)

    def soft(axis):
        powers = jnp.exp(logits - jnp.max(logits, axis, keepdims=True))
        return powers / jnp.sum(powers, axis, keepdims=True)

    dscore = (0.5 * logit_scale * (soft(1) + soft(0) - 2.0 * positive)).astype(BF)
    dunit = jnp.concatenate([mm(dscore, tgt), mm_tn(dscore, src)], 0)
    dy = radius * (dunit - unit * jnp.sum(dunit * unit, -1, keepdims=True))
    dg2, dc2 = colsum(dy * hat2), colsum(dy)
    dmixed = ln_back(dy, hat2, rstd2, gain[width:])
    dmixed_low = dmixed.astype(BF)
    dhidden = (mm_nt(dmixed_low, w_back) * slope).astype(BF)
    dnormed = dmixed + mm_nt(dhidden, w_in)
    dg1, dc1 = colsum(dnormed * hat1), colsum(dnormed)
    datt = ln_back(dnormed, hat1, rstd1, gain[:width])
    datt_low = datt.astype(BF)
    dctx = mm_nt(datt_low, w_out).astype(BF)
    grads = (mm_tn(normed_low, dhidden), mm_tn(activ, dmixed_low))
    vectors = dict(
        bv=colsum(dctx),
        b_resid=jnp.concatenate([colsum(datt), colsum(dmixed)]),
        gain=jnp.concatenate([dg1, dg2]),
        shift=jnp.concatenate([dc1, dc2]),
        b_in=colsum(dhidden),
    )
    return datt, dctx, grads, vectors


def per_device(short_tokens, long_tokens, short_len, long_len, pair_index, *params):
    n = lax.axis_size("stream") * lax.axis_size("dp")
    index = lax.axis_index("stream") * lax.axis_size("dp") + lax.axis_index("dp")
    width = short_tokens.shape[-1]
    spans = (short_tokens.shape[2], long_tokens.shape[2])
    counts = (short_tokens.shape[1], long_tokens.shape[1])
    sents = sum(counts)
    w_qkv, b_qv, w_out, b_resid, gain, shift, w_in, b_in, w_back = params
    w_qkv, b_qv, w_out, b_resid, gain, shift, w_in, b_in, w_back = (hbm(p) for p in (w_qkv, b_qv, w_out, b_resid, gain, shift, w_in, b_in, w_back))
    w = dict(qkv=w_qkv, b_qv=b_qv, out=w_out, b_resid=b_resid, gain=gain, shift=shift, b_in=b_in, back=w_back) | {"in": w_in}
    short, long = hbm(short_tokens.reshape(-1, width)), hbm(long_tokens.reshape(-1, width))
    lens = jnp.concatenate([short_len.reshape(-1), long_len.reshape(-1)])
    lens_wide = jnp.repeat(lens, HEADS)[:, None]

    y, *far = forward(short, long, lens, w, spans[0], counts[0])
    qkv, prob, ctx, hat1, rstd1, act, slope, hat2, rstd2 = (hbm(a) for a in far)
    sent, *kept = ask(y, lens_wide, w, spans, sents)
    every = gather_rows(sent, n)
    one_kernel = n * sents <= 512
    if one_kernel:
        top_args = (index.reshape(1).astype(jnp.int32), every, pair_index[None, :])
    else:
        datt, dctx, top_g, top_vec = top_rows(every, pair_index, tuple(p[1] for p in params))
        top_args = tuple(lax.dynamic_slice_in_dim(v, index * sents, sents, 0) for v in (datt, dctx))
    bits = my_bits(n)
    bit = bits[0].reshape(1).astype(jnp.int32)

    keep, send, dlow, sums2, *dy_top = turn(top_args, y, [hbm(a) for a in kept], w, hat2, rstd2, act, spans, sents)
    first = Lane(sum_steps(keep, send, n, bits), n)
    keep, send, datt0, dctx0, sums1, sumin = stage([first], lambda *a: ff_back(*a, w), (dlow, hat1, rstd1, slope, ctx))
    second = Lane(sum_steps(keep, send, n, bits), n)
    dqkv, keep, send = stage([first, second], lambda *a: attention_back(*a, short, long), (qkv, prob, dctx0, sums1, sums2, sumin))
    third = Lane(sum_steps(keep, send, n, bits), n)
    lanes = [first, second, third]
    dshort, dlong = stage(lanes, lambda *a: input_back(*a, w, counts[0] * spans[0]), (hbm(dqkv), datt0))
    if one_kernel:
        gin1, gback1, top_sums, top_sumin = stage(lanes, lambda *a: top_grads(*a, w), (every, *dy_top))
    else:
        gin1, gback1 = (jnp.stack([g, g]) for g in top_g)
        rows_of = [top_vec[k].reshape(2, width) for k in ("b_resid", "gain", "shift")]
        top_sums = jnp.concatenate(rows_of + [top_vec["bv"][None], jnp.zeros((1, width), F32)], 0)
        top_sumin = top_vec["b_in"][None]
    while first.result is None:
        stage(lanes)
    g_qkv, g_out, g_back = stage(lanes, lambda *a: unpack_first(bit, *a), (first.result, gback1))
    while second.result is None:
        stage(lanes)
    g_in, g_out = stage(lanes, lambda *a: unpack_second(bit, *a), (second.result, gin1, g_out))
    while third.result is None:
        stage(lanes)
    g_qkv, g_bqv, g_bresid, g_gain, g_shift, g_bin = unpack_third(bit, third.result, g_qkv, top_sums, top_sumin)
    outs = (g_qkv, g_bqv, g_out, g_bresid, g_gain, g_shift, g_in, g_bin, g_back)
    return outs + (dshort.reshape((1, counts[0], spans[0], width)), dlong.reshape((1, counts[1], spans[1], width)))


def solution(mesh):
    split = P("stream", "dp", None, None)
    in_specs = (split, split, P("stream", "dp"), P("stream", "dp")) + (P(),) * 10
    out_specs = (P(),) * 9 + (split, split)
    return jax.shard_map(per_device, mesh=mesh, in_specs=in_specs, out_specs=out_specs, check_vma=False)
```

```python
import functools
import math

import jax
import jax.numpy as jnp
from jax import lax
from jax.experimental import pallas as pl
from jax.experimental.pallas import tpu as pltpu
from jax.sharding import PartitionSpec as P

HEADS = 8
BF = jnp.bfloat16
F32 = jnp.float32
AXES = ("stream", "dp")
logit_scale = 40.0
margin = 0.3
norm_eps = 1e-12
unit_eps = 1e-06
BLOCK = 128
STEP = 256
VMEM = 30 * 1024 * 1024


def mm(a, b):
    return jnp.dot(a, b, preferred_element_type=F32)


def mm_nt(a, b):
    return lax.dot_general(a, b, (((1,), (1,)), ((), ())), preferred_element_type=F32)


def mm_tn(a, b):
    return lax.dot_general(a, b, (((0,), (0,)), ((), ())), preferred_element_type=F32)


def ln_stats(v):
    centre = v - jnp.mean(v, -1, keepdims=True)
    rstd = lax.rsqrt(jnp.mean(centre * centre, -1, keepdims=True) + norm_eps)
    return centre * rstd, rstd


def ln_back(dy, vhat, rstd, gain):
    dhat = dy * gain
    return (dhat - jnp.mean(dhat, -1, keepdims=True) - vhat * jnp.mean(dhat * vhat, -1, keepdims=True)) * rstd


def gelu_pair(v):
    cdf = 0.5 * (1.0 + lax.erf(v * (1.0 / math.sqrt(2.0))))
    pdf = jnp.exp(-0.5 * v * v) * (1.0 / math.sqrt(2.0 * math.pi))
    return v * cdf, cdf + v * pdf


def colsum(v):
    return jnp.sum(v.astype(F32), 0)


def rowsum(v):
    return jnp.sum(v.astype(F32), 0, keepdims=True)


SMEM = pl.BlockSpec(memory_space=pltpu.SMEM)
ANY = pl.BlockSpec(memory_space=pl.ANY)
AS_IS = pl.BlockSpec(memory_space=pl.ANY)


def hbm(a):
    return pltpu.with_memory_space_constraint(a, memory_space=pltpu.HBM)


def hbm_shape(dims, dtype):
    return pltpu.HBM(dims, dtype)


def whole(a):
    return pl.BlockSpec(a.shape, lambda i: (0,) * len(a.shape))


def shape(dims, dtype):
    return jax.ShapeDtypeStruct(dims, dtype)


def layer_of(a, level, rows=None, cols=None, at=lambda i: (0, 0)):
    rows, cols = rows or a.shape[1], cols or a.shape[2]
    return a, pl.BlockSpec((None, rows, cols), lambda i: (level, *at(i)))


def kernel_call(body, name, grid, ins, outs, flops, scratch=(), aliases=None, vmem=VMEM):
    size = sum(a.size * a.dtype.itemsize for a, _ in ins) + sum(
        math.prod(s.shape) * jnp.dtype(s.dtype).itemsize for s, _ in outs
    )
    return pl.pallas_call(
        body,
        grid=grid,
        in_specs=[s for _, s in ins],
        out_specs=[s for _, s in outs],
        out_shape=[s for s, _ in outs],
        scratch_shapes=list(scratch),
        input_output_aliases=aliases or {},
        compiler_params=pltpu.CompilerParams(vmem_limit_bytes=vmem),
        cost_estimate=pl.CostEstimate(flops=int(flops), bytes_accessed=int(size), transcendentals=0),
        name=name,
    )(*[hbm(a) if s is ANY else a for a, s in ins])


def routes(n):
    top, y = n >> 1, 2
    rest = [1 << k for k in range(2, n.bit_length() - 2)]
    for k in range(1, len(rest)):
        rest[k] |= rest[k - 1]
    halved = [(1, 1), (top, y), (y, top)]
    added = list(zip(rest, rest[::-1]))
    return halved, added


def swap(value, n, hop):
    return lax.ppermute(value, AXES, [(i, i ^ (hop[1] if i & 1 else hop[0])) for i in range(n)])


def device_index():
    return lax.axis_index("stream") * lax.axis_size("dp") + lax.axis_index("dp")


def coordinate(index, hop, n):
    value = (index // (1 << (hop.bit_length() - 1))) % 2
    if hop in (1, 2, n >> 1) or 2 * hop >= n >> 1:
        return value
    above = (index // (1 << hop.bit_length())) % 2
    return value + above - 2 * value * above


def my_bits(n):
    index = device_index()
    core = index % 2
    halved, _ = routes(n)
    return [jnp.where(core == 0, coordinate(index, a, n), coordinate(index, b, n)) for a, b in halved]


def split_body(bit_ref, mine_a, got_a, mine_b, got_b, keep_ref, send_ref):
    keep_ref[...] = (mine_a[...].astype(F32) + got_a[...].astype(F32)).astype(BF)
    send_ref[...] = (mine_b[...].astype(F32) + got_b[...].astype(F32)).astype(BF)


def add_and_split(mine, got, bit):
    rows, width = mine.shape[0] // 2, mine.shape[1]
    steps = 2 if rows % 32 == 0 and rows >= 256 else 1
    block = rows // steps
    kept = pl.BlockSpec((block, width), lambda j, bit: (bit[0] * steps + j, 0))
    sent = pl.BlockSpec((block, width), lambda j, bit: ((1 - bit[0]) * steps + j, 0))
    out = pl.BlockSpec((block, width), lambda j, bit: (j, 0))
    ins = [(mine, kept), (got, kept), (mine, sent), (got, sent)]
    outs = [(shape((rows, width), BF), out)] * 2
    return unpack_call(split_body, "add_and_split", bit.reshape(1).astype(jnp.int32), (steps,), ins, outs, {}, 12 * rows * width)


def sum_steps(keep, send, n, bits):
    halved, added = routes(n)
    for k, hop in enumerate(halved[:-1]):
        got = yield send, hop
        keep, send = add_and_split(keep, got, bits[k + 1])
    got = yield send, halved[-1]
    cur = (keep.astype(F32) + got.astype(F32)).astype(BF)
    for hop in added:
        got = yield cur, hop
        cur = (cur.astype(F32) + got.astype(F32)).astype(BF)
    for hop, bit in reversed(list(zip(halved, bits))[1:]):
        got = yield cur, hop
        low = jnp.where(bit == 0, cur, got)
        high = jnp.where(bit == 0, got, cur)
        cur = jnp.concatenate([low, high], 0)
    got = yield cur, halved[0]
    return cur, got


class Lane:
    def __init__(self, steps, n):
        self.n, self.steps, self.result = n, steps, None
        self.ask = next(self.steps)

    def feed(self, got):
        try:
            self.ask = self.steps.send(got)
        except StopIteration as end:
            self.result = end.value


def stage(lanes, work=None, args=()):
    lanes = [lane for lane in lanes if lane.result is None]
    asked, args = lax.optimization_barrier(([lane.ask[0] for lane in lanes], args))
    got = [swap(value, lane.n, lane.ask[1]) for value, lane in zip(asked, lanes)]
    out = work(*args) if work else ()
    got, out = lax.optimization_barrier((got, out))
    for lane, value in zip(lanes, got):
        lane.feed(value)
    return out


def gather_rows(rows, n):
    index = device_index()
    cur = rows[None]
    for flip in [1 << k for k in range(1, n.bit_length() - 1)] + [1]:
        got = swap(cur, n, (flip, flip))
        bit = (index // flip) % 2
        low, high = jnp.where(bit == 0, cur, got), jnp.where(bit == 0, got, cur)
        cur = jnp.stack([low, high], 1 if flip == 1 else 0).reshape((2 * cur.shape[0],) + rows.shape)
    return cur.reshape(n * rows.shape[0], rows.shape[1])


def hop_groups(n):
    hops = [1 << k for k in range(1, n.bit_length() - 1)]
    half = (len(hops) + 1) // 2
    hops = [hops[0], hops[-1]] + hops[1:-1] if len(hops) > 2 else hops
    groups = [hops[k : k + 2] for k in range(0, 2 * half, 2)]
    return [[a, b, a | b] if len(g) == 2 else g for g in groups for a, b in [(g[0], g[-1])]]


def gather_near(rows, n):
    cur = rows
    for group in hop_groups(n):
        cur = jnp.concatenate([cur] + [swap(cur, n, (hop, hop)) for hop in group], 0)
    return cur, swap(cur, n, (1, 1))


def near_offsets(n):
    offsets = [0]
    for group in hop_groups(n):
        offsets = offsets + [hop ^ o for hop in group for o in offsets]
    return offsets


def stream_in(pairs, sems):
    loads = [pltpu.make_async_copy(a, b, sems.at[k]) for k, (a, b) in enumerate(pairs)]
    for load in loads:
        load.start()
    return loads


class Halves:
    def __init__(self, keep, send, block, sems):
        self.keep, self.send, self.block, self.sems = keep, send, block, sems
        self.low_is_kept = lax.axis_index("dp") % 2 == 0
        self.pieces = 0
        self.waits = []

    def put(self, at, value):
        self.block[at : at + value.shape[0]] = value
        half = self.keep.shape[0]
        end = at + value.shape[0]
        for lower, a, b in ((True, at, min(end, half)), (False, max(at, half), end)):
            if a >= b:
                continue
            base = 0 if lower else half
            sem = self.sems.at[self.pieces]
            self.pieces += 1
            copies = [
                pltpu.make_async_copy(self.block.at[a:b], ref.at[a - base : b - base], sem) for ref in (self.keep, self.send)
            ]
            kept = self.low_is_kept if lower else jnp.logical_not(self.low_is_kept)

            @pl.when(kept)
            def _(copy=copies[0]):
                copy.start()

            @pl.when(jnp.logical_not(kept))
            def _(copy=copies[1]):
                copy.start()

            self.waits.append(copies[0])

    def finish(self):
        for copy in self.waits:
            copy.wait()


def starts(sents, spans, rows):
    s = lax.broadcasted_iota(jnp.int32, (sents, rows), 0)
    r = lax.broadcasted_iota(jnp.int32, (sents, rows), 1)
    half = sents // 2
    at = jnp.where(s < half, s * spans[0], half * spans[0] + (s - half) * spans[1])
    return (r == at).astype(BF)


def spread(sents):
    a = lax.broadcasted_iota(jnp.int32, (sents * HEADS, sents), 0) // HEADS
    return (a == lax.broadcasted_iota(jnp.int32, (sents * HEADS, sents), 1)).astype(BF)


def own_head(sents, width):
    a = lax.broadcasted_iota(jnp.int32, (sents * HEADS, width), 0) % HEADS
    return a == lax.broadcasted_iota(jnp.int32, (sents * HEADS, width), 1) // (width // HEADS)


def sum_heads(v, keep, sents):
    return jnp.sum(jnp.where(keep, v, 0.0).reshape(sents, HEADS, v.shape[1]), 1)


def ask(y, spans, lens, wqkv_ref, wout_ref, bq, bv, bo, sents):
    rows, width = y.shape
    keep = own_head(sents, width)
    cls = mm(starts(sents, spans, rows), y).astype(BF)
    q = (mm(cls, wqkv_ref[:, :width]) + bq).astype(BF)
    wide = jnp.where(keep, mm(spread(sents), q), 0.0).astype(BF)
    key = mm_nt(wide, wqkv_ref[:, width : 2 * width]).astype(BF)
    half = sents // 2
    sent = lax.broadcasted_iota(jnp.int32, (sents * HEADS, 1), 0) // HEADS
    begin = jnp.where(sent < half, sent * spans[0], half * spans[0] + (sent - half) * spans[1])
    place = lax.broadcasted_iota(jnp.int32, (sents * HEADS, rows), 1) - begin
    seen = (place >= 0) & (place < lens)
    logit = jnp.where(seen, mm_nt(key, y) * (1.0 / math.sqrt(width // HEADS)), -jnp.inf)
    power = jnp.exp(logit - jnp.max(logit, 1, keepdims=True))
    prob = (power * (1.0 / jnp.sum(power, 1, keepdims=True))).astype(BF)
    mixed = mm(prob, y).astype(BF)
    ctx = (sum_heads(mm(mixed, wqkv_ref[:, 2 * width :]), keep, sents) + bv).astype(BF)
    attended = (cls.astype(F32) + mm(ctx, wout_ref[...]) + bo).astype(BF)
    return attended, ctx, wide, key, prob, mixed


def halves(v, first):
    zero = jnp.zeros_like(v)
    return jnp.concatenate([jnp.where(first, v, zero), jnp.where(first, zero, v)], 0)


def join_halves(v, first):
    return jnp.where(first, v[: v.shape[0] // 2], v[v.shape[0] // 2 :])


def first_head(width):
    return lax.broadcasted_iota(jnp.int32, (1, 2 * width // HEADS), 1) < width // HEADS


def key_bias(lens_ref, block, span_short, count_short):
    key = lax.broadcasted_iota(jnp.int32, (BLOCK, 1), 0)
    query = lax.broadcasted_iota(jnp.int32, (1, BLOCK), 1)
    per = BLOCK // span_short
    blocks_short = count_short // per
    is_short = block < blocks_short
    at = jnp.where(is_short, block * per, count_short + block - blocks_short)
    limit = jnp.zeros((BLOCK, 1), jnp.int32)
    for s in range(per):
        inside = key // span_short == s
        limit = jnp.where(inside, jnp.where(is_short, lens_ref[at + jnp.where(is_short, s, 0)] + s * span_short, 0), limit)
    limit = jnp.where(is_short, limit, lens_ref[at])
    same = (key // span_short == query // span_short) | jnp.logical_not(is_short)
    return jnp.where((key < limit) & same, 0.0, -jnp.inf).astype(F32)


def vectors(level, width, bqv_ref, bresid_ref, gain_ref, shift_ref):
    row = slice(level, level + 1)
    low, high = slice(0, width), slice(width, 2 * width)
    return [ref[row, part] for ref in (bqv_ref, bresid_ref, gain_ref, shift_ref) for part in (low, high)]


def forward_body(
    spans, count, lens_ref, short_ref, long_ref, wqkv_ref, wout_ref, win_ref, wback_ref, bin_ref, bqv_ref, bresid_ref, gain_ref, shift_ref,
    wide_lens_ref, wqkv_hbm, wout_hbm,
    y_ref, qkv_ref, prob_ref, ctx_ref, hat1_ref, rstd1_ref, act_ref, slope_ref, hat2_ref, rstd2_ref,
    sent_ref, ctx1_ref, wide_ref, key_ref, prob1_ref, mixed_ref, y_s, wqkv1_ref, wout1_ref, got,
):
    step = pl.program_id(0)
    loads = [pltpu.make_async_copy(a.at[1], b, got.at[k]) for k, (a, b) in enumerate(((wqkv_hbm, wqkv1_ref), (wout_hbm, wout1_ref)))]

    @pl.when(step == 0)
    def _():
        for load in loads:
            load.start()

    x = jnp.where(step == 0, short_ref[...], long_ref[...])
    rows, width = x.shape
    bq, bv, bo, bb, g1, g2, c1, c2 = vectors(0, width, bqv_ref, bresid_ref, gain_ref, shift_ref)
    pair = 2 * width // HEADS
    first = first_head(width)
    scale = 1.0 / math.sqrt(width // HEADS)
    bias = jnp.concatenate([bq, jnp.zeros_like(bq), bv], 1)
    qkv = (mm(x, wqkv_ref[...]) + bias).astype(BF)
    qkv_ref[...] = qkv
    blocks = []
    for b in range(rows // BLOCK):
        r = slice(b * BLOCK, (b + 1) * BLOCK)
        hide = key_bias(lens_ref, step * (rows // BLOCK) + b, spans[0], count)
        hide = jnp.concatenate([hide, hide], 1)
        cols = []
        for p in range(HEADS // 2):
            q, k, v = (qkv[r, m * width + p * pair : m * width + (p + 1) * pair] for m in range(3))
            logit = mm_nt(k, halves(q, first)) * scale + hide
            power = jnp.exp(logit - jnp.max(logit, 0, keepdims=True))
            prob = (power * (1.0 / jnp.sum(power, 0, keepdims=True))).astype(BF)
            prob_ref[b, p] = prob
            cols.append(join_halves(mm_tn(prob, v), first))
        blocks.append(jnp.concatenate(cols, 1).astype(BF))
    ctx = jnp.concatenate(blocks, 0)
    ctx_ref[...] = ctx
    hat1, rstd1 = ln_stats(x.astype(F32) + mm(ctx, wout_ref[...]) + bo)
    normed = hat1 * g1 + c1
    low = normed.astype(BF)
    hat1_ref[...] = hat1.astype(BF)
    rstd1_ref[...] = jnp.broadcast_to(rstd1, rstd1_ref.shape)
    act, slope = gelu_pair(mm(low, win_ref[...]) + bin_ref[0:1])
    act = act.astype(BF)
    act_ref[...] = act
    slope_ref[...] = slope.astype(BF)
    hat2, rstd2 = ln_stats(normed + mm(act, wback_ref[...]) + bb)
    hat2_ref[...] = hat2.astype(BF)
    rstd2_ref[...] = jnp.broadcast_to(rstd2, rstd2_ref.shape)
    y = (hat2 * g2 + c2).astype(BF)
    y_ref[...] = y
    y_s[pl.ds(pl.multiple_of(step * rows, rows), rows)] = y

    @pl.when(step == pl.num_programs(0) - 1)
    def _():
        for load in loads:
            load.wait()
        bq, bv, bo = vectors(1, width, bqv_ref, bresid_ref, gain_ref, shift_ref)[:3]
        outs = ask(y_s[...], spans, wide_lens_ref[...], wqkv1_ref, wout1_ref, bq, bv, bo, sent_ref.shape[0])
        for ref, value in zip((sent_ref, ctx1_ref, wide_ref, key_ref, prob1_ref, mixed_ref), outs):
            ref[...] = value


def by_rows(cols):
    return pl.BlockSpec((STEP, cols), lambda i: (i, 0))


def from_buckets(short, long):
    width = short.shape[1]
    return [
        (short, pl.BlockSpec((STEP, width), lambda i: (0, 0))),
        (long, pl.BlockSpec((STEP, width), lambda i: (jnp.maximum(i - 1, 0), 0))),
    ]


def small_ins(w):
    return [(w[k], whole(w[k])) for k in ("b_qv", "b_resid", "gain", "shift")]


def forward(short, long, lens, wide_lens, w, spans, count, sents):
    rows, width = short.shape[0] + long.shape[0], short.shape[1]
    ff = w["in"].shape[2]
    per = STEP // BLOCK
    prob = pl.BlockSpec((per, HEADS // 2, BLOCK, 2 * BLOCK), lambda i: (i, 0, 0, 0))
    ins = [(lens, SMEM)] + from_buckets(short, long)
    ins += [layer_of(w[name], 0) for name in ("qkv", "out", "in", "back")] + [(w["b_in"], whole(w["b_in"]))] + small_ins(w)
    cols = [(width, BF), (3 * width, BF), None, (width, BF), (width, BF), (128, F32), (ff, BF), (ff, BF), (width, BF), (128, F32)]
    outs = [(hbm_shape((rows, c[0]), c[1]), by_rows(c[0])) if c else (hbm_shape((rows // BLOCK, HEADS // 2, BLOCK, 2 * BLOCK), BF), prob) for c in cols]
    ins += [(wide_lens, whole(wide_lens)), (w["qkv"], ANY), (w["out"], ANY)]
    wide = sents * HEADS
    outs += [(s, whole(s)) for s in [shape((sents, width), BF)] + [hbm_shape(d, BF) for d in ((sents, width), (wide, width), (wide, width), (wide, rows), (wide, width))]]
    scratch = [pltpu.VMEM(d, BF) for d in ((rows, width), (width, 3 * width), (width, width))] + [pltpu.SemaphoreType.DMA((2,))]
    body = functools.partial(forward_body, spans, count)
    return kernel_call(body, "layer0_forward", (rows // STEP,), ins, outs, 2 * rows * width * (4 * width + 2 * ff), scratch, vmem=VMEM + VMEM // 4)


def top_forward(attended, win_ref, bin_ref, g1, c1):
    hat1, rstd1 = ln_stats(attended.astype(F32))
    normed = hat1 * g1 + c1
    low = normed.astype(BF)
    return hat1, rstd1, normed, low, mm(low, win_ref[...]) + bin_ref[1:2]


def gelu(v):
    return v * (0.5 * (1.0 + lax.erf(v * (1.0 / math.sqrt(2.0)))))


def top_part(index_ref, every_ref, pair_ref, dy_ref, hat2_s, rstd2_s, low_vectors, bin_ref, win, wback, wout_ref, sents):
    pairs = pair_ref.shape[1]
    _, _, _, bb, g1, g2, c1, c2 = low_vectors
    hat1, _ = ln_stats(every_ref[...].astype(F32))
    normed = hat1 * g1 + c1
    win_ref = win()
    act = gelu(mm(normed.astype(BF), win_ref[...]) + bin_ref[1:2]).astype(BF)
    wback_ref = wback()
    hat2, rstd2 = ln_stats(normed + mm(act, wback_ref[...]) + bb)
    hat2_s[...] = hat2
    rstd2_s[...] = jnp.broadcast_to(rstd2, rstd2_s.shape)
    pooled = hat2 * g2 + c2
    radius = lax.rsqrt(jnp.sum(pooled * pooled, -1, keepdims=True) + unit_eps)
    unit = pooled * radius
    src, tgt = unit[:pairs].astype(BF), unit[pairs:].astype(BF)
    positive = (pair_ref[...] == lax.broadcasted_iota(jnp.int32, (pairs, pairs), 0)).astype(F32)
    logits = logit_scale * (mm_nt(tgt, src) - margin * positive)

    def soft(axis):
        powers = jnp.exp(logits - jnp.max(logits, axis, keepdims=True))
        return powers * (1.0 / jnp.sum(powers, axis, keepdims=True))

    dscore = (0.5 * logit_scale * (soft(1) + soft(0) - 2.0 * positive)).astype(BF)
    dunit = jnp.concatenate([mm_tn(dscore, tgt), mm(dscore, src)], 0)
    dy_ref[...] = radius * (dunit - unit * jnp.sum(dunit * unit, -1, keepdims=True))
    mine = pl.ds(pl.multiple_of(index_ref[0] * sents, sents), sents)
    own_hat1, own_rstd1, _, _, own_hid = top_forward(every_ref[mine], win_ref, bin_ref, g1, c1)
    dmixed = ln_back(dy_ref[mine], hat2_s[mine], rstd2_s[mine, 0:1], g2)
    dhidden = (mm_nt(dmixed.astype(BF), wback_ref[...]) * gelu_pair(own_hid)[1]).astype(BF)
    dnormed = dmixed + mm_nt(dhidden, win_ref[...])
    datt = ln_back(dnormed, own_hat1, own_rstd1, g1)
    return datt, mm_nt(datt.astype(BF), wout_ref[...]).astype(BF)


def top_grads_body(every_ref, dy_ref, wout_ref, win_ref, wback_ref, bin_ref, bqv_ref, bresid_ref, gain_ref, shift_ref,
                   gin_ref, gback_ref, sums_ref, sumin_ref):
    width = dy_ref.shape[1]
    _, _, _, bb, g1, g2, c1, c2 = vectors(1, width, bqv_ref, bresid_ref, gain_ref, shift_ref)
    hat1, rstd1, normed, low, hid = top_forward(every_ref[...], win_ref, bin_ref, g1, c1)
    act, slope = gelu_pair(hid)
    act = act.astype(BF)
    hat2, rstd2 = ln_stats(normed + mm(act, wback_ref[...]) + bb)
    dy = dy_ref[...]
    dmixed = ln_back(dy, hat2, rstd2, g2)
    dmixed_low = dmixed.astype(BF)
    gback_ref[...] = mm_tn(act, dmixed_low)
    dhidden = (mm_nt(dmixed_low, wback_ref[...]) * slope).astype(BF)
    gin_ref[...] = mm_tn(low, dhidden)
    dnormed = dmixed + mm_nt(dhidden, win_ref[...])
    datt = ln_back(dnormed, hat1, rstd1, g1)
    sumin_ref[...] = rowsum(dhidden)
    parts = (datt, dmixed, dnormed * hat1, dy * hat2, dnormed, dy, mm_nt(datt.astype(BF), wout_ref[...]).astype(BF))
    for k, part in enumerate(parts):
        sums_ref[k : k + 1] = rowsum(part)
    sums_ref[7:8] = jnp.zeros((1, width), F32)


def top_grads(every, dy, w):
    width = dy.shape[1]
    ff = w["in"].shape[2]
    rows = every.shape[0]
    ins = [(every, whole(every)), (dy, whole(dy))] + [layer_of(w[k], 1) for k in ("out", "in", "back")]
    ins += [(w["b_in"], whole(w["b_in"]))] + small_ins(w)

    def upper(a, b):
        return hbm_shape((2, a, b), F32), pl.BlockSpec((None, a, b), lambda i: (1, 0, 0))

    sums, sumin = shape((8, width), F32), shape((1, ff), F32)
    outs = [upper(width, ff), upper(ff, width), (sums, whole(sums)), (sumin, whole(sumin))]
    return kernel_call(top_grads_body, "top_grads", (1,), ins, outs, 6 * rows * width * (width + 2 * ff))


def turn_body(spans, sents, with_top, *refs):
    refs = list(refs)

    def take(count):
        out, refs[:count] = refs[:count], []
        return out

    wide_ref, key_ref, prob_ref, mixed_ref, ctx_ref, gain_ref = take(6)
    wqkv_hbm, y_hbm, hat2_hbm, rstd2_hbm, act_hbm = take(5)
    if with_top:
        index_ref, near_ref, other_ref, pair_ref, wout_ref, bin_ref, bqv_ref, bresid_ref, shift_ref, win_hbm, wback_hbm = take(11)
    else:
        datt_ref, dctx_ref = take(2)
    keep_hbm, send_hbm, low_ref, sums_ref = take(4)
    if with_top:
        every_ref, dy_ref = take(2)
    wqkv_ref, y_ref, hat2_ref, rstd2_ref, act_ref, block, got, sent = take(8)
    loads = [(wqkv_hbm.at[1], wqkv_ref), (y_hbm, y_ref), (hat2_hbm, hat2_ref), (rstd2_hbm, rstd2_ref), (act_hbm, act_ref)]
    if with_top:
        win_ref, wback_ref, top_hat2, top_rstd2, arrivals = take(5)
        offsets = near_offsets(2 * near_ref.shape[0] // sents)
        pieces = []
        for p, offset in enumerate(offsets):
            for core, ref in enumerate((near_ref, other_ref)):
                device = index_ref[0] ^ (offset + core)
                to = every_ref.at[pl.ds(pl.multiple_of(device * sents, sents), sents)]
                pieces.append(pltpu.make_async_copy(ref.at[p * sents : (p + 1) * sents], to, arrivals.at[2 * p + core]))
        for piece in pieces:
            piece.start()
        loads = [(win_hbm.at[1], win_ref), (wback_hbm.at[1], wback_ref)] + loads
    loads = [pltpu.make_async_copy(a, b, got.at[k]) for k, (a, b) in enumerate(loads)]
    for load in loads:
        load.start()
    rows, width = y_ref.shape
    if with_top:

        def arrived(load, ref):
            def wait():
                load.wait()
                return ref

            return wait

        values = vectors(1, width, bqv_ref, bresid_ref, gain_ref, shift_ref)
        for piece in pieces:
            piece.wait()
        win, wback = arrived(loads[0], win_ref), arrived(loads[1], wback_ref)
        datt, dctx = top_part(index_ref, every_ref, pair_ref, dy_ref, top_hat2, top_rstd2, values, bin_ref, win, wback, wout_ref, sents)
        loads = loads[2:]
    else:
        datt, dctx = datt_ref[...], dctx_ref[...]
    keep = own_head(sents, width)
    first = starts(sents, spans, rows)
    prob_low = prob_ref[...]
    d_wide = jnp.where(keep, mm(spread(sents), dctx), 0.0).astype(BF)
    loads[0].wait()
    d_value = mm_nt(d_wide, wqkv_ref[:, 2 * width :]).astype(BF)
    loads[1].wait()
    y = y_ref[...]
    dprob = mm_nt(d_value, y)
    prob = prob_low.astype(F32)
    dlogit = prob * (dprob - jnp.sum(prob * dprob, 1, keepdims=True))
    dscore = (dlogit * (1.0 / math.sqrt(width // HEADS))).astype(BF)
    pulled = mm(dscore, y).astype(BF)
    dq = sum_heads(mm(pulled, wqkv_ref[:, width : 2 * width]), keep, sents).astype(BF)
    dcls = mm_nt(dq, wqkv_ref[:, :width]) + datt
    high = dcls.astype(BF)
    left = jnp.concatenate([dscore, prob_low, first, first], 0)
    right = jnp.concatenate([key_ref[...], d_value, high, (dcls - high.astype(F32)).astype(BF)], 0)
    dy = mm_tn(left, right)
    loads[2].wait()
    loads[3].wait()
    hat2 = hat2_ref[...].astype(F32)
    dmixed = ln_back(dy, hat2, rstd2_ref[:, 0:1], gain_ref[0:1, width:])
    low_ref[...] = dmixed.astype(BF)
    sums_ref[0:1] = rowsum(dmixed)
    sums_ref[1:2] = rowsum(dy * hat2)
    sums_ref[2:3] = rowsum(dy)
    sums_ref[3:4] = rowsum(dq)
    sums_ref[4:8] = jnp.zeros((4, width), F32)
    place = Halves(keep_hbm, send_hbm, block, sent)
    ff = act_ref.shape[1]
    tiles = ff // width
    cls = mm(first, y).astype(BF)
    tail = ((cls, dq), (pulled, wide_ref[...]), (mixed_ref[...], d_wide), (ctx_ref[...], datt.astype(BF)))
    for k, (a, b) in enumerate(tail):
        place.put((tiles + k) * width, mm_tn(a, b).astype(BF))
    loads[4].wait()
    for k in range(tiles):
        place.put(k * width, mm_tn(act_ref[:, k * width : (k + 1) * width], low_ref[...]).astype(BF))
    place.finish()


def turn(top_args, y, kept, w, hat2, rstd2, act, spans, sents):
    rows, width = y.shape
    ff = act.shape[1]
    ctx, wide, key, prob, mixed = kept
    with_top = len(top_args) == 4
    ins = [(a, whole(a)) for a in (wide, key, prob, mixed, ctx, w["gain"])]
    ins += [(a, ANY) for a in (w["qkv"], y, hat2, rstd2, act)]
    blocks = ff // width + 4
    outs = [(shape((blocks * width // 2, width), BF), ANY)] * 2
    outs += [(s, whole(s)) for s in (hbm_shape((rows, width), BF), shape((8, width), F32))]
    scratch = [pltpu.VMEM(d, t) for d, t in (((width, 3 * width), BF), ((rows, width), BF), ((rows, width), BF), ((rows, 128), F32), ((rows, ff), BF), ((blocks * width, width), BF))]
    scratch += [pltpu.SemaphoreType.DMA((7,)), pltpu.SemaphoreType.DMA((blocks,))]
    flops = 2 * rows * width * (ff + 512)
    if with_top:
        index, near, other, pair = top_args
        every = shape((2 * near.shape[0], width), BF)
        ins += [(index, SMEM), (near, AS_IS), (other, AS_IS), (pair, whole(pair)), layer_of(w["out"], 1)]
        ins += [(w[k], whole(w[k])) for k in ("b_in", "b_qv", "b_resid", "shift")] + [(w["in"], ANY), (w["back"], ANY)]
        outs += [(hbm_shape(every.shape, t), whole(every)) for t in (BF, F32)]
        scratch += [pltpu.VMEM((width, ff), BF), pltpu.VMEM((ff, width), BF), pltpu.VMEM(every.shape, F32), pltpu.VMEM((every.shape[0], 128), F32)]
        scratch += [pltpu.SemaphoreType.DMA((every.shape[0] // sents,))]
        flops += 4 * every.shape[0] * width * ff
    else:
        ins += [(a, whole(a)) for a in top_args]
    return kernel_call(functools.partial(turn_body, spans, sents, with_top), "turn", (1,), ins, outs, flops, scratch, vmem=VMEM + VMEM // 4)


VECTOR_ROWS = 128


def ff_back_body(gain_ref, shift_ref, low_hbm, hat1_hbm, rstd1_hbm, wback_hbm, slope_hbm, win_hbm, wout_hbm, ctx_hbm,
                 keep_hbm, send_hbm, datt_ref, dctx_ref, sums_ref, sumin_ref,
                 low_ref, hat1_ref, rstd1_ref, wback_ref, slope_ref, win_ref, wout_ref, ctx_ref, nlow_ref, dhidden_ref, block, got, sent):
    rows, width = low_ref.shape
    ff = slope_ref.shape[1]
    tiles = ff // width
    loads = [(hat1_hbm, hat1_ref), (low_hbm, low_ref)]
    for t in range(tiles):
        part = slice(t * width, (t + 1) * width)
        loads += [(wback_hbm.at[0, part], wback_ref.at[part]), (slope_hbm.at[:, part], slope_ref.at[:, part])]
    loads += [(win_hbm.at[0], win_ref), (rstd1_hbm, rstd1_ref), (wout_hbm.at[0], wout_ref), (ctx_hbm, ctx_ref)]
    loads = stream_in(loads, got)
    place = Halves(keep_hbm, send_hbm, block, sent)
    gain, shift = gain_ref[0:1, :width], shift_ref[0:1, :width]
    loads.pop(0).wait()
    nlow_ref[...] = (hat1_ref[...].astype(F32) * gain + shift).astype(BF)
    loads[0].wait()
    for t in range(tiles):
        part = slice(t * width, (t + 1) * width)
        loads[1 + 2 * t].wait()
        loads[2 + 2 * t].wait()
        dhidden = (mm_nt(low_ref[...], wback_ref[part]) * slope_ref[:, part].astype(F32)).astype(BF)
        dhidden_ref[:, part] = dhidden
        sumin_ref[:, part] = rowsum(dhidden)
        place.put(t * width, mm_tn(nlow_ref[...], dhidden).astype(BF))
    for load in loads[1 + 2 * tiles :]:
        load.wait()
    sums_ref[...] = jnp.zeros_like(sums_ref)
    for r in range(0, rows, STEP):
        r = slice(r, r + STEP)
        dnormed = low_ref[r].astype(F32) + mm_nt(dhidden_ref[r], win_ref[...])
        hat1 = hat1_ref[r].astype(F32)
        datt = ln_back(dnormed, hat1, rstd1_ref[r, 0:1], gain)
        low = datt.astype(BF)
        datt_ref[r] = low
        dctx_ref[r] = mm_nt(low, wout_ref[...]).astype(BF)
        sums_ref[0:1] += rowsum(datt)
        sums_ref[1:2] += rowsum(dnormed * hat1)
        sums_ref[2:3] += rowsum(dnormed)
    place.put(ff, mm_tn(ctx_ref[...], datt_ref[...]).astype(BF))
    place.finish()


def ff_back(low, hat1, rstd1, slope, ctx, w):
    rows, width = low.shape
    ff = slope.shape[1]
    ins = [(w["gain"], whole(w["gain"])), (w["shift"], whole(w["shift"]))]
    ins += [(a, ANY) for a in (low, hat1, rstd1, w["back"], slope, w["in"], w["out"], ctx)]
    half = (ff + width) // 2
    outs = [(shape((half, width), BF), ANY)] * 2
    outs += [(s, whole(s)) for s in (shape((rows, width), BF), shape((rows, width), BF), shape((8, width), F32), shape((1, ff), F32))]
    scratch = [((rows, width), BF), ((rows, width), BF), ((rows, 128), F32), ((ff, width), BF), ((rows, ff), BF), ((width, ff), BF), ((width, width), BF), ((rows, width), BF)]
    scratch += [((rows, width), BF), ((rows, ff), BF), ((ff + width, width), BF)]
    scratch = [pltpu.VMEM(d, t) for d, t in scratch]
    scratch += [pltpu.SemaphoreType.DMA((6 + 2 * (ff // width),)), pltpu.SemaphoreType.DMA((8,))]
    return kernel_call(ff_back_body, "layer0_ff_back", (1,), ins, outs, 2 * rows * width * (3 * ff + 2 * width), scratch)


def attention_back_body(qkv_ref, prob_ref, dctx_ref, short_ref, long_ref, sums1_ref, sums2_ref, sumin_ref, dqkv_ref, keep_hbm, send_hbm, acc, sums, block, sent):
    step = pl.program_id(0)
    x = jnp.where(step == 0, short_ref[...], long_ref[...])
    rows, width = x.shape
    pair = 2 * width // HEADS
    first = first_head(width)
    scale = 1.0 / math.sqrt(width // HEADS)

    @pl.when(step == 0)
    def _():
        acc[...] = jnp.zeros_like(acc)
        sums[...] = jnp.zeros_like(sums)

    pairs = range(HEADS // 2)
    c = [[slice(m * width + p * pair, m * width + (p + 1) * pair) for m in range(3)] for p in pairs]
    for b in range(rows // BLOCK):
        r = slice(b * BLOCK, (b + 1) * BLOCK)
        dd = [halves(dctx_ref[r, c[p][0]], first) for p in pairs]
        dprob = [mm_nt(qkv_ref[r, c[p][2]], dd[p]) for p in pairs]
        dscore = []
        for p in pairs:
            prob = prob_ref[b, p].astype(F32)
            dscore.append((prob * (dprob[p] - jnp.sum(prob * dprob[p], 0, keepdims=True)) * scale).astype(BF))
        dv = [mm(prob_ref[b, p], dd[p]).astype(BF) for p in pairs]
        dk = [mm(dscore[p], halves(qkv_ref[r, c[p][0]], first)).astype(BF) for p in pairs]
        dq = [join_halves(mm_tn(dscore[p], qkv_ref[r, c[p][1]]), first).astype(BF) for p in pairs]
        dqkv_ref[r] = jnp.concatenate(dq + dk + dv, 1)
    dqkv = dqkv_ref[...]
    acc[...] += mm_tn(x, dqkv)
    sums[0:1] += rowsum(dqkv)

    @pl.when(step == pl.num_programs(0) - 1)
    def _():
        place = Halves(keep_hbm, send_hbm, block, sent)
        for m in range(3):
            place.put(m * width, acc[:, m * width : (m + 1) * width].astype(BF))
        rows_of = [sums[0:1, :width], sums[0:1, 2 * width :]]
        for k in range(3):
            rows_of += [sums1_ref[k : k + 1], sums2_ref[k : k + 1]]
        rows_of += [sumin_ref[:, k * width : (k + 1) * width] for k in range(sumin_ref.shape[1] // width)]
        rows_of += [sums2_ref[3:4], jnp.zeros((3, width), F32)]
        rows_of += [jnp.zeros((VECTOR_ROWS - 16, width), F32)]
        place.put(3 * width, jnp.concatenate(rows_of, 0).astype(BF))
        place.finish()


def attention_back(qkv, prob, dctx, sums1, sums2, sumin, short, long):
    rows, width = dctx.shape
    per = STEP // BLOCK
    ins = [(qkv, by_rows(3 * width)), (prob, pl.BlockSpec((per,) + prob.shape[1:], lambda i: (i, 0, 0, 0))), (dctx, by_rows(width))]
    ins += from_buckets(short, long) + [(a, whole(a)) for a in (sums1, sums2, sumin)]
    total = 3 * width + VECTOR_ROWS
    outs = [(hbm_shape((rows, 3 * width), BF), by_rows(3 * width))] + [(shape((total // 2, width), BF), ANY)] * 2
    scratch = [pltpu.VMEM((width, 3 * width), F32), pltpu.VMEM((8, 3 * width), F32), pltpu.VMEM((total, width), BF), pltpu.SemaphoreType.DMA((8,))]
    flops = 2 * rows * width * (3 * width + 10 * BLOCK)
    return kernel_call(attention_back_body, "layer0_attention_back", (rows // STEP,), ins, outs, flops, scratch)


def input_back_body(dqkv_ref, datt_ref, wqkv_ref, short_ref, long_ref):
    dx = datt_ref[...].astype(F32) + mm_nt(dqkv_ref[...], wqkv_ref[...])

    @pl.when(pl.program_id(0) == 0)
    def _():
        short_ref[...] = dx

    @pl.when(pl.program_id(0) > 0)
    def _():
        long_ref[...] = dx


def input_back(dqkv, datt, w, cut):
    rows, width = datt.shape
    ins = [(dqkv, by_rows(3 * width)), (datt, by_rows(width)), layer_of(w["qkv"], 0)]
    outs = [
        (shape((cut, width), F32), pl.BlockSpec((STEP, width), lambda i: (0, 0))),
        (shape((rows - cut, width), F32), pl.BlockSpec((STEP, width), lambda i: (jnp.maximum(i - 1, 0), 0))),
    ]
    return kernel_call(input_back_body, "layer0_input_back", (rows // STEP,), ins, outs, 2 * rows * width * 3 * width)


def unpack_call(body, name, bit, grid, ins, outs, aliases, size):
    return pl.pallas_call(
        body,
        grid_spec=pltpu.PrefetchScalarGridSpec(
            num_scalar_prefetch=1,
            grid=grid,
            in_specs=[s for _, s in ins],
            out_specs=[s for _, s in outs],
        ),
        out_shape=[s for s, _ in outs],
        input_output_aliases=aliases,
        compiler_params=pltpu.CompilerParams(vmem_limit_bytes=VMEM),
        cost_estimate=pl.CostEstimate(flops=0, bytes_accessed=size, transcendentals=0),
        name=name,
    )(bit, *[hbm(a) if s is ANY else a for a, s in ins])


def in_order(bit_ref, mine_ref, theirs_ref):
    mine, theirs = mine_ref[...].astype(F32), theirs_ref[...].astype(F32)
    low = bit_ref[0] == 0
    return jnp.where(low, mine, theirs), jnp.where(low, theirs, mine)


def unpack_first(bit, pair, back):
    _, ff, width = back.shape
    steps = ff // width
    block = pl.BlockSpec((width, width), lambda j, bit: (j, 0))

    def body(bit_ref, mine_ref, theirs_ref, _, qkv_ref, out_ref, back_ref):
        low, high = in_order(bit_ref, mine_ref, theirs_ref)
        back_ref[...] = low
        step = pl.program_id(0)

        @pl.when(step < steps - 1)
        def _():
            qkv_ref[...] = high

        @pl.when(step == steps - 1)
        def _():
            out_ref[...] = high

    outs = [
        (shape((2, width, 3 * width), F32), pl.BlockSpec((None, width, width), lambda j, bit: (1, 0, jnp.minimum(j, 2)))),
        (shape((2, width, width), F32), pl.BlockSpec((None, width, width), lambda j, bit: (1, 0, 0))),
        (shape(back.shape, F32), pl.BlockSpec((None, width, width), lambda j, bit: (0, j, 0))),
    ]
    ins = [(pair[0], block), (pair[1], block), (back, ANY)]
    return unpack_call(body, "unpack_first", bit, (steps,), ins, outs, {3: 2}, 12 * steps * width * width)


def unpack_second(bit, pair, gin, gout):
    _, width, ff = gin.shape
    rows = width // 2
    half = pair[0].shape[0] // rows
    count = 2 * ff // width
    block = [pl.BlockSpec((rows, width), lambda j, bit, low=low: (jnp.where((bit[0] == 0) == low, jnp.minimum(j, half - 1), jnp.maximum(j - half, 0)), 0)) for low in (True, False)]

    def body(bit_ref, mine_ref, theirs_ref, _, __, in_ref, out_ref):
        step = pl.program_id(0)
        mine = (step < half) == (bit_ref[0] == 0)
        value = jnp.where(mine, mine_ref[...], theirs_ref[...]).astype(F32)

        @pl.when(step < count)
        def _():
            in_ref[...] = value

        @pl.when(step >= count)
        def _():
            out_ref[...] = value

    def at_in(j, bit):
        j = jnp.minimum(j, count - 1)
        return 0, j % 2, j // 2

    outs = [
        (shape(gin.shape, F32), pl.BlockSpec((None, rows, width), at_in)),
        (shape(gout.shape, F32), pl.BlockSpec((None, rows, width), lambda j, bit: (0, jnp.maximum(j - count, 0), 0))),
    ]
    ins = [(pair[0], block[0]), (pair[1], block[1]), (gin, ANY), (gout, ANY)]
    return unpack_call(body, "unpack_second", bit, (2 * half,), ins, outs, {3: 0, 4: 1}, 12 * half * rows * width)


def unpack_third(bit, pair, qkv, sums, sumin):
    _, width, _ = qkv.shape
    ff = sumin.shape[1]
    total = 3 * width + VECTOR_ROWS

    def fixed(a):
        return pl.BlockSpec(a.shape, lambda j, bit: (0,) * len(a.shape))

    def body(bit_ref, mine_ref, theirs_ref, _, sums_ref, sumin_ref, qkv_ref, bqv_ref, bresid_ref, gain_ref, shift_ref, bin_ref):
        low, high = in_order(bit_ref, mine_ref, theirs_ref)
        value = jnp.concatenate([low, high], 0)
        for m in range(3):
            qkv_ref[:, m * width : (m + 1) * width] = value[m * width : (m + 1) * width]
        value = value[3 * width :]
        for ref, lower, upper in (
            (bqv_ref, (value[0:1], value[1:2]), (value[12:13], sums_ref[6:7])),
            (bresid_ref, (value[2:3], value[3:4]), (sums_ref[0:1], sums_ref[1:2])),
            (gain_ref, (value[4:5], value[5:6]), (sums_ref[2:3], sums_ref[3:4])),
            (shift_ref, (value[6:7], value[7:8]), (sums_ref[4:5], sums_ref[5:6])),
        ):
            for level, both in enumerate((lower, upper)):
                for k in range(2):
                    ref[level : level + 1, k * width : (k + 1) * width] = both[k]
        for k in range(ff // width):
            bin_ref[0:1, k * width : (k + 1) * width] = value[8 + k : 9 + k]
        bin_ref[1:2, :] = sumin_ref[...]

    outs = [(shape(qkv.shape, F32), pl.BlockSpec((None, width, 3 * width), lambda j, bit: (0, 0, 0)))]
    outs += [(s, fixed(s)) for s in [shape((2, 2 * width), F32)] * 4 + [shape((2, ff), F32)]]
    ins = [(pair[0], fixed(pair[0])), (pair[1], fixed(pair[1])), (qkv, ANY), (sums, fixed(sums)), (sumin, fixed(sumin))]
    return unpack_call(body, "unpack_third", bit, (1,), ins, outs, {3: 0}, 6 * total * width)


def top_rows(attended, pair_index, weights):
    w_qkv, b_qv, w_out, b_resid, gain, shift, w_in, b_in, w_back = weights
    rows, width = attended.shape
    pairs = rows // 2
    hat1, rstd1 = ln_stats(attended.astype(F32))
    normed = hat1 * gain[:width] + shift[:width]
    normed_low = normed.astype(BF)
    activ, slope = gelu_pair(mm(normed_low, w_in) + b_in)
    activ = activ.astype(BF)
    hat2, rstd2 = ln_stats(normed + mm(activ, w_back) + b_resid[width:])
    pooled = hat2 * gain[width:] + shift[width:]
    radius = lax.rsqrt(jnp.sum(pooled * pooled, -1, keepdims=True) + unit_eps)
    unit = pooled * radius
    unit_low = unit.astype(BF)
    src, tgt = unit_low[:pairs], unit_low[pairs:]
    positive = (pair_index[:, None] == jnp.arange(pairs)[None, :]).astype(F32)
    logits = logit_scale * (mm_nt(src, tgt) - margin * positive)

    def soft(axis):
        powers = jnp.exp(logits - jnp.max(logits, axis, keepdims=True))
        return powers / jnp.sum(powers, axis, keepdims=True)

    dscore = (0.5 * logit_scale * (soft(1) + soft(0) - 2.0 * positive)).astype(BF)
    dunit = jnp.concatenate([mm(dscore, tgt), mm_tn(dscore, src)], 0)
    dy = radius * (dunit - unit * jnp.sum(dunit * unit, -1, keepdims=True))
    dg2, dc2 = colsum(dy * hat2), colsum(dy)
    dmixed = ln_back(dy, hat2, rstd2, gain[width:])
    dmixed_low = dmixed.astype(BF)
    dhidden = (mm_nt(dmixed_low, w_back) * slope).astype(BF)
    dnormed = dmixed + mm_nt(dhidden, w_in)
    dg1, dc1 = colsum(dnormed * hat1), colsum(dnormed)
    datt = ln_back(dnormed, hat1, rstd1, gain[:width])
    datt_low = datt.astype(BF)
    dctx = mm_nt(datt_low, w_out).astype(BF)
    grads = (mm_tn(normed_low, dhidden), mm_tn(activ, dmixed_low))
    vectors = dict(
        bv=colsum(dctx),
        b_resid=jnp.concatenate([colsum(datt), colsum(dmixed)]),
        gain=jnp.concatenate([dg1, dg2]),
        shift=jnp.concatenate([dc1, dc2]),
        b_in=colsum(dhidden),
    )
    return datt, dctx, grads, vectors


def per_device(short_tokens, long_tokens, short_len, long_len, pair_index, *params):
    n = lax.axis_size("stream") * lax.axis_size("dp")
    index = lax.axis_index("stream") * lax.axis_size("dp") + lax.axis_index("dp")
    width = short_tokens.shape[-1]
    spans = (short_tokens.shape[2], long_tokens.shape[2])
    counts = (short_tokens.shape[1], long_tokens.shape[1])
    sents = sum(counts)
    w_qkv, b_qv, w_out, b_resid, gain, shift, w_in, b_in, w_back = params
    w_qkv, b_qv, w_out, b_resid, gain, shift, w_in, b_in, w_back = (hbm(p) for p in (w_qkv, b_qv, w_out, b_resid, gain, shift, w_in, b_in, w_back))
    w = dict(qkv=w_qkv, b_qv=b_qv, out=w_out, b_resid=b_resid, gain=gain, shift=shift, b_in=b_in, back=w_back) | {"in": w_in}
    short, long = hbm(short_tokens.reshape(-1, width)), hbm(long_tokens.reshape(-1, width))
    lens = jnp.concatenate([short_len.reshape(-1), long_len.reshape(-1)])
    lens_wide = jnp.repeat(lens, HEADS)[:, None]

    outs = forward(short, long, lens, lens_wide, w, spans, counts[0], sents)
    y, qkv, prob, ctx, hat1, rstd1, act, slope, hat2, rstd2 = (hbm(a) for a in outs[:10])
    sent, *kept = outs[10:]
    one_kernel = n * sents <= 512
    if one_kernel:
        top_args = (index.reshape(1).astype(jnp.int32), *gather_near(sent, n), pair_index[None, :])
    else:
        datt, dctx, top_g, top_vec = top_rows(gather_rows(sent, n), pair_index, tuple(p[1] for p in params))
        top_args = tuple(lax.dynamic_slice_in_dim(v, index * sents, sents, 0) for v in (datt, dctx))
    bits = my_bits(n)
    bit = bits[0].reshape(1).astype(jnp.int32)

    keep, send, dlow, sums2, *top_kept = turn(top_args, y, [hbm(a) for a in kept], w, hat2, rstd2, act, spans, sents)
    first = Lane(sum_steps(keep, send, n, bits), n)
    stage([first])
    keep, send, datt0, dctx0, sums1, sumin = stage([first], lambda *a: ff_back(*a, w), (dlow, hat1, rstd1, slope, ctx))
    second = Lane(sum_steps(keep, send, n, bits), n)
    stage([first, second])
    dqkv, keep, send = stage([first, second], lambda *a: attention_back(*a, short, long), (qkv, prob, dctx0, sums1, sums2, sumin))
    third = Lane(sum_steps(keep, send, n, bits), n)
    lanes = [first, second, third]
    stage([third])
    dshort, dlong = stage(lanes, lambda *a: input_back(*a, w, counts[0] * spans[0]), (hbm(dqkv), datt0))
    stage(lanes)
    if one_kernel:
        gin1, gback1, top_sums, top_sumin = stage([first, second], lambda *a: top_grads(*a, w), [hbm(a) for a in top_kept])
    else:
        gin1, gback1 = (jnp.stack([g, g]) for g in top_g)
        rows_of = [top_vec[k].reshape(2, width) for k in ("b_resid", "gain", "shift")]
        top_sums = jnp.concatenate(rows_of + [top_vec["bv"][None], jnp.zeros((1, width), F32)], 0)
        top_sumin = top_vec["b_in"][None]
    while first.result is None:
        stage(lanes)
    g_qkv, g_out, g_back = stage([second, third], lambda *a: unpack_first(bit, *a), (first.result, gback1))
    while second.result is None:
        stage([second, third])
    g_in, g_out = stage([third], lambda *a: unpack_second(bit, *a), (second.result, gin1, g_out))
    while third.result is None:
        stage([third])
    g_qkv, g_bqv, g_bresid, g_gain, g_shift, g_bin = unpack_third(bit, third.result, g_qkv, top_sums, top_sumin)
    outs = (g_qkv, g_bqv, g_out, g_bresid, g_gain, g_shift, g_in, g_bin, g_back)
    return outs + (dshort.reshape((1, counts[0], spans[0], width)), dlong.reshape((1, counts[1], spans[1], width)))


def solution(mesh):
    split = P("stream", "dp", None, None)
    in_specs = (split, split, P("stream", "dp"), P("stream", "dp")) + (P(),) * 10
    out_specs = (P(),) * 9 + (split, split)
    return jax.shard_map(per_device, mesh=mesh, in_specs=in_specs, out_specs=out_specs, check_vma=False)
```

```python
import functools
import math

import jax
import jax.numpy as jnp
from jax import lax
from jax.experimental import pallas as pl
from jax.experimental.pallas import tpu as pltpu
from jax.sharding import PartitionSpec as P

HEADS = 8
BF = jnp.bfloat16
F32 = jnp.float32
AXES = ("stream", "dp")
logit_scale = 40.0
margin = 0.3
norm_eps = 1e-12
unit_eps = 1e-06
BLOCK = 128
STEP = 256
VMEM = 30 * 1024 * 1024
SCHEDULE = (
    ("1", ""), ("1", "ff"), ("12", ""), ("12", "attention"), ("3", ""), ("123", "input"), ("123", ""),
    ("12", "top"), ("123", ""), ("23", "unpack1"), ("23", ""), ("3", "unpack2"), ("3", ""),
)


def mm(a, b):
    return jnp.dot(a, b, preferred_element_type=F32)


def mm_nt(a, b):
    return lax.dot_general(a, b, (((1,), (1,)), ((), ())), preferred_element_type=F32)


def mm_tn(a, b):
    return lax.dot_general(a, b, (((0,), (0,)), ((), ())), preferred_element_type=F32)


def ln_stats(v):
    centre = v - jnp.mean(v, -1, keepdims=True)
    rstd = lax.rsqrt(jnp.mean(centre * centre, -1, keepdims=True) + norm_eps)
    return centre * rstd, rstd


def ln_back(dy, vhat, rstd, gain):
    dhat = dy * gain
    return (dhat - jnp.mean(dhat, -1, keepdims=True) - vhat * jnp.mean(dhat * vhat, -1, keepdims=True)) * rstd


def gelu_pair(v):
    cdf = 0.5 * (1.0 + lax.erf(v * (1.0 / math.sqrt(2.0))))
    pdf = jnp.exp(-0.5 * v * v) * (1.0 / math.sqrt(2.0 * math.pi))
    return v * cdf, cdf + v * pdf


def colsum(v):
    return jnp.sum(v.astype(F32), 0)


def rowsum(v):
    return jnp.sum(v.astype(F32), 0, keepdims=True)


SMEM = pl.BlockSpec(memory_space=pltpu.SMEM)
ANY = pl.BlockSpec(memory_space=pl.ANY)
AS_IS = pl.BlockSpec(memory_space=pl.ANY)


def hbm(a):
    return pltpu.with_memory_space_constraint(a, memory_space=pltpu.HBM)


def hbm_shape(dims, dtype):
    return pltpu.HBM(dims, dtype)


def whole(a):
    return pl.BlockSpec(a.shape, lambda i: (0,) * len(a.shape))


def shape(dims, dtype):
    return jax.ShapeDtypeStruct(dims, dtype)


def layer_of(a, level, rows=None, cols=None, at=lambda i: (0, 0)):
    rows, cols = rows or a.shape[1], cols or a.shape[2]
    return a, pl.BlockSpec((None, rows, cols), lambda i: (level, *at(i)))


def kernel_call(body, name, grid, ins, outs, flops, scratch=(), aliases=None, vmem=VMEM):
    size = sum(a.size * a.dtype.itemsize for a, _ in ins) + sum(
        math.prod(s.shape) * jnp.dtype(s.dtype).itemsize for s, _ in outs
    )
    return pl.pallas_call(
        body,
        grid=grid,
        in_specs=[s for _, s in ins],
        out_specs=[s for _, s in outs],
        out_shape=[s for s, _ in outs],
        scratch_shapes=list(scratch),
        input_output_aliases=aliases or {},
        compiler_params=pltpu.CompilerParams(vmem_limit_bytes=vmem),
        cost_estimate=pl.CostEstimate(flops=int(flops), bytes_accessed=int(size), transcendentals=0),
        name=name,
    )(*[hbm(a) if s is ANY else a for a, s in ins])


def routes(n):
    top, y = n >> 1, 2
    rest = [1 << k for k in range(2, n.bit_length() - 2)]
    for k in range(1, len(rest)):
        rest[k] |= rest[k - 1]
    halved = [(1, 1), (top, y), (y, top)]
    added = list(zip(rest, rest[::-1]))
    return halved, added


def swap(value, n, hop):
    return lax.ppermute(value, AXES, [(i, i ^ (hop[1] if i & 1 else hop[0])) for i in range(n)])


def device_index():
    return lax.axis_index("stream") * lax.axis_size("dp") + lax.axis_index("dp")


def coordinate(index, hop, n):
    value = (index // (1 << (hop.bit_length() - 1))) % 2
    if hop in (1, 2, n >> 1) or 2 * hop >= n >> 1:
        return value
    above = (index // (1 << hop.bit_length())) % 2
    return value + above - 2 * value * above


def my_bits(n):
    index = device_index()
    core = index % 2
    halved, _ = routes(n)
    return [jnp.where(core == 0, coordinate(index, a, n), coordinate(index, b, n)) for a, b in halved]


def split_body(bit_ref, mine_a, got_a, mine_b, got_b, keep_ref, send_ref):
    keep_ref[...] = (mine_a[...].astype(F32) + got_a[...].astype(F32)).astype(BF)
    send_ref[...] = (mine_b[...].astype(F32) + got_b[...].astype(F32)).astype(BF)


def add_and_split(mine, got, bit):
    rows, width = mine.shape[0] // 2, mine.shape[1]
    steps = 2 if rows % 32 == 0 and rows >= 256 else 1
    block = rows // steps
    kept = pl.BlockSpec((block, width), lambda j, bit: (bit[0] * steps + j, 0))
    sent = pl.BlockSpec((block, width), lambda j, bit: ((1 - bit[0]) * steps + j, 0))
    out = pl.BlockSpec((block, width), lambda j, bit: (j, 0))
    ins = [(mine, kept), (got, kept), (mine, sent), (got, sent)]
    outs = [(shape((rows, width), BF), out)] * 2
    return unpack_call(split_body, "add_and_split", bit.reshape(1).astype(jnp.int32), (steps,), ins, outs, {}, 12 * rows * width)


def sum_steps(keep, send, n, bits):
    halved, added = routes(n)
    for k, hop in enumerate(halved[:-1]):
        got = yield send, hop
        keep, send = add_and_split(keep, got, bits[k + 1])
    got = yield send, halved[-1]
    cur = (keep.astype(F32) + got.astype(F32)).astype(BF)
    for hop in added:
        got = yield cur, hop
        cur = (cur.astype(F32) + got.astype(F32)).astype(BF)
    for hop, bit in reversed(list(zip(halved, bits))[1:]):
        got = yield cur, hop
        low = jnp.where(bit == 0, cur, got)
        high = jnp.where(bit == 0, got, cur)
        cur = jnp.concatenate([low, high], 0)
    got = yield cur, halved[0]
    return cur, got


class Lane:
    def __init__(self, steps, n):
        self.n, self.steps, self.result = n, steps, None
        self.ask = next(self.steps)

    def feed(self, got):
        try:
            self.ask = self.steps.send(got)
        except StopIteration as end:
            self.result = end.value


def stage(lanes, work=None, args=()):
    lanes = [lane for lane in lanes if lane.result is None]
    asked, args = lax.optimization_barrier(([lane.ask[0] for lane in lanes], args))
    got = [swap(value, lane.n, lane.ask[1]) for value, lane in zip(asked, lanes)]
    out = work(*args) if work else ()
    got, out = lax.optimization_barrier((got, out))
    for lane, value in zip(lanes, got):
        lane.feed(value)
    return out


def gather_rows(rows, n):
    index = device_index()
    cur = rows[None]
    for flip in [1 << k for k in range(1, n.bit_length() - 1)] + [1]:
        got = swap(cur, n, (flip, flip))
        bit = (index // flip) % 2
        low, high = jnp.where(bit == 0, cur, got), jnp.where(bit == 0, got, cur)
        cur = jnp.stack([low, high], 1 if flip == 1 else 0).reshape((2 * cur.shape[0],) + rows.shape)
    return cur.reshape(n * rows.shape[0], rows.shape[1])


def hop_groups(n):
    hops = [1 << k for k in range(1, n.bit_length() - 1)]
    half = (len(hops) + 1) // 2
    hops = [hops[0], hops[-1]] + hops[1:-1] if len(hops) > 2 else hops
    groups = [hops[k : k + 2] for k in range(0, 2 * half, 2)]
    return [[a, b, a | b] if len(g) == 2 else g for g in groups for a, b in [(g[0], g[-1])]]


def gather_near(rows, n):
    cur = rows
    for group in hop_groups(n):
        cur = jnp.concatenate([cur] + [swap(cur, n, (hop, hop)) for hop in group], 0)
    return cur, swap(cur, n, (1, 1))


def near_offsets(n):
    offsets = [0]
    for group in hop_groups(n):
        offsets = offsets + [hop ^ o for hop in group for o in offsets]
    return offsets


def stream_in(pairs, sems):
    loads = [pltpu.make_async_copy(a, b, sems.at[k]) for k, (a, b) in enumerate(pairs)]
    for load in loads:
        load.start()
    return loads


class Halves:
    def __init__(self, keep, send, block, sems):
        self.keep, self.send, self.block, self.sems = keep, send, block, sems
        self.low_is_kept = lax.axis_index("dp") % 2 == 0
        self.pieces = 0
        self.waits = []

    def put(self, at, value):
        self.block[at : at + value.shape[0]] = value
        half = self.keep.shape[0]
        end = at + value.shape[0]
        for lower, a, b in ((True, at, min(end, half)), (False, max(at, half), end)):
            if a >= b:
                continue
            base = 0 if lower else half
            sem = self.sems.at[self.pieces]
            self.pieces += 1
            copies = [
                pltpu.make_async_copy(self.block.at[a:b], ref.at[a - base : b - base], sem) for ref in (self.keep, self.send)
            ]
            kept = self.low_is_kept if lower else jnp.logical_not(self.low_is_kept)

            @pl.when(kept)
            def _(copy=copies[0]):
                copy.start()

            @pl.when(jnp.logical_not(kept))
            def _(copy=copies[1]):
                copy.start()

            self.waits.append(copies[0])

    def finish(self):
        for copy in self.waits:
            copy.wait()


def starts(sents, spans, rows):
    s = lax.broadcasted_iota(jnp.int32, (sents, rows), 0)
    r = lax.broadcasted_iota(jnp.int32, (sents, rows), 1)
    half = sents // 2
    at = jnp.where(s < half, s * spans[0], half * spans[0] + (s - half) * spans[1])
    return (r == at).astype(BF)


def spread(sents):
    a = lax.broadcasted_iota(jnp.int32, (sents * HEADS, sents), 0) // HEADS
    return (a == lax.broadcasted_iota(jnp.int32, (sents * HEADS, sents), 1)).astype(BF)


def own_head(sents, width):
    a = lax.broadcasted_iota(jnp.int32, (sents * HEADS, width), 0) % HEADS
    return a == lax.broadcasted_iota(jnp.int32, (sents * HEADS, width), 1) // (width // HEADS)


def sum_heads(v, keep, sents):
    return jnp.sum(jnp.where(keep, v, 0.0).reshape(sents, HEADS, v.shape[1]), 1)


def ask(y, spans, lens, wqkv_ref, wout_ref, bq, bv, bo, sents):
    rows, width = y.shape
    keep = own_head(sents, width)
    cls = mm(starts(sents, spans, rows), y).astype(BF)
    q = (mm(cls, wqkv_ref[:, :width]) + bq).astype(BF)
    wide = jnp.where(keep, mm(spread(sents), q), 0.0).astype(BF)
    key = mm_nt(wide, wqkv_ref[:, width : 2 * width]).astype(BF)
    half = sents // 2
    sent = lax.broadcasted_iota(jnp.int32, (sents * HEADS, 1), 0) // HEADS
    begin = jnp.where(sent < half, sent * spans[0], half * spans[0] + (sent - half) * spans[1])
    place = lax.broadcasted_iota(jnp.int32, (sents * HEADS, rows), 1) - begin
    seen = (place >= 0) & (place < lens)
    logit = jnp.where(seen, mm_nt(key, y) * (1.0 / math.sqrt(width // HEADS)), -jnp.inf)
    power = jnp.exp(logit - jnp.max(logit, 1, keepdims=True))
    prob = (power * (1.0 / jnp.sum(power, 1, keepdims=True))).astype(BF)
    mixed = mm(prob, y).astype(BF)
    ctx = (sum_heads(mm(mixed, wqkv_ref[:, 2 * width :]), keep, sents) + bv).astype(BF)
    attended = (cls.astype(F32) + mm(ctx, wout_ref[...]) + bo).astype(BF)
    return attended, ctx, wide, key, prob, mixed


def halves(v, first):
    zero = jnp.zeros_like(v)
    return jnp.concatenate([jnp.where(first, v, zero), jnp.where(first, zero, v)], 0)


def join_halves(v, first):
    return jnp.where(first, v[: v.shape[0] // 2], v[v.shape[0] // 2 :])


def first_head(width):
    return lax.broadcasted_iota(jnp.int32, (1, 2 * width // HEADS), 1) < width // HEADS


def key_bias(lens_ref, block, span_short, count_short):
    key = lax.broadcasted_iota(jnp.int32, (BLOCK, 1), 0)
    query = lax.broadcasted_iota(jnp.int32, (1, BLOCK), 1)
    per = BLOCK // span_short
    blocks_short = count_short // per
    is_short = block < blocks_short
    at = jnp.where(is_short, block * per, count_short + block - blocks_short)
    limit = jnp.zeros((BLOCK, 1), jnp.int32)
    for s in range(per):
        inside = key // span_short == s
        limit = jnp.where(inside, jnp.where(is_short, lens_ref[at + jnp.where(is_short, s, 0)] + s * span_short, 0), limit)
    limit = jnp.where(is_short, limit, lens_ref[at])
    same = (key // span_short == query // span_short) | jnp.logical_not(is_short)
    return jnp.where((key < limit) & same, 0.0, -jnp.inf).astype(F32)


def vectors(level, width, bqv_ref, bresid_ref, gain_ref, shift_ref):
    row = slice(level, level + 1)
    low, high = slice(0, width), slice(width, 2 * width)
    return [ref[row, part] for ref in (bqv_ref, bresid_ref, gain_ref, shift_ref) for part in (low, high)]


def forward_body(
    spans, count, lens_ref, short_ref, long_ref, wqkv_ref, wout_ref, win_ref, wback_ref, bin_ref, bqv_ref, bresid_ref, gain_ref, shift_ref,
    wide_lens_ref, wqkv_hbm, wout_hbm,
    y_hbm, qkv_hbm, prob_hbm, ctx_hbm, hat1_hbm, rstd1_hbm, act_hbm, slope_hbm, hat2_hbm, rstd2_hbm,
    sent_ref, ctx1_ref, wide_ref, key_ref, prob1_ref, mixed_ref, y_s, wqkv1_ref, wout1_ref, got,
    y_2, qkv_2, prob_2, ctx_2, hat1_2, rstd1_2, act_2, slope_2, hat2_2, rstd2_2, left,
):
    step = pl.program_id(0)
    loads = [pltpu.make_async_copy(a.at[1], b, got.at[k]) for k, (a, b) in enumerate(((wqkv_hbm, wqkv1_ref), (wout_hbm, wout1_ref)))]

    @pl.when(step == 0)
    def _():
        for load in loads:
            load.start()

    far = (y_hbm, qkv_hbm, prob_hbm, ctx_hbm, hat1_hbm, rstd1_hbm, act_hbm, slope_hbm, hat2_hbm, rstd2_hbm)
    slots = (y_2, qkv_2, prob_2, ctx_2, hat1_2, rstd1_2, act_2, slope_2, hat2_2, rstd2_2)
    slot = step % 2

    def stores(slot, step):
        copies = []
        for k, (near, there) in enumerate(zip(slots, far)):
            size = near.shape[1]
            to = there.at[pl.ds(pl.multiple_of(step * size, size), size)]
            copies.append(pltpu.make_async_copy(near.at[slot], to, left.at[slot, k]))
        return copies

    @pl.when(step >= 2)
    def _():
        for store in stores(slot, 0):
            store.wait()

    y_ref, qkv_ref, prob_ref, ctx_ref, hat1_ref, rstd1_ref, act_ref, slope_ref, hat2_ref, rstd2_ref = (near.at[slot] for near in slots)
    x = jnp.where(step == 0, short_ref[...], long_ref[...])
    rows, width = x.shape
    bq, bv, bo, bb, g1, g2, c1, c2 = vectors(0, width, bqv_ref, bresid_ref, gain_ref, shift_ref)
    pair = 2 * width // HEADS
    first = first_head(width)
    scale = 1.0 / math.sqrt(width // HEADS)
    bias = jnp.concatenate([bq, jnp.zeros_like(bq), bv], 1)
    qkv = (mm(x, wqkv_ref[...]) + bias).astype(BF)
    qkv_ref[...] = qkv
    blocks = []
    for b in range(rows // BLOCK):
        r = slice(b * BLOCK, (b + 1) * BLOCK)
        hide = key_bias(lens_ref, step * (rows // BLOCK) + b, spans[0], count)
        hide = jnp.concatenate([hide, hide], 1)
        cols = []
        for p in range(HEADS // 2):
            q, k, v = (qkv[r, m * width + p * pair : m * width + (p + 1) * pair] for m in range(3))
            logit = mm_nt(k, halves(q, first)) * scale + hide
            power = jnp.exp(logit - jnp.max(logit, 0, keepdims=True))
            prob = (power * (1.0 / jnp.sum(power, 0, keepdims=True))).astype(BF)
            prob_ref[b, p] = prob
            cols.append(join_halves(mm_tn(prob, v), first))
        blocks.append(jnp.concatenate(cols, 1).astype(BF))
    ctx = jnp.concatenate(blocks, 0)
    ctx_ref[...] = ctx
    hat1, rstd1 = ln_stats(x.astype(F32) + mm(ctx, wout_ref[...]) + bo)
    normed = hat1 * g1 + c1
    low = normed.astype(BF)
    hat1_ref[...] = hat1.astype(BF)
    rstd1_ref[...] = jnp.broadcast_to(rstd1, rstd1_ref.shape)
    act, slope = gelu_pair(mm(low, win_ref[...]) + bin_ref[0:1])
    act = act.astype(BF)
    act_ref[...] = act
    slope_ref[...] = slope.astype(BF)
    hat2, rstd2 = ln_stats(normed + mm(act, wback_ref[...]) + bb)
    hat2_ref[...] = hat2.astype(BF)
    rstd2_ref[...] = jnp.broadcast_to(rstd2, rstd2_ref.shape)
    y = (hat2 * g2 + c2).astype(BF)
    y_ref[...] = y
    y_s[pl.ds(pl.multiple_of(step * rows, rows), rows)] = y
    for store in stores(slot, step):
        store.start()

    @pl.when(step == pl.num_programs(0) - 1)
    def _():
        for load in loads:
            load.wait()
        bq, bv, bo = vectors(1, width, bqv_ref, bresid_ref, gain_ref, shift_ref)[:3]
        outs = ask(y_s[...], spans, wide_lens_ref[...], wqkv1_ref, wout1_ref, bq, bv, bo, sent_ref.shape[0])
        for ref, value in zip((sent_ref, ctx1_ref, wide_ref, key_ref, prob1_ref, mixed_ref), outs):
            ref[...] = value
        for k in range(2):
            for store in stores(k, 0):
                store.wait()


def by_rows(cols):
    return pl.BlockSpec((STEP, cols), lambda i: (i, 0))


def from_buckets(short, long):
    width = short.shape[1]
    return [
        (short, pl.BlockSpec((STEP, width), lambda i: (0, 0))),
        (long, pl.BlockSpec((STEP, width), lambda i: (jnp.maximum(i - 1, 0), 0))),
    ]


def small_ins(w):
    return [(w[k], whole(w[k])) for k in ("b_qv", "b_resid", "gain", "shift")]


def forward(short, long, lens, wide_lens, w, spans, count, sents):
    rows, width = short.shape[0] + long.shape[0], short.shape[1]
    ff = w["in"].shape[2]
    per = STEP // BLOCK
    ins = [(lens, SMEM)] + from_buckets(short, long)
    ins += [layer_of(w[name], 0) for name in ("qkv", "out", "in", "back")] + [(w["b_in"], whole(w["b_in"]))] + small_ins(w)
    cols = [(width, BF), (3 * width, BF), None, (width, BF), (width, BF), (128, F32), (ff, BF), (ff, BF), (width, BF), (128, F32)]
    outs = [(hbm_shape((rows, c[0]), c[1]) if c else hbm_shape((rows // BLOCK, HEADS // 2, BLOCK, 2 * BLOCK), BF), ANY) for c in cols]
    slots = [pltpu.VMEM((2, STEP, c[0]), c[1]) if c else pltpu.VMEM((2, per, HEADS // 2, BLOCK, 2 * BLOCK), BF) for c in cols]
    ins += [(wide_lens, whole(wide_lens)), (w["qkv"], ANY), (w["out"], ANY)]
    wide = sents * HEADS
    outs += [(s, whole(s)) for s in [shape((sents, width), BF)] + [hbm_shape(d, BF) for d in ((sents, width), (wide, width), (wide, width), (wide, rows), (wide, width))]]
    scratch = [pltpu.VMEM(d, BF) for d in ((rows, width), (width, 3 * width), (width, width))] + [pltpu.SemaphoreType.DMA((2,))]
    scratch += slots + [pltpu.SemaphoreType.DMA((2, len(slots)))]
    body = functools.partial(forward_body, spans, count)
    return kernel_call(body, "layer0_forward", (rows // STEP,), ins, outs, 2 * rows * width * (4 * width + 2 * ff), scratch, vmem=VMEM + VMEM // 4)


def top_forward(attended, win_ref, bin_ref, g1, c1):
    hat1, rstd1 = ln_stats(attended.astype(F32))
    normed = hat1 * g1 + c1
    low = normed.astype(BF)
    return hat1, rstd1, normed, low, mm(low, win_ref[...]) + bin_ref[1:2]


def gelu(v):
    return v * (0.5 * (1.0 + lax.erf(v * (1.0 / math.sqrt(2.0)))))


def top_part(index_ref, every_ref, pair_ref, dy_ref, hat2_s, rstd2_s, low_vectors, bin_ref, win, wback, wout, sents):
    pairs = pair_ref.shape[1]
    _, _, _, bb, g1, g2, c1, c2 = low_vectors
    hat1, _ = ln_stats(every_ref[...].astype(F32))
    normed = hat1 * g1 + c1
    win_ref = win()
    act = gelu(mm(normed.astype(BF), win_ref[...]) + bin_ref[1:2]).astype(BF)
    wback_ref = wback()
    hat2, rstd2 = ln_stats(normed + mm(act, wback_ref[...]) + bb)
    hat2_s[...] = hat2
    rstd2_s[...] = jnp.broadcast_to(rstd2, rstd2_s.shape)
    pooled = hat2 * g2 + c2
    radius = lax.rsqrt(jnp.sum(pooled * pooled, -1, keepdims=True) + unit_eps)
    unit = pooled * radius
    src, tgt = unit[:pairs].astype(BF), unit[pairs:].astype(BF)
    positive = (pair_ref[...] == lax.broadcasted_iota(jnp.int32, (pairs, pairs), 0)).astype(F32)
    logits = logit_scale * (mm_nt(tgt, src) - margin * positive)

    def soft(axis):
        powers = jnp.exp(logits - jnp.max(logits, axis, keepdims=True))
        return powers * (1.0 / jnp.sum(powers, axis, keepdims=True))

    dscore = (0.5 * logit_scale * (soft(1) + soft(0) - 2.0 * positive)).astype(BF)
    dunit = jnp.concatenate([mm_tn(dscore, tgt), mm(dscore, src)], 0)
    dy_ref[...] = radius * (dunit - unit * jnp.sum(dunit * unit, -1, keepdims=True))
    mine = pl.ds(pl.multiple_of(index_ref[0] * sents, sents), sents)
    own_hat1, own_rstd1, _, _, own_hid = top_forward(every_ref[mine], win_ref, bin_ref, g1, c1)
    dmixed = ln_back(dy_ref[mine], hat2_s[mine], rstd2_s[mine, 0:1], g2)
    dhidden = (mm_nt(dmixed.astype(BF), wback_ref[...]) * gelu_pair(own_hid)[1]).astype(BF)
    dnormed = dmixed + mm_nt(dhidden, win_ref[...])
    datt = ln_back(dnormed, own_hat1, own_rstd1, g1)
    return datt, mm_nt(datt.astype(BF), wout()[...]).astype(BF)


def top_grads_body(every_ref, dy_ref, wout_ref, win_ref, wback_ref, bin_ref, bqv_ref, bresid_ref, gain_ref, shift_ref,
                   gin_ref, gback_ref, sums_ref, sumin_ref):
    width = dy_ref.shape[1]
    _, _, _, bb, g1, g2, c1, c2 = vectors(1, width, bqv_ref, bresid_ref, gain_ref, shift_ref)
    hat1, rstd1, normed, low, hid = top_forward(every_ref[...], win_ref, bin_ref, g1, c1)
    act, slope = gelu_pair(hid)
    act = act.astype(BF)
    hat2, rstd2 = ln_stats(normed + mm(act, wback_ref[...]) + bb)
    dy = dy_ref[...]
    dmixed = ln_back(dy, hat2, rstd2, g2)
    dmixed_low = dmixed.astype(BF)
    gback_ref[...] = mm_tn(act, dmixed_low)
    dhidden = (mm_nt(dmixed_low, wback_ref[...]) * slope).astype(BF)
    gin_ref[...] = mm_tn(low, dhidden)
    dnormed = dmixed + mm_nt(dhidden, win_ref[...])
    datt = ln_back(dnormed, hat1, rstd1, g1)
    sumin_ref[...] = rowsum(dhidden)
    parts = (datt, dmixed, dnormed * hat1, dy * hat2, dnormed, dy, mm_nt(datt.astype(BF), wout_ref[...]).astype(BF))
    for k, part in enumerate(parts):
        sums_ref[k : k + 1] = rowsum(part)
    sums_ref[7:8] = jnp.zeros((1, width), F32)


def top_grads(every, dy, w):
    width = dy.shape[1]
    ff = w["in"].shape[2]
    rows = every.shape[0]
    ins = [(every, whole(every)), (dy, whole(dy))] + [layer_of(w[k], 1) for k in ("out", "in", "back")]
    ins += [(w["b_in"], whole(w["b_in"]))] + small_ins(w)

    def upper(a, b):
        return hbm_shape((2, a, b), F32), pl.BlockSpec((None, a, b), lambda i: (1, 0, 0))

    sums, sumin = shape((8, width), F32), shape((1, ff), F32)
    outs = [upper(width, ff), upper(ff, width), (sums, whole(sums)), (sumin, whole(sumin))]
    return kernel_call(top_grads_body, "top_grads", (1,), ins, outs, 6 * rows * width * (width + 2 * ff))


def turn_body(spans, sents, with_top, *refs):
    refs = list(refs)

    def take(count):
        out, refs[:count] = refs[:count], []
        return out

    (gain_ref,) = take(1)
    late = take(10)
    if with_top:
        index_ref, near_ref, other_ref, pair_ref, wout_hbm, bin_ref, bqv_ref, bresid_ref, shift_ref, win_hbm, wback_hbm = take(11)
    else:
        datt_ref, dctx_ref = take(2)
    keep_hbm, send_hbm, low_hbm, sums_ref = take(4)
    if with_top:
        every_hbm, dy_hbm = take(2)
    here = take(10)
    wqkv_ref, y_ref, wide_ref, key_ref, prob_ref, mixed_ref, ctx_ref, hat2_ref, rstd2_ref, act_ref = here
    low_ref, block, got, sent, left_sem = take(5)
    loads = list(zip([late[0].at[1]] + late[1:], here))
    if with_top:
        win_ref, wback_ref, wout_ref, top_hat2, top_rstd2, every_ref, dy_ref, arrivals = take(8)
        offsets = near_offsets(2 * near_ref.shape[0] // sents)
        pieces = []
        for p, offset in enumerate(offsets):
            for core, ref in enumerate((near_ref, other_ref)):
                device = index_ref[0] ^ (offset + core)
                to = every_ref.at[pl.ds(pl.multiple_of(device * sents, sents), sents)]
                pieces.append(pltpu.make_async_copy(ref.at[p * sents : (p + 1) * sents], to, arrivals.at[2 * p + core]))
        for piece in pieces:
            piece.start()
        loads = [(win_hbm.at[1], win_ref), (wback_hbm.at[1], wback_ref), (wout_hbm.at[1], wout_ref)] + loads
    loads = [pltpu.make_async_copy(a, b, got.at[k]) for k, (a, b) in enumerate(loads)]
    for load in loads:
        load.start()
    rows, width = y_ref.shape
    if with_top:

        def arrived(load, ref):
            def wait():
                load.wait()
                return ref

            return wait

        values = vectors(1, width, bqv_ref, bresid_ref, gain_ref, shift_ref)
        for piece in pieces:
            piece.wait()
        win, wback, wout = (arrived(load, ref) for load, ref in zip(loads, (win_ref, wback_ref, wout_ref)))
        datt, dctx = top_part(index_ref, every_ref, pair_ref, dy_ref, top_hat2, top_rstd2, values, bin_ref, win, wback, wout, sents)
        loads = loads[3:]
        left = [(every_ref, every_hbm), (dy_ref, dy_hbm)]
    else:
        datt, dctx = datt_ref[...], dctx_ref[...]
        left = []
    keep = own_head(sents, width)
    first = starts(sents, spans, rows)
    d_wide = jnp.where(keep, mm(spread(sents), dctx), 0.0).astype(BF)
    for load in loads[:7]:
        load.wait()
    prob_low = prob_ref[...]
    d_value = mm_nt(d_wide, wqkv_ref[:, 2 * width :]).astype(BF)
    y = y_ref[...]
    dprob = mm_nt(d_value, y)
    prob = prob_low.astype(F32)
    dlogit = prob * (dprob - jnp.sum(prob * dprob, 1, keepdims=True))
    dscore = (dlogit * (1.0 / math.sqrt(width // HEADS))).astype(BF)
    pulled = mm(dscore, y).astype(BF)
    dq = sum_heads(mm(pulled, wqkv_ref[:, width : 2 * width]), keep, sents).astype(BF)
    dcls = mm_nt(dq, wqkv_ref[:, :width]) + datt
    high = dcls.astype(BF)
    from_left = jnp.concatenate([dscore, prob_low, first, first], 0)
    from_right = jnp.concatenate([key_ref[...], d_value, high, (dcls - high.astype(F32)).astype(BF)], 0)
    dy = mm_tn(from_left, from_right)
    loads[7].wait()
    loads[8].wait()
    hat2 = hat2_ref[...].astype(F32)
    dmixed = ln_back(dy, hat2, rstd2_ref[:, 0:1], gain_ref[0:1, width:])
    low_ref[...] = dmixed.astype(BF)
    left = stream_in([(low_ref, low_hbm)] + left, left_sem)
    sums_ref[0:1] = rowsum(dmixed)
    sums_ref[1:2] = rowsum(dy * hat2)
    sums_ref[2:3] = rowsum(dy)
    sums_ref[3:4] = rowsum(dq)
    sums_ref[4:8] = jnp.zeros((4, width), F32)
    place = Halves(keep_hbm, send_hbm, block, sent)
    ff = act_ref.shape[1]
    tiles = ff // width
    cls = mm(first, y).astype(BF)
    tail = ((cls, dq), (pulled, wide_ref[...]), (mixed_ref[...], d_wide), (ctx_ref[...], datt.astype(BF)))
    for k, (a, b) in enumerate(tail):
        place.put((tiles + k) * width, mm_tn(a, b).astype(BF))
    loads[9].wait()
    for k in range(tiles):
        place.put(k * width, mm_tn(act_ref[:, k * width : (k + 1) * width], low_ref[...]).astype(BF))
    place.finish()
    for copy in left:
        copy.wait()


def turn(top_args, y, kept, w, hat2, rstd2, act, spans, sents):
    rows, width = y.shape
    ff = act.shape[1]
    ctx, wide, key, prob, mixed = kept
    with_top = len(top_args) == 4
    ins = [(w["gain"], whole(w["gain"]))]
    ins += [(a, ANY) for a in (w["qkv"], y, wide, key, prob, mixed, ctx, hat2, rstd2, act)]
    blocks = ff // width + 4
    outs = [(shape((blocks * width // 2, width), BF), ANY)] * 2
    outs += [(hbm_shape((rows, width), BF), ANY)] + [(s, whole(s)) for s in (shape((8, width), F32),)]
    asked = sents * HEADS
    dims = [((width, 3 * width), BF), ((rows, width), BF), ((asked, width), BF), ((asked, width), BF), ((asked, rows), BF), ((asked, width), BF)]
    dims += [((sents, width), BF), ((rows, width), BF), ((rows, 128), F32), ((rows, ff), BF), ((rows, width), BF), ((blocks * width, width), BF)]
    scratch = [pltpu.VMEM(*d) for d in dims]
    scratch += [pltpu.SemaphoreType.DMA((13,)), pltpu.SemaphoreType.DMA((blocks,)), pltpu.SemaphoreType.DMA((3,))]
    flops = 2 * rows * width * (ff + 512)
    if with_top:
        index, near, other, pair = top_args
        every = shape((2 * near.shape[0], width), BF)
        ins += [(index, SMEM), (near, AS_IS), (other, AS_IS), (pair, whole(pair)), (w["out"], ANY)]
        ins += [(w[k], whole(w[k])) for k in ("b_in", "b_qv", "b_resid", "shift")] + [(w["in"], ANY), (w["back"], ANY)]
        outs += [(hbm_shape(every.shape, t), ANY) for t in (BF, F32)]
        dims = [((width, ff), BF), ((ff, width), BF), ((width, width), BF), (every.shape, F32), ((every.shape[0], 128), F32), (every.shape, BF), (every.shape, F32)]
        scratch += [pltpu.VMEM(*d) for d in dims]
        scratch += [pltpu.SemaphoreType.DMA((every.shape[0] // sents,))]
        flops += 4 * every.shape[0] * width * ff
    else:
        ins += [(a, whole(a)) for a in top_args]
    return kernel_call(functools.partial(turn_body, spans, sents, with_top), "turn", (1,), ins, outs, flops, scratch, vmem=VMEM + VMEM // 4)


VECTOR_ROWS = 128


def ff_back_body(gain_ref, shift_ref, low_hbm, hat1_hbm, rstd1_hbm, wback_hbm, slope_hbm, win_hbm, wout_hbm, ctx_hbm,
                 keep_hbm, send_hbm, datt_ref, dctx_ref, sums_ref, sumin_ref,
                 low_ref, hat1_ref, rstd1_ref, wback_ref, slope_ref, win_ref, wout_ref, ctx_ref, nlow_ref, dhidden_ref, block, got, sent):
    rows, width = low_ref.shape
    ff = slope_ref.shape[1]
    tiles = ff // width
    loads = [(low_hbm, low_ref)]
    for t in range(tiles):
        part = slice(t * width, (t + 1) * width)
        loads += [(wback_hbm.at[0, part], wback_ref.at[part]), (slope_hbm.at[:, part], slope_ref.at[:, part])]
    loads.insert(3, (hat1_hbm, hat1_ref))
    loads += [(win_hbm.at[0], win_ref), (rstd1_hbm, rstd1_ref), (wout_hbm.at[0], wout_ref), (ctx_hbm, ctx_ref)]
    loads = stream_in(loads, got)
    place = Halves(keep_hbm, send_hbm, block, sent)
    gain, shift = gain_ref[0:1, :width], shift_ref[0:1, :width]
    hat1_load = loads.pop(3)
    loads[0].wait()
    for t in range(tiles):
        part = slice(t * width, (t + 1) * width)
        loads[1 + 2 * t].wait()
        loads[2 + 2 * t].wait()
        dhidden = (mm_nt(low_ref[...], wback_ref[part]) * slope_ref[:, part].astype(F32)).astype(BF)
        dhidden_ref[:, part] = dhidden
        if t == 0:
            hat1_load.wait()
            nlow_ref[...] = (hat1_ref[...].astype(F32) * gain + shift).astype(BF)
        sumin_ref[:, part] = rowsum(dhidden)
        place.put(t * width, mm_tn(nlow_ref[...], dhidden).astype(BF))
    for load in loads[1 + 2 * tiles :]:
        load.wait()
    sums_ref[...] = jnp.zeros_like(sums_ref)
    for r in range(0, rows, STEP):
        r = slice(r, r + STEP)
        dnormed = low_ref[r].astype(F32) + mm_nt(dhidden_ref[r], win_ref[...])
        hat1 = hat1_ref[r].astype(F32)
        datt = ln_back(dnormed, hat1, rstd1_ref[r, 0:1], gain)
        low = datt.astype(BF)
        datt_ref[r] = low
        dctx_ref[r] = mm_nt(low, wout_ref[...]).astype(BF)
        sums_ref[0:1] += rowsum(datt)
        sums_ref[1:2] += rowsum(dnormed * hat1)
        sums_ref[2:3] += rowsum(dnormed)
    place.put(ff, mm_tn(ctx_ref[...], datt_ref[...]).astype(BF))
    place.finish()


def ff_back(low, hat1, rstd1, slope, ctx, w):
    rows, width = low.shape
    ff = slope.shape[1]
    ins = [(w["gain"], whole(w["gain"])), (w["shift"], whole(w["shift"]))]
    ins += [(a, ANY) for a in (low, hat1, rstd1, w["back"], slope, w["in"], w["out"], ctx)]
    half = (ff + width) // 2
    outs = [(shape((half, width), BF), ANY)] * 2
    outs += [(s, whole(s)) for s in (shape((rows, width), BF), shape((rows, width), BF), shape((8, width), F32), shape((1, ff), F32))]
    scratch = [((rows, width), BF), ((rows, width), BF), ((rows, 128), F32), ((ff, width), BF), ((rows, ff), BF), ((width, ff), BF), ((width, width), BF), ((rows, width), BF)]
    scratch += [((rows, width), BF), ((rows, ff), BF), ((ff + width, width), BF)]
    scratch = [pltpu.VMEM(d, t) for d, t in scratch]
    scratch += [pltpu.SemaphoreType.DMA((6 + 2 * (ff // width),)), pltpu.SemaphoreType.DMA((8,))]
    return kernel_call(ff_back_body, "layer0_ff_back", (1,), ins, outs, 2 * rows * width * (3 * ff + 2 * width), scratch)


def attention_back_body(qkv_ref, prob_ref, dctx_ref, short_ref, long_ref, sums1_ref, sums2_ref, sumin_ref, dqkv_ref, keep_hbm, send_hbm, acc, sums, block, sent):
    step = pl.program_id(0)
    x = jnp.where(step == 0, short_ref[...], long_ref[...])
    rows, width = x.shape
    pair = 2 * width // HEADS
    first = first_head(width)
    scale = 1.0 / math.sqrt(width // HEADS)

    @pl.when(step == 0)
    def _():
        acc[...] = jnp.zeros_like(acc)
        sums[...] = jnp.zeros_like(sums)

    pairs = range(HEADS // 2)
    c = [[slice(m * width + p * pair, m * width + (p + 1) * pair) for m in range(3)] for p in pairs]
    for b in range(rows // BLOCK):
        r = slice(b * BLOCK, (b + 1) * BLOCK)
        dd = [halves(dctx_ref[r, c[p][0]], first) for p in pairs]
        dprob = [mm_nt(qkv_ref[r, c[p][2]], dd[p]) for p in pairs]
        dscore = []
        for p in pairs:
            prob = prob_ref[b, p].astype(F32)
            dscore.append((prob * (dprob[p] - jnp.sum(prob * dprob[p], 0, keepdims=True)) * scale).astype(BF))
        dv = [mm(prob_ref[b, p], dd[p]).astype(BF) for p in pairs]
        dk = [mm(dscore[p], halves(qkv_ref[r, c[p][0]], first)).astype(BF) for p in pairs]
        dq = [join_halves(mm_tn(dscore[p], qkv_ref[r, c[p][1]]), first).astype(BF) for p in pairs]
        dqkv_ref[r] = jnp.concatenate(dq + dk + dv, 1)
    dqkv = dqkv_ref[...]
    acc[...] += mm_tn(x, dqkv)
    sums[0:1] += rowsum(dqkv)

    @pl.when(step == pl.num_programs(0) - 1)
    def _():
        place = Halves(keep_hbm, send_hbm, block, sent)
        for m in range(3):
            place.put(m * width, acc[:, m * width : (m + 1) * width].astype(BF))
        rows_of = [sums[0:1, :width], sums[0:1, 2 * width :]]
        for k in range(3):
            rows_of += [sums1_ref[k : k + 1], sums2_ref[k : k + 1]]
        rows_of += [sumin_ref[:, k * width : (k + 1) * width] for k in range(sumin_ref.shape[1] // width)]
        rows_of += [sums2_ref[3:4], jnp.zeros((3, width), F32)]
        rows_of += [jnp.zeros((VECTOR_ROWS - 16, width), F32)]
        place.put(3 * width, jnp.concatenate(rows_of, 0).astype(BF))
        place.finish()


def attention_back(qkv, prob, dctx, sums1, sums2, sumin, short, long):
    rows, width = dctx.shape
    per = STEP // BLOCK
    ins = [(qkv, by_rows(3 * width)), (prob, pl.BlockSpec((per,) + prob.shape[1:], lambda i: (i, 0, 0, 0))), (dctx, by_rows(width))]
    ins += from_buckets(short, long) + [(a, whole(a)) for a in (sums1, sums2, sumin)]
    total = 3 * width + VECTOR_ROWS
    outs = [(hbm_shape((rows, 3 * width), BF), by_rows(3 * width))] + [(shape((total // 2, width), BF), ANY)] * 2
    scratch = [pltpu.VMEM((width, 3 * width), F32), pltpu.VMEM((8, 3 * width), F32), pltpu.VMEM((total, width), BF), pltpu.SemaphoreType.DMA((8,))]
    flops = 2 * rows * width * (3 * width + 10 * BLOCK)
    return kernel_call(attention_back_body, "layer0_attention_back", (rows // STEP,), ins, outs, flops, scratch)


def input_back_body(dqkv_ref, datt_ref, wqkv_ref, short_ref, long_ref):
    dx = datt_ref[...].astype(F32) + mm_nt(dqkv_ref[...], wqkv_ref[...])

    @pl.when(pl.program_id(0) == 0)
    def _():
        short_ref[...] = dx

    @pl.when(pl.program_id(0) > 0)
    def _():
        long_ref[...] = dx


def input_back(dqkv, datt, w, cut):
    rows, width = datt.shape
    ins = [(dqkv, by_rows(3 * width)), (datt, by_rows(width)), layer_of(w["qkv"], 0)]
    outs = [
        (shape((cut, width), F32), pl.BlockSpec((STEP, width), lambda i: (0, 0))),
        (shape((rows - cut, width), F32), pl.BlockSpec((STEP, width), lambda i: (jnp.maximum(i - 1, 0), 0))),
    ]
    return kernel_call(input_back_body, "layer0_input_back", (rows // STEP,), ins, outs, 2 * rows * width * 3 * width)


def unpack_call(body, name, bit, grid, ins, outs, aliases, size):
    return pl.pallas_call(
        body,
        grid_spec=pltpu.PrefetchScalarGridSpec(
            num_scalar_prefetch=1,
            grid=grid,
            in_specs=[s for _, s in ins],
            out_specs=[s for _, s in outs],
        ),
        out_shape=[s for s, _ in outs],
        input_output_aliases=aliases,
        compiler_params=pltpu.CompilerParams(vmem_limit_bytes=VMEM),
        cost_estimate=pl.CostEstimate(flops=0, bytes_accessed=size, transcendentals=0),
        name=name,
    )(bit, *[hbm(a) if s is ANY else a for a, s in ins])


def in_order(bit_ref, mine_ref, theirs_ref):
    mine, theirs = mine_ref[...].astype(F32), theirs_ref[...].astype(F32)
    low = bit_ref[0] == 0
    return jnp.where(low, mine, theirs), jnp.where(low, theirs, mine)


def unpack_first(bit, pair, back):
    _, ff, width = back.shape
    steps = ff // width
    block = pl.BlockSpec((width, width), lambda j, bit: (j, 0))

    def body(bit_ref, mine_ref, theirs_ref, _, qkv_ref, out_ref, back_ref):
        low, high = in_order(bit_ref, mine_ref, theirs_ref)
        back_ref[...] = low
        step = pl.program_id(0)

        @pl.when(step < steps - 1)
        def _():
            qkv_ref[...] = high

        @pl.when(step == steps - 1)
        def _():
            out_ref[...] = high

    outs = [
        (shape((2, width, 3 * width), F32), pl.BlockSpec((None, width, width), lambda j, bit: (1, 0, jnp.minimum(j, 2)))),
        (shape((2, width, width), F32), pl.BlockSpec((None, width, width), lambda j, bit: (1, 0, 0))),
        (shape(back.shape, F32), pl.BlockSpec((None, width, width), lambda j, bit: (0, j, 0))),
    ]
    ins = [(pair[0], block), (pair[1], block), (back, ANY)]
    return unpack_call(body, "unpack_first", bit, (steps,), ins, outs, {3: 2}, 12 * steps * width * width)


def unpack_second(bit, pair, gin, gout):
    _, width, ff = gin.shape
    rows = width // 2
    half = pair[0].shape[0] // rows
    count = 2 * ff // width
    block = [pl.BlockSpec((rows, width), lambda j, bit, low=low: (jnp.where((bit[0] == 0) == low, jnp.minimum(j, half - 1), jnp.maximum(j - half, 0)), 0)) for low in (True, False)]

    def body(bit_ref, mine_ref, theirs_ref, _, __, in_ref, out_ref):
        step = pl.program_id(0)
        mine = (step < half) == (bit_ref[0] == 0)
        value = jnp.where(mine, mine_ref[...], theirs_ref[...]).astype(F32)

        @pl.when(step < count)
        def _():
            in_ref[...] = value

        @pl.when(step >= count)
        def _():
            out_ref[...] = value

    def at_in(j, bit):
        j = jnp.minimum(j, count - 1)
        return 0, j % 2, j // 2

    outs = [
        (shape(gin.shape, F32), pl.BlockSpec((None, rows, width), at_in)),
        (shape(gout.shape, F32), pl.BlockSpec((None, rows, width), lambda j, bit: (0, jnp.maximum(j - count, 0), 0))),
    ]
    ins = [(pair[0], block[0]), (pair[1], block[1]), (gin, ANY), (gout, ANY)]
    return unpack_call(body, "unpack_second", bit, (2 * half,), ins, outs, {3: 0, 4: 1}, 12 * half * rows * width)


def unpack_third(bit, pair, qkv, sums, sumin):
    _, width, _ = qkv.shape
    ff = sumin.shape[1]
    total = 3 * width + VECTOR_ROWS

    def fixed(a):
        return pl.BlockSpec(a.shape, lambda j, bit: (0,) * len(a.shape))

    def body(bit_ref, mine_ref, theirs_ref, _, sums_ref, sumin_ref, qkv_ref, bqv_ref, bresid_ref, gain_ref, shift_ref, bin_ref):
        low, high = in_order(bit_ref, mine_ref, theirs_ref)
        value = jnp.concatenate([low, high], 0)
        for m in range(3):
            qkv_ref[:, m * width : (m + 1) * width] = value[m * width : (m + 1) * width]
        value = value[3 * width :]
        for ref, lower, upper in (
            (bqv_ref, (value[0:1], value[1:2]), (value[12:13], sums_ref[6:7])),
            (bresid_ref, (value[2:3], value[3:4]), (sums_ref[0:1], sums_ref[1:2])),
            (gain_ref, (value[4:5], value[5:6]), (sums_ref[2:3], sums_ref[3:4])),
            (shift_ref, (value[6:7], value[7:8]), (sums_ref[4:5], sums_ref[5:6])),
        ):
            for level, both in enumerate((lower, upper)):
                for k in range(2):
                    ref[level : level + 1, k * width : (k + 1) * width] = both[k]
        for k in range(ff // width):
            bin_ref[0:1, k * width : (k + 1) * width] = value[8 + k : 9 + k]
        bin_ref[1:2, :] = sumin_ref[...]

    outs = [(shape(qkv.shape, F32), pl.BlockSpec((None, width, 3 * width), lambda j, bit: (0, 0, 0)))]
    outs += [(s, fixed(s)) for s in [shape((2, 2 * width), F32)] * 4 + [shape((2, ff), F32)]]
    ins = [(pair[0], fixed(pair[0])), (pair[1], fixed(pair[1])), (qkv, ANY), (sums, fixed(sums)), (sumin, fixed(sumin))]
    return unpack_call(body, "unpack_third", bit, (1,), ins, outs, {3: 0}, 6 * total * width)


def top_rows(attended, pair_index, weights):
    w_qkv, b_qv, w_out, b_resid, gain, shift, w_in, b_in, w_back = weights
    rows, width = attended.shape
    pairs = rows // 2
    hat1, rstd1 = ln_stats(attended.astype(F32))
    normed = hat1 * gain[:width] + shift[:width]
    normed_low = normed.astype(BF)
    activ, slope = gelu_pair(mm(normed_low, w_in) + b_in)
    activ = activ.astype(BF)
    hat2, rstd2 = ln_stats(normed + mm(activ, w_back) + b_resid[width:])
    pooled = hat2 * gain[width:] + shift[width:]
    radius = lax.rsqrt(jnp.sum(pooled * pooled, -1, keepdims=True) + unit_eps)
    unit = pooled * radius
    unit_low = unit.astype(BF)
    src, tgt = unit_low[:pairs], unit_low[pairs:]
    positive = (pair_index[:, None] == jnp.arange(pairs)[None, :]).astype(F32)
    logits = logit_scale * (mm_nt(src, tgt) - margin * positive)

    def soft(axis):
        powers = jnp.exp(logits - jnp.max(logits, axis, keepdims=True))
        return powers / jnp.sum(powers, axis, keepdims=True)

    dscore = (0.5 * logit_scale * (soft(1) + soft(0) - 2.0 * positive)).astype(BF)
    dunit = jnp.concatenate([mm(dscore, tgt), mm_tn(dscore, src)], 0)
    dy = radius * (dunit - unit * jnp.sum(dunit * unit, -1, keepdims=True))
    dg2, dc2 = colsum(dy * hat2), colsum(dy)
    dmixed = ln_back(dy, hat2, rstd2, gain[width:])
    dmixed_low = dmixed.astype(BF)
    dhidden = (mm_nt(dmixed_low, w_back) * slope).astype(BF)
    dnormed = dmixed + mm_nt(dhidden, w_in)
    dg1, dc1 = colsum(dnormed * hat1), colsum(dnormed)
    datt = ln_back(dnormed, hat1, rstd1, gain[:width])
    datt_low = datt.astype(BF)
    dctx = mm_nt(datt_low, w_out).astype(BF)
    grads = (mm_tn(normed_low, dhidden), mm_tn(activ, dmixed_low))
    vectors = dict(
        bv=colsum(dctx),
        b_resid=jnp.concatenate([colsum(datt), colsum(dmixed)]),
        gain=jnp.concatenate([dg1, dg2]),
        shift=jnp.concatenate([dc1, dc2]),
        b_in=colsum(dhidden),
    )
    return datt, dctx, grads, vectors


def per_device(short_tokens, long_tokens, short_len, long_len, pair_index, *params):
    n = lax.axis_size("stream") * lax.axis_size("dp")
    index = lax.axis_index("stream") * lax.axis_size("dp") + lax.axis_index("dp")
    width = short_tokens.shape[-1]
    spans = (short_tokens.shape[2], long_tokens.shape[2])
    counts = (short_tokens.shape[1], long_tokens.shape[1])
    sents = sum(counts)
    w_qkv, b_qv, w_out, b_resid, gain, shift, w_in, b_in, w_back = params
    w_qkv, b_qv, w_out, b_resid, gain, shift, w_in, b_in, w_back = (hbm(p) for p in (w_qkv, b_qv, w_out, b_resid, gain, shift, w_in, b_in, w_back))
    w = dict(qkv=w_qkv, b_qv=b_qv, out=w_out, b_resid=b_resid, gain=gain, shift=shift, b_in=b_in, back=w_back) | {"in": w_in}
    short, long = hbm(short_tokens.reshape(-1, width)), hbm(long_tokens.reshape(-1, width))
    lens = jnp.concatenate([short_len.reshape(-1), long_len.reshape(-1)])
    lens_wide = jnp.repeat(lens, HEADS)[:, None]

    outs = forward(short, long, lens, lens_wide, w, spans, counts[0], sents)
    y, qkv, prob, ctx, hat1, rstd1, act, slope, hat2, rstd2 = (hbm(a) for a in outs[:10])
    sent, *kept = outs[10:]
    one_kernel = n * sents <= 512
    if one_kernel:
        top_args = (index.reshape(1).astype(jnp.int32), *gather_near(sent, n), pair_index[None, :])
    else:
        datt, dctx, top_g, top_vec = top_rows(gather_rows(sent, n), pair_index, tuple(p[1] for p in params))
        top_args = tuple(lax.dynamic_slice_in_dim(v, index * sents, sents, 0) for v in (datt, dctx))
    bits = my_bits(n)
    bit = bits[0].reshape(1).astype(jnp.int32)

    keep, send, dlow, sums2, *top_kept = turn(top_args, y, [hbm(a) for a in kept], w, hat2, rstd2, act, spans, sents)
    lanes = {"1": Lane(sum_steps(keep, send, n, bits), n)}
    v = {}

    def ff():
        return (dlow, hat1, rstd1, slope, ctx), lambda *a: ff_back(*a, w)

    def attention():
        return (qkv, prob, v["dctx"], v["sums1"], sums2, v["sumin"]), lambda *a: attention_back(*a, short, long)

    def input_():
        return (hbm(v["dqkv"]), v["datt"]), lambda *a: input_back(*a, w, counts[0] * spans[0])

    def top():
        if one_kernel:
            return [hbm(a) for a in top_kept], lambda *a: top_grads(*a, w)
        return (), None

    def unpack1():
        return (lanes["1"].result, v["gback"]), lambda *a: unpack_first(bit, *a)

    def unpack2():
        return (lanes["2"].result, v["gin"], v["gout"]), lambda *a: unpack_second(bit, *a)

    work = dict(ff=ff, attention=attention, input=input_, top=top, unpack1=unpack1, unpack2=unpack2)
    gives = dict(
        ff=("keep", "send", "datt", "dctx", "sums1", "sumin"), attention=("dqkv", "keep", "send"), input=("dshort", "dlong"),
        top=("gin", "gback", "top_sums", "top_sumin"), unpack1=("gqkv", "gout", "gback"), unpack2=("gin", "gout"),
    )
    if not one_kernel:
        v["gin"], v["gback"] = (jnp.stack([g, g]) for g in top_g)
        rows_of = [top_vec[k].reshape(2, width) for k in ("b_resid", "gain", "shift")]
        v["top_sums"] = jnp.concatenate(rows_of + [top_vec["bv"][None], jnp.zeros((1, width), F32)], 0)
        v["top_sumin"] = top_vec["b_in"][None]
    for moved, piece in SCHEDULE:
        if piece[:6] == "unpack":
            while lanes[piece[6:]].result is None:
                stage(lanes.values())
        args, body = work[piece]() if piece else ((), None)
        v.update(zip(gives.get(piece, ()), stage([lanes[k] for k in moved], body, args)))
        if piece in ("ff", "attention"):
            lanes["2" if piece == "ff" else "3"] = Lane(sum_steps(v["keep"], v["send"], n, bits), n)
    while lanes["3"].result is None:
        stage(lanes.values())
    g_qkv, g_bqv, g_bresid, g_gain, g_shift, g_bin = unpack_third(bit, lanes["3"].result, v["gqkv"], v["top_sums"], v["top_sumin"])
    g_out, g_in, g_back, dshort, dlong = (v[k] for k in ("gout", "gin", "gback", "dshort", "dlong"))
    outs = (g_qkv, g_bqv, g_out, g_bresid, g_gain, g_shift, g_in, g_bin, g_back)
    return outs + (dshort.reshape((1, counts[0], spans[0], width)), dlong.reshape((1, counts[1], spans[1], width)))


def solution(mesh):
    split = P("stream", "dp", None, None)
    in_specs = (split, split, P("stream", "dp"), P("stream", "dp")) + (P(),) * 10
    out_specs = (P(),) * 9 + (split, split)
    return jax.shard_map(per_device, mesh=mesh, in_specs=in_specs, out_specs=out_specs, check_vma=False)
```

```python
import functools
import math

import jax
import jax.numpy as jnp
from jax import lax
from jax.experimental import pallas as pl
from jax.experimental.pallas import tpu as pltpu
from jax.sharding import PartitionSpec as P

HEADS = 8
BF = jnp.bfloat16
F32 = jnp.float32
AXES = ("stream", "dp")
logit_scale = 40.0
margin = 0.3
norm_eps = 1e-12
unit_eps = 1e-06
BLOCK = 128
STEP = 256
VMEM = 30 * 1024 * 1024
SCHEDULE = (
    ("1", ""), ("1", "ff"), ("12", ""), ("12", "attention"), ("3", ""), ("123", "input"), ("123", ""),
    ("12", "top"), ("123", ""), ("23", "unpack1"), ("23", ""), ("3", "unpack2"), ("3", "unpack3"),
)


def mm(a, b):
    return jnp.dot(a, b, preferred_element_type=F32)


def mm_nt(a, b):
    return lax.dot_general(a, b, (((1,), (1,)), ((), ())), preferred_element_type=F32)


def mm_tn(a, b):
    return lax.dot_general(a, b, (((0,), (0,)), ((), ())), preferred_element_type=F32)


def ln_stats(v):
    centre = v - jnp.mean(v, -1, keepdims=True)
    rstd = lax.rsqrt(jnp.mean(centre * centre, -1, keepdims=True) + norm_eps)
    return centre * rstd, rstd


def ln_back(dy, vhat, rstd, gain):
    dhat = dy * gain
    return (dhat - jnp.mean(dhat, -1, keepdims=True) - vhat * jnp.mean(dhat * vhat, -1, keepdims=True)) * rstd


def gelu_pair(v):
    cdf = 0.5 * (1.0 + lax.erf(v * (1.0 / math.sqrt(2.0))))
    pdf = jnp.exp(-0.5 * v * v) * (1.0 / math.sqrt(2.0 * math.pi))
    return v * cdf, cdf + v * pdf


def colsum(v):
    return jnp.sum(v.astype(F32), 0)


def rowsum(v):
    return jnp.sum(v.astype(F32), 0, keepdims=True)


SMEM = pl.BlockSpec(memory_space=pltpu.SMEM)
ANY = pl.BlockSpec(memory_space=pl.ANY)
AS_IS = pl.BlockSpec(memory_space=pl.ANY)


def hbm(a):
    return pltpu.with_memory_space_constraint(a, memory_space=pltpu.HBM)


def hbm_shape(dims, dtype):
    return pltpu.HBM(dims, dtype)


def whole(a):
    return pl.BlockSpec(a.shape, lambda i: (0,) * len(a.shape))


def shape(dims, dtype):
    return jax.ShapeDtypeStruct(dims, dtype)


def layer_of(a, level, rows=None, cols=None, at=lambda i: (0, 0)):
    rows, cols = rows or a.shape[1], cols or a.shape[2]
    return a, pl.BlockSpec((None, rows, cols), lambda i: (level, *at(i)))


def kernel_call(body, name, grid, ins, outs, flops, scratch=(), aliases=None, vmem=VMEM):
    size = sum(a.size * a.dtype.itemsize for a, _ in ins) + sum(
        math.prod(s.shape) * jnp.dtype(s.dtype).itemsize for s, _ in outs
    )
    return pl.pallas_call(
        body,
        grid=grid,
        in_specs=[s for _, s in ins],
        out_specs=[s for _, s in outs],
        out_shape=[s for s, _ in outs],
        scratch_shapes=list(scratch),
        input_output_aliases=aliases or {},
        compiler_params=pltpu.CompilerParams(vmem_limit_bytes=vmem),
        cost_estimate=pl.CostEstimate(flops=int(flops), bytes_accessed=int(size), transcendentals=0),
        name=name,
    )(*[hbm(a) if s is ANY else a for a, s in ins])


def routes(n):
    top, y = n >> 1, 2
    rest = [1 << k for k in range(2, n.bit_length() - 2)]
    for k in range(1, len(rest)):
        rest[k] |= rest[k - 1]
    halved = [(1, 1), (top, y), (y, top)]
    added = list(zip(rest, rest[::-1]))
    return halved, added


def swap(value, n, hop):
    return lax.ppermute(value, AXES, [(i, i ^ (hop[1] if i & 1 else hop[0])) for i in range(n)])


def device_index():
    return lax.axis_index("stream") * lax.axis_size("dp") + lax.axis_index("dp")


def coordinate(index, hop, n):
    value = (index // (1 << (hop.bit_length() - 1))) % 2
    if hop in (1, 2, n >> 1) or 2 * hop >= n >> 1:
        return value
    above = (index // (1 << hop.bit_length())) % 2
    return value + above - 2 * value * above


def my_bits(n):
    index = device_index()
    core = index % 2
    halved, _ = routes(n)
    return [jnp.where(core == 0, coordinate(index, a, n), coordinate(index, b, n)) for a, b in halved]


def split_body(bit_ref, mine_a, got_a, mine_b, got_b, keep_ref, send_ref):
    keep_ref[...] = (mine_a[...].astype(F32) + got_a[...].astype(F32)).astype(BF)
    send_ref[...] = (mine_b[...].astype(F32) + got_b[...].astype(F32)).astype(BF)


def add_and_split(mine, got, bit):
    rows, width = mine.shape[0] // 2, mine.shape[1]
    steps = 2 if rows % 32 == 0 and rows >= 256 else 1
    block = rows // steps
    kept = pl.BlockSpec((block, width), lambda j, bit: (bit[0] * steps + j, 0))
    sent = pl.BlockSpec((block, width), lambda j, bit: ((1 - bit[0]) * steps + j, 0))
    out = pl.BlockSpec((block, width), lambda j, bit: (j, 0))
    ins = [(mine, kept), (got, kept), (mine, sent), (got, sent)]
    outs = [(shape((rows, width), BF), out)] * 2
    return unpack_call(split_body, "add_and_split", bit.reshape(1).astype(jnp.int32), (steps,), ins, outs, {}, 12 * rows * width)


def sum_steps(keep, send, n, bits):
    halved, added = routes(n)
    for k, hop in enumerate(halved[:-1]):
        got = yield send, hop
        keep, send = add_and_split(keep, got, bits[k + 1])
    got = yield send, halved[-1]
    cur = (keep.astype(F32) + got.astype(F32)).astype(BF)
    for hop in added:
        got = yield cur, hop
        cur = (cur.astype(F32) + got.astype(F32)).astype(BF)
    for hop, bit in reversed(list(zip(halved, bits))[1:]):
        got = yield cur, hop
        low = jnp.where(bit == 0, cur, got)
        high = jnp.where(bit == 0, got, cur)
        cur = jnp.concatenate([low, high], 0)
    got = yield cur, halved[0]
    return cur, got


class Lane:
    def __init__(self, steps, n):
        halved, added = routes(n)
        self.n, self.steps, self.result, self.left = n, steps, None, 2 * len(halved) + len(added)
        self.ask = next(self.steps)

    def feed(self, got):
        self.left -= 1
        try:
            self.ask = self.steps.send(got)
        except StopIteration as end:
            self.result = end.value


def stage(lanes, work=None, args=()):
    lanes = [lane for lane in lanes if lane.result is None]
    asked, args = lax.optimization_barrier(([lane.ask[0] for lane in lanes], args))
    got = [swap(value, lane.n, lane.ask[1]) for value, lane in zip(asked, lanes)]
    out = work(*args) if work else ()
    got, out = lax.optimization_barrier((got, out))
    for lane, value in zip(lanes, got):
        lane.feed(value)
    return out


def gather_rows(rows, n):
    index = device_index()
    cur = rows[None]
    for flip in [1 << k for k in range(1, n.bit_length() - 1)] + [1]:
        got = swap(cur, n, (flip, flip))
        bit = (index // flip) % 2
        low, high = jnp.where(bit == 0, cur, got), jnp.where(bit == 0, got, cur)
        cur = jnp.stack([low, high], 1 if flip == 1 else 0).reshape((2 * cur.shape[0],) + rows.shape)
    return cur.reshape(n * rows.shape[0], rows.shape[1])


def hop_groups(n):
    hops = [1 << k for k in range(1, n.bit_length() - 1)]
    half = (len(hops) + 1) // 2
    hops = [hops[0], hops[-1]] + hops[1:-1] if len(hops) > 2 else hops
    groups = [hops[k : k + 2] for k in range(0, 2 * half, 2)]
    return [[a, b, a | b] if len(g) == 2 else g for g in groups for a, b in [(g[0], g[-1])]]


def gather_near(rows, n):
    cur = rows
    for group in hop_groups(n):
        cur = jnp.concatenate([cur] + [swap(cur, n, (hop, hop)) for hop in group], 0)
    return cur, swap(cur, n, (1, 1))


def near_offsets(n):
    offsets = [0]
    for group in hop_groups(n):
        offsets = offsets + [hop ^ o for hop in group for o in offsets]
    return offsets


def stream_in(pairs, sems):
    loads = [pltpu.make_async_copy(a, b, sems.at[k]) for k, (a, b) in enumerate(pairs)]
    for load in loads:
        load.start()
    return loads


class Halves:
    def __init__(self, keep, send, block, sems):
        self.keep, self.send, self.block, self.sems = keep, send, block, sems
        self.low_is_kept = lax.axis_index("dp") % 2 == 0
        self.pieces = 0
        self.waits = []

    def put(self, at, value):
        self.block[at : at + value.shape[0]] = value
        half = self.keep.shape[0]
        end = at + value.shape[0]
        for lower, a, b in ((True, at, min(end, half)), (False, max(at, half), end)):
            if a >= b:
                continue
            base = 0 if lower else half
            sem = self.sems.at[self.pieces]
            self.pieces += 1
            copies = [
                pltpu.make_async_copy(self.block.at[a:b], ref.at[a - base : b - base], sem) for ref in (self.keep, self.send)
            ]
            kept = self.low_is_kept if lower else jnp.logical_not(self.low_is_kept)

            @pl.when(kept)
            def _(copy=copies[0]):
                copy.start()

            @pl.when(jnp.logical_not(kept))
            def _(copy=copies[1]):
                copy.start()

            self.waits.append(copies[0])

    def finish(self):
        for copy in self.waits:
            copy.wait()


def starts(sents, spans, rows):
    s = lax.broadcasted_iota(jnp.int32, (sents, rows), 0)
    r = lax.broadcasted_iota(jnp.int32, (sents, rows), 1)
    half = sents // 2
    at = jnp.where(s < half, s * spans[0], half * spans[0] + (s - half) * spans[1])
    return (r == at).astype(BF)


def spread(sents):
    a = lax.broadcasted_iota(jnp.int32, (sents * HEADS, sents), 0) // HEADS
    return (a == lax.broadcasted_iota(jnp.int32, (sents * HEADS, sents), 1)).astype(BF)


def own_head(sents, width):
    a = lax.broadcasted_iota(jnp.int32, (sents * HEADS, width), 0) % HEADS
    return a == lax.broadcasted_iota(jnp.int32, (sents * HEADS, width), 1) // (width // HEADS)


def sum_heads(v, keep, sents):
    return jnp.sum(jnp.where(keep, v, 0.0).reshape(sents, HEADS, v.shape[1]), 1)


def ask(y, spans, lens, wqkv_ref, wout_ref, bq, bv, bo, sents):
    rows, width = y.shape
    keep = own_head(sents, width)
    cls = mm(starts(sents, spans, rows), y).astype(BF)
    q = (mm(cls, wqkv_ref[:, :width]) + bq).astype(BF)
    wide = jnp.where(keep, mm(spread(sents), q), 0.0).astype(BF)
    key = mm_nt(wide, wqkv_ref[:, width : 2 * width]).astype(BF)
    half = sents // 2
    sent = lax.broadcasted_iota(jnp.int32, (sents * HEADS, 1), 0) // HEADS
    begin = jnp.where(sent < half, sent * spans[0], half * spans[0] + (sent - half) * spans[1])
    place = lax.broadcasted_iota(jnp.int32, (sents * HEADS, rows), 1) - begin
    seen = (place >= 0) & (place < lens)
    logit = jnp.where(seen, mm_nt(key, y) * (1.0 / math.sqrt(width // HEADS)), -jnp.inf)
    power = jnp.exp(logit - jnp.max(logit, 1, keepdims=True))
    prob = (power * (1.0 / jnp.sum(power, 1, keepdims=True))).astype(BF)
    mixed = mm(prob, y).astype(BF)
    ctx = (sum_heads(mm(mixed, wqkv_ref[:, 2 * width :]), keep, sents) + bv).astype(BF)
    attended = (cls.astype(F32) + mm(ctx, wout_ref[...]) + bo).astype(BF)
    return attended, ctx, wide, key, prob, mixed


def halves(v, first):
    zero = jnp.zeros_like(v)
    return jnp.concatenate([jnp.where(first, v, zero), jnp.where(first, zero, v)], 0)


def join_halves(v, first):
    return jnp.where(first, v[: v.shape[0] // 2], v[v.shape[0] // 2 :])


def first_head(width):
    return lax.broadcasted_iota(jnp.int32, (1, 2 * width // HEADS), 1) < width // HEADS


def key_bias(lens_ref, block, span_short, count_short):
    key = lax.broadcasted_iota(jnp.int32, (BLOCK, 1), 0)
    query = lax.broadcasted_iota(jnp.int32, (1, BLOCK), 1)
    per = BLOCK // span_short
    blocks_short = count_short // per
    is_short = block < blocks_short
    at = jnp.where(is_short, block * per, count_short + block - blocks_short)
    limit = jnp.zeros((BLOCK, 1), jnp.int32)
    for s in range(per):
        inside = key // span_short == s
        limit = jnp.where(inside, jnp.where(is_short, lens_ref[at + jnp.where(is_short, s, 0)] + s * span_short, 0), limit)
    limit = jnp.where(is_short, limit, lens_ref[at])
    same = (key // span_short == query // span_short) | jnp.logical_not(is_short)
    return jnp.where((key < limit) & same, 0.0, -jnp.inf).astype(F32)


def vectors(level, width, bqv_ref, bresid_ref, gain_ref, shift_ref):
    row = slice(level, level + 1)
    low, high = slice(0, width), slice(width, 2 * width)
    return [ref[row, part] for ref in (bqv_ref, bresid_ref, gain_ref, shift_ref) for part in (low, high)]


def forward_body(
    spans, count, lens_ref, short_ref, long_ref, wqkv_ref, wout_ref, win_ref, wback_ref, bin_ref, bqv_ref, bresid_ref, gain_ref, shift_ref,
    wide_lens_ref, wqkv_hbm, wout_hbm,
    y_hbm, qkv_hbm, prob_hbm, ctx_hbm, hat1_hbm, rstd1_hbm, act_hbm, slope_hbm, hat2_hbm, rstd2_hbm,
    sent_ref, ctx1_ref, wide_ref, key_ref, prob1_ref, mixed_ref, y_s, wqkv1_ref, wout1_ref, got,
    y_2, qkv_2, prob_2, ctx_2, hat1_2, rstd1_2, act_2, slope_2, hat2_2, rstd2_2, left,
):
    step = pl.program_id(0)
    loads = [pltpu.make_async_copy(a.at[1], b, got.at[k]) for k, (a, b) in enumerate(((wqkv_hbm, wqkv1_ref), (wout_hbm, wout1_ref)))]

    @pl.when(step == 0)
    def _():
        for load in loads:
            load.start()

    far = (y_hbm, qkv_hbm, prob_hbm, ctx_hbm, hat1_hbm, rstd1_hbm, act_hbm, slope_hbm, hat2_hbm, rstd2_hbm)
    slots = (y_2, qkv_2, prob_2, ctx_2, hat1_2, rstd1_2, act_2, slope_2, hat2_2, rstd2_2)
    slot = step % 2

    def stores(slot, step):
        copies = []
        for k, (near, there) in enumerate(zip(slots, far)):
            size = near.shape[1]
            to = there.at[pl.ds(pl.multiple_of(step * size, size), size)]
            copies.append(pltpu.make_async_copy(near.at[slot], to, left.at[slot, k]))
        return copies

    @pl.when(step >= 2)
    def _():
        for store in stores(slot, 0):
            store.wait()

    y_ref, qkv_ref, prob_ref, ctx_ref, hat1_ref, rstd1_ref, act_ref, slope_ref, hat2_ref, rstd2_ref = (near.at[slot] for near in slots)
    x = jnp.where(step == 0, short_ref[...], long_ref[...])
    rows, width = x.shape
    bq, bv, bo, bb, g1, g2, c1, c2 = vectors(0, width, bqv_ref, bresid_ref, gain_ref, shift_ref)
    pair = 2 * width // HEADS
    first = first_head(width)
    scale = 1.0 / math.sqrt(width // HEADS)
    bias = jnp.concatenate([bq, jnp.zeros_like(bq), bv], 1)
    qkv = (mm(x, wqkv_ref[...]) + bias).astype(BF)
    qkv_ref[...] = qkv
    blocks = []
    for b in range(rows // BLOCK):
        r = slice(b * BLOCK, (b + 1) * BLOCK)
        hide = key_bias(lens_ref, step * (rows // BLOCK) + b, spans[0], count)
        hide = jnp.concatenate([hide, hide], 1)
        cols = []
        for p in range(HEADS // 2):
            q, k, v = (qkv[r, m * width + p * pair : m * width + (p + 1) * pair] for m in range(3))
            logit = mm_nt(k, halves(q, first)) * scale + hide
            power = jnp.exp(logit - jnp.max(logit, 0, keepdims=True))
            prob = (power * (1.0 / jnp.sum(power, 0, keepdims=True))).astype(BF)
            prob_ref[b, p] = prob
            cols.append(join_halves(mm_tn(prob, v), first))
        blocks.append(jnp.concatenate(cols, 1).astype(BF))
    ctx = jnp.concatenate(blocks, 0)
    ctx_ref[...] = ctx
    hat1, rstd1 = ln_stats(x.astype(F32) + mm(ctx, wout_ref[...]) + bo)
    normed = hat1 * g1 + c1
    low = normed.astype(BF)
    hat1_ref[...] = hat1.astype(BF)
    rstd1_ref[...] = jnp.broadcast_to(rstd1, rstd1_ref.shape)
    act, slope = gelu_pair(mm(low, win_ref[...]) + bin_ref[0:1])
    act = act.astype(BF)
    act_ref[...] = act
    slope_ref[...] = slope.astype(BF)
    hat2, rstd2 = ln_stats(normed + mm(act, wback_ref[...]) + bb)
    hat2_ref[...] = hat2.astype(BF)
    rstd2_ref[...] = jnp.broadcast_to(rstd2, rstd2_ref.shape)
    y = (hat2 * g2 + c2).astype(BF)
    y_ref[...] = y
    y_s[pl.ds(pl.multiple_of(step * rows, rows), rows)] = y
    for store in stores(slot, step):
        store.start()

    @pl.when(step == pl.num_programs(0) - 1)
    def _():
        for load in loads:
            load.wait()
        bq, bv, bo = vectors(1, width, bqv_ref, bresid_ref, gain_ref, shift_ref)[:3]
        outs = ask(y_s[...], spans, wide_lens_ref[...], wqkv1_ref, wout1_ref, bq, bv, bo, sent_ref.shape[0])
        for ref, value in zip((sent_ref, ctx1_ref, wide_ref, key_ref, prob1_ref, mixed_ref), outs):
            ref[...] = value
        for k in range(2):
            for store in stores(k, 0):
                store.wait()


def by_rows(cols):
    return pl.BlockSpec((STEP, cols), lambda i: (i, 0))


def from_buckets(short, long):
    width = short.shape[1]
    return [
        (short, pl.BlockSpec((STEP, width), lambda i: (0, 0))),
        (long, pl.BlockSpec((STEP, width), lambda i: (jnp.maximum(i - 1, 0), 0))),
    ]


def small_ins(w):
    return [(w[k], whole(w[k])) for k in ("b_qv", "b_resid", "gain", "shift")]


def forward(short, long, lens, wide_lens, w, spans, count, sents):
    rows, width = short.shape[0] + long.shape[0], short.shape[1]
    ff = w["in"].shape[2]
    per = STEP // BLOCK
    ins = [(lens, SMEM)] + from_buckets(short, long)
    ins += [layer_of(w[name], 0) for name in ("qkv", "out", "in", "back")] + [(w["b_in"], whole(w["b_in"]))] + small_ins(w)
    cols = [(width, BF), (3 * width, BF), None, (width, BF), (width, BF), (128, F32), (ff, BF), (ff, BF), (width, BF), (128, F32)]
    outs = [(hbm_shape((rows, c[0]), c[1]) if c else hbm_shape((rows // BLOCK, HEADS // 2, BLOCK, 2 * BLOCK), BF), ANY) for c in cols]
    slots = [pltpu.VMEM((2, STEP, c[0]), c[1]) if c else pltpu.VMEM((2, per, HEADS // 2, BLOCK, 2 * BLOCK), BF) for c in cols]
    ins += [(wide_lens, whole(wide_lens)), (w["qkv"], ANY), (w["out"], ANY)]
    wide = sents * HEADS
    outs += [(s, whole(s)) for s in [shape((sents, width), BF)] + [hbm_shape(d, BF) for d in ((sents, width), (wide, width), (wide, width), (wide, rows), (wide, width))]]
    scratch = [pltpu.VMEM(d, BF) for d in ((rows, width), (width, 3 * width), (width, width))] + [pltpu.SemaphoreType.DMA((2,))]
    scratch += slots + [pltpu.SemaphoreType.DMA((2, len(slots)))]
    body = functools.partial(forward_body, spans, count)
    return kernel_call(body, "layer0_forward", (rows // STEP,), ins, outs, 2 * rows * width * (4 * width + 2 * ff), scratch, vmem=VMEM + VMEM // 4)


def top_forward(attended, win_ref, bin_ref, g1, c1):
    hat1, rstd1 = ln_stats(attended.astype(F32))
    normed = hat1 * g1 + c1
    low = normed.astype(BF)
    return hat1, rstd1, normed, low, mm(low, win_ref[...]) + bin_ref[1:2]


def gelu(v):
    return v * (0.5 * (1.0 + lax.erf(v * (1.0 / math.sqrt(2.0)))))


def top_part(index_ref, every_ref, pair_ref, dy_ref, hat2_s, rstd2_s, low_vectors, bin_ref, win, wback, wout, sents):
    pairs = pair_ref.shape[1]
    _, _, _, bb, g1, g2, c1, c2 = low_vectors
    hat1, _ = ln_stats(every_ref[...].astype(F32))
    normed = hat1 * g1 + c1
    win_ref = win()
    act = gelu(mm(normed.astype(BF), win_ref[...]) + bin_ref[1:2]).astype(BF)
    wback_ref = wback()
    hat2, rstd2 = ln_stats(normed + mm(act, wback_ref[...]) + bb)
    hat2_s[...] = hat2
    rstd2_s[...] = jnp.broadcast_to(rstd2, rstd2_s.shape)
    pooled = hat2 * g2 + c2
    radius = lax.rsqrt(jnp.sum(pooled * pooled, -1, keepdims=True) + unit_eps)
    unit = pooled * radius
    src, tgt = unit[:pairs].astype(BF), unit[pairs:].astype(BF)
    positive = (pair_ref[...] == lax.broadcasted_iota(jnp.int32, (pairs, pairs), 0)).astype(F32)
    logits = logit_scale * (mm_nt(tgt, src) - margin * positive)

    def soft(axis):
        powers = jnp.exp(logits - jnp.max(logits, axis, keepdims=True))
        return powers * (1.0 / jnp.sum(powers, axis, keepdims=True))

    dscore = (0.5 * logit_scale * (soft(1) + soft(0) - 2.0 * positive)).astype(BF)
    dunit = jnp.concatenate([mm_tn(dscore, tgt), mm(dscore, src)], 0)
    dy_ref[...] = radius * (dunit - unit * jnp.sum(dunit * unit, -1, keepdims=True))
    mine = pl.ds(pl.multiple_of(index_ref[0] * sents, sents), sents)
    own_hat1, own_rstd1, _, _, own_hid = top_forward(every_ref[mine], win_ref, bin_ref, g1, c1)
    dmixed = ln_back(dy_ref[mine], hat2_s[mine], rstd2_s[mine, 0:1], g2)
    dhidden = (mm_nt(dmixed.astype(BF), wback_ref[...]) * gelu_pair(own_hid)[1]).astype(BF)
    dnormed = dmixed + mm_nt(dhidden, win_ref[...])
    datt = ln_back(dnormed, own_hat1, own_rstd1, g1)
    return datt, mm_nt(datt.astype(BF), wout()[...]).astype(BF)


def top_grads_body(every_ref, dy_ref, wout_ref, win_ref, wback_ref, bin_ref, bqv_ref, bresid_ref, gain_ref, shift_ref,
                   gin_ref, gback_ref, sums_ref, sumin_ref):
    width = dy_ref.shape[1]
    _, _, _, bb, g1, g2, c1, c2 = vectors(1, width, bqv_ref, bresid_ref, gain_ref, shift_ref)
    hat1, rstd1, normed, low, hid = top_forward(every_ref[...], win_ref, bin_ref, g1, c1)
    act, slope = gelu_pair(hid)
    act = act.astype(BF)
    hat2, rstd2 = ln_stats(normed + mm(act, wback_ref[...]) + bb)
    dy = dy_ref[...]
    dmixed = ln_back(dy, hat2, rstd2, g2)
    dmixed_low = dmixed.astype(BF)
    gback_ref[...] = mm_tn(act, dmixed_low)
    dhidden = (mm_nt(dmixed_low, wback_ref[...]) * slope).astype(BF)
    gin_ref[...] = mm_tn(low, dhidden)
    dnormed = dmixed + mm_nt(dhidden, win_ref[...])
    datt = ln_back(dnormed, hat1, rstd1, g1)
    sumin_ref[...] = rowsum(dhidden)
    parts = (datt, dmixed, dnormed * hat1, dy * hat2, dnormed, dy, mm_nt(datt.astype(BF), wout_ref[...]).astype(BF))
    for k, part in enumerate(parts):
        sums_ref[k : k + 1] = rowsum(part)
    sums_ref[7:8] = jnp.zeros((1, width), F32)


def top_grads(every, dy, w):
    width = dy.shape[1]
    ff = w["in"].shape[2]
    rows = every.shape[0]
    ins = [(every, whole(every)), (dy, whole(dy))] + [layer_of(w[k], 1) for k in ("out", "in", "back")]
    ins += [(w["b_in"], whole(w["b_in"]))] + small_ins(w)

    def upper(a, b):
        return hbm_shape((2, a, b), F32), pl.BlockSpec((None, a, b), lambda i: (1, 0, 0))

    sums, sumin = shape((8, width), F32), shape((1, ff), F32)
    outs = [upper(width, ff), upper(ff, width), (sums, whole(sums)), (sumin, whole(sumin))]
    return kernel_call(top_grads_body, "top_grads", (1,), ins, outs, 6 * rows * width * (width + 2 * ff))


def turn_body(spans, sents, with_top, *refs):
    refs = list(refs)

    def take(count):
        out, refs[:count] = refs[:count], []
        return out

    (gain_ref,) = take(1)
    late = take(10)
    if with_top:
        index_ref, near_ref, other_ref, pair_ref, wout_hbm, bin_ref, bqv_ref, bresid_ref, shift_ref, win_hbm, wback_hbm = take(11)
    else:
        datt_ref, dctx_ref = take(2)
    keep_hbm, send_hbm, low_hbm, sums_ref = take(4)
    if with_top:
        every_hbm, dy_hbm = take(2)
    here = take(10)
    wqkv_ref, y_ref, wide_ref, key_ref, prob_ref, mixed_ref, ctx_ref, hat2_ref, rstd2_ref, act_ref = here
    low_ref, block, got, sent, left_sem = take(5)
    loads = list(zip([late[0].at[1]] + late[1:], here))
    if with_top:
        win_ref, wback_ref, wout_ref, top_hat2, top_rstd2, every_ref, dy_ref, arrivals = take(8)
        offsets = near_offsets(2 * near_ref.shape[0] // sents)
        pieces = []
        for p, offset in enumerate(offsets):
            for core, ref in enumerate((near_ref, other_ref)):
                device = index_ref[0] ^ (offset + core)
                to = every_ref.at[pl.ds(pl.multiple_of(device * sents, sents), sents)]
                pieces.append(pltpu.make_async_copy(ref.at[p * sents : (p + 1) * sents], to, arrivals.at[2 * p + core]))
        for piece in pieces:
            piece.start()
        loads = [(win_hbm.at[1], win_ref), (wback_hbm.at[1], wback_ref), (wout_hbm.at[1], wout_ref)] + loads
    loads = [pltpu.make_async_copy(a, b, got.at[k]) for k, (a, b) in enumerate(loads)]
    for load in loads:
        load.start()
    rows, width = y_ref.shape
    if with_top:

        def arrived(load, ref):
            def wait():
                load.wait()
                return ref

            return wait

        values = vectors(1, width, bqv_ref, bresid_ref, gain_ref, shift_ref)
        for piece in pieces:
            piece.wait()
        win, wback, wout = (arrived(load, ref) for load, ref in zip(loads, (win_ref, wback_ref, wout_ref)))
        datt, dctx = top_part(index_ref, every_ref, pair_ref, dy_ref, top_hat2, top_rstd2, values, bin_ref, win, wback, wout, sents)
        loads = loads[3:]
        left = [(every_ref, every_hbm), (dy_ref, dy_hbm)]
    else:
        datt, dctx = datt_ref[...], dctx_ref[...]
        left = []
    keep = own_head(sents, width)
    first = starts(sents, spans, rows)
    d_wide = jnp.where(keep, mm(spread(sents), dctx), 0.0).astype(BF)
    for load in loads[:7]:
        load.wait()
    prob_low = prob_ref[...]
    d_value = mm_nt(d_wide, wqkv_ref[:, 2 * width :]).astype(BF)
    y = y_ref[...]
    dprob = mm_nt(d_value, y)
    prob = prob_low.astype(F32)
    dlogit = prob * (dprob - jnp.sum(prob * dprob, 1, keepdims=True))
    dscore = (dlogit * (1.0 / math.sqrt(width // HEADS))).astype(BF)
    pulled = mm(dscore, y).astype(BF)
    dq = sum_heads(mm(pulled, wqkv_ref[:, width : 2 * width]), keep, sents).astype(BF)
    dcls = mm_nt(dq, wqkv_ref[:, :width]) + datt
    high = dcls.astype(BF)
    from_left = jnp.concatenate([dscore, prob_low, first, first], 0)
    from_right = jnp.concatenate([key_ref[...], d_value, high, (dcls - high.astype(F32)).astype(BF)], 0)
    dy = mm_tn(from_left, from_right)
    loads[7].wait()
    loads[8].wait()
    hat2 = hat2_ref[...].astype(F32)
    dmixed = ln_back(dy, hat2, rstd2_ref[:, 0:1], gain_ref[0:1, width:])
    low_ref[...] = dmixed.astype(BF)
    left = stream_in([(low_ref, low_hbm)] + left, left_sem)
    sums_ref[0:1] = rowsum(dmixed)
    sums_ref[1:2] = rowsum(dy * hat2)
    sums_ref[2:3] = rowsum(dy)
    sums_ref[3:4] = rowsum(dq)
    sums_ref[4:8] = jnp.zeros((4, width), F32)
    place = Halves(keep_hbm, send_hbm, block, sent)
    ff = act_ref.shape[1]
    tiles = ff // width
    cls = mm(first, y).astype(BF)
    tail = ((cls, dq), (pulled, wide_ref[...]), (mixed_ref[...], d_wide), (ctx_ref[...], datt.astype(BF)))
    for k, (a, b) in enumerate(tail):
        place.put((tiles + k) * width, mm_tn(a, b).astype(BF))
    loads[9].wait()
    for k in range(tiles):
        place.put(k * width, mm_tn(act_ref[:, k * width : (k + 1) * width], low_ref[...]).astype(BF))
    place.finish()
    for copy in left:
        copy.wait()


def turn(top_args, y, kept, w, hat2, rstd2, act, spans, sents):
    rows, width = y.shape
    ff = act.shape[1]
    ctx, wide, key, prob, mixed = kept
    with_top = len(top_args) == 4
    ins = [(w["gain"], whole(w["gain"]))]
    ins += [(a, ANY) for a in (w["qkv"], y, wide, key, prob, mixed, ctx, hat2, rstd2, act)]
    blocks = ff // width + 4
    outs = [(shape((blocks * width // 2, width), BF), ANY)] * 2
    outs += [(hbm_shape((rows, width), BF), ANY)] + [(s, whole(s)) for s in (shape((8, width), F32),)]
    asked = sents * HEADS
    dims = [((width, 3 * width), BF), ((rows, width), BF), ((asked, width), BF), ((asked, width), BF), ((asked, rows), BF), ((asked, width), BF)]
    dims += [((sents, width), BF), ((rows, width), BF), ((rows, 128), F32), ((rows, ff), BF), ((rows, width), BF), ((blocks * width, width), BF)]
    scratch = [pltpu.VMEM(*d) for d in dims]
    scratch += [pltpu.SemaphoreType.DMA((13,)), pltpu.SemaphoreType.DMA((blocks,)), pltpu.SemaphoreType.DMA((3,))]
    flops = 2 * rows * width * (ff + 512)
    if with_top:
        index, near, other, pair = top_args
        every = shape((2 * near.shape[0], width), BF)
        ins += [(index, SMEM), (near, AS_IS), (other, AS_IS), (pair, whole(pair)), (w["out"], ANY)]
        ins += [(w[k], whole(w[k])) for k in ("b_in", "b_qv", "b_resid", "shift")] + [(w["in"], ANY), (w["back"], ANY)]
        outs += [(hbm_shape(every.shape, t), ANY) for t in (BF, F32)]
        dims = [((width, ff), BF), ((ff, width), BF), ((width, width), BF), (every.shape, F32), ((every.shape[0], 128), F32), (every.shape, BF), (every.shape, F32)]
        scratch += [pltpu.VMEM(*d) for d in dims]
        scratch += [pltpu.SemaphoreType.DMA((every.shape[0] // sents,))]
        flops += 4 * every.shape[0] * width * ff
    else:
        ins += [(a, whole(a)) for a in top_args]
    return kernel_call(functools.partial(turn_body, spans, sents, with_top), "turn", (1,), ins, outs, flops, scratch, vmem=VMEM + VMEM // 4)


VECTOR_ROWS = 128


def ff_back_body(gain_ref, shift_ref, low_hbm, hat1_hbm, rstd1_hbm, wback_hbm, slope_hbm, win_hbm, wout_hbm, ctx_hbm,
                 keep_hbm, send_hbm, datt_ref, dctx_ref, sums_ref, sumin_ref,
                 low_ref, hat1_ref, rstd1_ref, wback_ref, slope_ref, win_ref, wout_ref, ctx_ref, nlow_ref, dhidden_ref, block, got, sent):
    rows, width = low_ref.shape
    ff = slope_ref.shape[1]
    tiles = ff // width
    loads = [(low_hbm, low_ref)]
    for t in range(tiles):
        part = slice(t * width, (t + 1) * width)
        loads += [(wback_hbm.at[0, part], wback_ref.at[part]), (slope_hbm.at[:, part], slope_ref.at[:, part])]
    loads.insert(3, (hat1_hbm, hat1_ref))
    loads += [(win_hbm.at[0], win_ref), (rstd1_hbm, rstd1_ref), (wout_hbm.at[0], wout_ref), (ctx_hbm, ctx_ref)]
    loads = stream_in(loads, got)
    place = Halves(keep_hbm, send_hbm, block, sent)
    gain, shift = gain_ref[0:1, :width], shift_ref[0:1, :width]
    hat1_load = loads.pop(3)
    loads[0].wait()
    for t in range(tiles):
        part = slice(t * width, (t + 1) * width)
        loads[1 + 2 * t].wait()
        loads[2 + 2 * t].wait()
        dhidden = (mm_nt(low_ref[...], wback_ref[part]) * slope_ref[:, part].astype(F32)).astype(BF)
        dhidden_ref[:, part] = dhidden
        if t == 0:
            hat1_load.wait()
            nlow_ref[...] = (hat1_ref[...].astype(F32) * gain + shift).astype(BF)
        sumin_ref[:, part] = rowsum(dhidden)
        place.put(t * width, mm_tn(nlow_ref[...], dhidden).astype(BF))
    for load in loads[1 + 2 * tiles :]:
        load.wait()
    sums_ref[...] = jnp.zeros_like(sums_ref)
    for r in range(0, rows, STEP):
        r = slice(r, r + STEP)
        dnormed = low_ref[r].astype(F32) + mm_nt(dhidden_ref[r], win_ref[...])
        hat1 = hat1_ref[r].astype(F32)
        datt = ln_back(dnormed, hat1, rstd1_ref[r, 0:1], gain)
        low = datt.astype(BF)
        datt_ref[r] = low
        dctx_ref[r] = mm_nt(low, wout_ref[...]).astype(BF)
        sums_ref[0:1] += rowsum(datt)
        sums_ref[1:2] += rowsum(dnormed * hat1)
        sums_ref[2:3] += rowsum(dnormed)
    place.put(ff, mm_tn(ctx_ref[...], datt_ref[...]).astype(BF))
    place.finish()


def ff_back(low, hat1, rstd1, slope, ctx, w):
    rows, width = low.shape
    ff = slope.shape[1]
    ins = [(w["gain"], whole(w["gain"])), (w["shift"], whole(w["shift"]))]
    ins += [(a, ANY) for a in (low, hat1, rstd1, w["back"], slope, w["in"], w["out"], ctx)]
    half = (ff + width) // 2
    outs = [(shape((half, width), BF), ANY)] * 2
    outs += [(s, whole(s)) for s in (shape((rows, width), BF), shape((rows, width), BF), shape((8, width), F32), shape((1, ff), F32))]
    scratch = [((rows, width), BF), ((rows, width), BF), ((rows, 128), F32), ((ff, width), BF), ((rows, ff), BF), ((width, ff), BF), ((width, width), BF), ((rows, width), BF)]
    scratch += [((rows, width), BF), ((rows, ff), BF), ((ff + width, width), BF)]
    scratch = [pltpu.VMEM(d, t) for d, t in scratch]
    scratch += [pltpu.SemaphoreType.DMA((6 + 2 * (ff // width),)), pltpu.SemaphoreType.DMA((8,))]
    return kernel_call(ff_back_body, "layer0_ff_back", (1,), ins, outs, 2 * rows * width * (3 * ff + 2 * width), scratch)


def attention_back_body(qkv_ref, prob_ref, dctx_ref, short_ref, long_ref, sums1_ref, sums2_ref, sumin_ref, dqkv_ref, keep_hbm, send_hbm, acc, sums, block, sent):
    step = pl.program_id(0)
    x = jnp.where(step == 0, short_ref[...], long_ref[...])
    rows, width = x.shape
    pair = 2 * width // HEADS
    first = first_head(width)
    scale = 1.0 / math.sqrt(width // HEADS)

    @pl.when(step == 0)
    def _():
        acc[...] = jnp.zeros_like(acc)
        sums[...] = jnp.zeros_like(sums)

    pairs = range(HEADS // 2)
    c = [[slice(m * width + p * pair, m * width + (p + 1) * pair) for m in range(3)] for p in pairs]
    for b in range(rows // BLOCK):
        r = slice(b * BLOCK, (b + 1) * BLOCK)
        dd = [halves(dctx_ref[r, c[p][0]], first) for p in pairs]
        dprob = [mm_nt(qkv_ref[r, c[p][2]], dd[p]) for p in pairs]
        dscore = []
        for p in pairs:
            prob = prob_ref[b, p].astype(F32)
            dscore.append((prob * (dprob[p] - jnp.sum(prob * dprob[p], 0, keepdims=True)) * scale).astype(BF))
        dv = [mm(prob_ref[b, p], dd[p]).astype(BF) for p in pairs]
        dk = [mm(dscore[p], halves(qkv_ref[r, c[p][0]], first)).astype(BF) for p in pairs]
        dq = [join_halves(mm_tn(dscore[p], qkv_ref[r, c[p][1]]), first).astype(BF) for p in pairs]
        dqkv_ref[r] = jnp.concatenate(dq + dk + dv, 1)
    dqkv = dqkv_ref[...]
    acc[...] += mm_tn(x, dqkv)
    sums[0:1] += rowsum(dqkv)

    @pl.when(step == pl.num_programs(0) - 1)
    def _():
        place = Halves(keep_hbm, send_hbm, block, sent)
        for m in range(3):
            place.put(m * width, acc[:, m * width : (m + 1) * width].astype(BF))
        rows_of = [sums[0:1, :width], sums[0:1, 2 * width :]]
        for k in range(3):
            rows_of += [sums1_ref[k : k + 1], sums2_ref[k : k + 1]]
        rows_of += [sumin_ref[:, k * width : (k + 1) * width] for k in range(sumin_ref.shape[1] // width)]
        rows_of += [sums2_ref[3:4], jnp.zeros((3, width), F32)]
        rows_of += [jnp.zeros((VECTOR_ROWS - 16, width), F32)]
        place.put(3 * width, jnp.concatenate(rows_of, 0).astype(BF))
        place.finish()


def attention_back(qkv, prob, dctx, sums1, sums2, sumin, short, long):
    rows, width = dctx.shape
    per = STEP // BLOCK
    ins = [(qkv, by_rows(3 * width)), (prob, pl.BlockSpec((per,) + prob.shape[1:], lambda i: (i, 0, 0, 0))), (dctx, by_rows(width))]
    ins += from_buckets(short, long) + [(a, whole(a)) for a in (sums1, sums2, sumin)]
    total = 3 * width + VECTOR_ROWS
    outs = [(shape((rows, 3 * width), BF), by_rows(3 * width))] + [(shape((total // 2, width), BF), ANY)] * 2
    scratch = [pltpu.VMEM((width, 3 * width), F32), pltpu.VMEM((8, 3 * width), F32), pltpu.VMEM((total, width), BF), pltpu.SemaphoreType.DMA((8,))]
    flops = 2 * rows * width * (3 * width + 10 * BLOCK)
    return kernel_call(attention_back_body, "layer0_attention_back", (rows // STEP,), ins, outs, flops, scratch)


def input_back_body(dqkv_ref, datt_ref, wqkv_ref, short_ref, long_ref):
    dx = datt_ref[...].astype(F32) + mm_nt(dqkv_ref[...], wqkv_ref[...])

    @pl.when(pl.program_id(0) == 0)
    def _():
        short_ref[...] = dx

    @pl.when(pl.program_id(0) > 0)
    def _():
        long_ref[...] = dx


def input_back(dqkv, datt, w, cut):
    rows, width = datt.shape
    ins = [(dqkv, by_rows(3 * width)), (datt, by_rows(width)), layer_of(w["qkv"], 0)]
    outs = [
        (shape((cut, width), F32), pl.BlockSpec((STEP, width), lambda i: (0, 0))),
        (shape((rows - cut, width), F32), pl.BlockSpec((STEP, width), lambda i: (jnp.maximum(i - 1, 0), 0))),
    ]
    return kernel_call(input_back_body, "layer0_input_back", (rows // STEP,), ins, outs, 2 * rows * width * 3 * width)


def unpack_call(body, name, bit, grid, ins, outs, aliases, size):
    return pl.pallas_call(
        body,
        grid_spec=pltpu.PrefetchScalarGridSpec(
            num_scalar_prefetch=1,
            grid=grid,
            in_specs=[s for _, s in ins],
            out_specs=[s for _, s in outs],
        ),
        out_shape=[s for s, _ in outs],
        input_output_aliases=aliases,
        compiler_params=pltpu.CompilerParams(vmem_limit_bytes=VMEM),
        cost_estimate=pl.CostEstimate(flops=0, bytes_accessed=size, transcendentals=0),
        name=name,
    )(bit, *[hbm(a) if s is ANY else a for a, s in ins])


def in_order(bit_ref, mine_ref, theirs_ref):
    mine, theirs = mine_ref[...].astype(F32), theirs_ref[...].astype(F32)
    low = bit_ref[0] == 0
    return jnp.where(low, mine, theirs), jnp.where(low, theirs, mine)


def unpack_first(bit, pair, back):
    _, ff, width = back.shape
    steps = ff // width
    block = pl.BlockSpec((width, width), lambda j, bit: (j, 0))

    def body(bit_ref, mine_ref, theirs_ref, _, qkv_ref, out_ref, back_ref):
        low, high = in_order(bit_ref, mine_ref, theirs_ref)
        back_ref[...] = low
        step = pl.program_id(0)

        @pl.when(step < steps - 1)
        def _():
            qkv_ref[...] = high

        @pl.when(step == steps - 1)
        def _():
            out_ref[...] = high

    outs = [
        (shape((2, width, 3 * width), F32), pl.BlockSpec((None, width, width), lambda j, bit: (1, 0, jnp.minimum(j, 2)))),
        (shape((2, width, width), F32), pl.BlockSpec((None, width, width), lambda j, bit: (1, 0, 0))),
        (shape(back.shape, F32), pl.BlockSpec((None, width, width), lambda j, bit: (0, j, 0))),
    ]
    ins = [(pair[0], block), (pair[1], block), (back, ANY)]
    return unpack_call(body, "unpack_first", bit, (steps,), ins, outs, {3: 2}, 12 * steps * width * width)


def unpack_second(bit, pair, gin, gout):
    _, width, ff = gin.shape
    rows = width // 2
    half = pair[0].shape[0] // rows
    count = 2 * ff // width
    block = [pl.BlockSpec((rows, width), lambda j, bit, low=low: (jnp.where((bit[0] == 0) == low, jnp.minimum(j, half - 1), jnp.maximum(j - half, 0)), 0)) for low in (True, False)]

    def body(bit_ref, mine_ref, theirs_ref, _, __, in_ref, out_ref):
        step = pl.program_id(0)
        mine = (step < half) == (bit_ref[0] == 0)
        value = jnp.where(mine, mine_ref[...], theirs_ref[...]).astype(F32)

        @pl.when(step < count)
        def _():
            in_ref[...] = value

        @pl.when(step >= count)
        def _():
            out_ref[...] = value

    def at_in(j, bit):
        j = jnp.minimum(j, count - 1)
        return 0, j % 2, j // 2

    outs = [
        (shape(gin.shape, F32), pl.BlockSpec((None, rows, width), at_in)),
        (shape(gout.shape, F32), pl.BlockSpec((None, rows, width), lambda j, bit: (0, jnp.maximum(j - count, 0), 0))),
    ]
    ins = [(pair[0], block[0]), (pair[1], block[1]), (gin, ANY), (gout, ANY)]
    return unpack_call(body, "unpack_second", bit, (2 * half,), ins, outs, {3: 0, 4: 1}, 12 * half * rows * width)


def third_half_body(bit_ref, half_ref, _, qkv_hbm, vec_ref, wide, sems):
    rows, width = wide.shape
    wide[...] = half_ref[...].astype(F32)
    vec_ref[...] = wide[rows - VECTOR_ROWS : rows - VECTOR_ROWS + 16]
    cut = rows - width

    def copies(parts):
        return [
            pltpu.make_async_copy(
                wide.at[start : start + size], qkv_hbm.at[0, at : at + size, third * width : (third + 1) * width], sems.at[k]
            )
            for k, (start, size, at, third) in enumerate(parts)
        ]

    for lower, parts in ((True, ((0, width, 0, 0), (width, cut, 0, 1))), (False, ((0, width - cut, cut, 1), (width - cut, width, 0, 2)))):

        @pl.when((bit_ref[0] == 0) == lower)
        def _(parts=parts):
            for copy in copies(parts):
                copy.start()
            for copy in copies(parts):
                copy.wait()


def third_half(bit, half, qkv):
    rows, width = half.shape
    vec = shape((16, width), F32)
    ins = [(bit, SMEM), (half, whole(half)), (qkv, ANY)]
    outs = [(hbm_shape(qkv.shape, F32), ANY), (vec, whole(vec))]
    scratch = [pltpu.VMEM((rows, width), F32), pltpu.SemaphoreType.DMA((2,))]
    return kernel_call(third_half_body, "unpack_third", (1,), ins, outs, 0, scratch, {2: 0})


def unpack_vectors(bit, mine, theirs, sums, sumin):
    width, ff = sums.shape[1], sumin.shape[1]

    def body(bit_ref, mine_ref, theirs_ref, sums_ref, sumin_ref, bqv_ref, bresid_ref, gain_ref, shift_ref, bin_ref):
        value = jnp.where(bit_ref[0] == 0, theirs_ref[...], mine_ref[...])
        for ref, lower, upper in (
            (bqv_ref, (value[0:1], value[1:2]), (value[12:13], sums_ref[6:7])),
            (bresid_ref, (value[2:3], value[3:4]), (sums_ref[0:1], sums_ref[1:2])),
            (gain_ref, (value[4:5], value[5:6]), (sums_ref[2:3], sums_ref[3:4])),
            (shift_ref, (value[6:7], value[7:8]), (sums_ref[4:5], sums_ref[5:6])),
        ):
            for level, both in enumerate((lower, upper)):
                for k in range(2):
                    ref[level : level + 1, k * width : (k + 1) * width] = both[k]
        for k in range(ff // width):
            bin_ref[0:1, k * width : (k + 1) * width] = value[8 + k : 9 + k]
        bin_ref[1:2, :] = sumin_ref[...]

    outs = [(s, whole(s)) for s in [shape((2, 2 * width), F32)] * 4 + [shape((2, ff), F32)]]
    ins = [(bit, SMEM)] + [(a, whole(a)) for a in (mine, theirs, sums, sumin)]
    return kernel_call(body, "unpack_vectors", (1,), ins, outs, 0)


def top_rows(attended, pair_index, weights):
    w_qkv, b_qv, w_out, b_resid, gain, shift, w_in, b_in, w_back = weights
    rows, width = attended.shape
    pairs = rows // 2
    hat1, rstd1 = ln_stats(attended.astype(F32))
    normed = hat1 * gain[:width] + shift[:width]
    normed_low = normed.astype(BF)
    activ, slope = gelu_pair(mm(normed_low, w_in) + b_in)
    activ = activ.astype(BF)
    hat2, rstd2 = ln_stats(normed + mm(activ, w_back) + b_resid[width:])
    pooled = hat2 * gain[width:] + shift[width:]
    radius = lax.rsqrt(jnp.sum(pooled * pooled, -1, keepdims=True) + unit_eps)
    unit = pooled * radius
    unit_low = unit.astype(BF)
    src, tgt = unit_low[:pairs], unit_low[pairs:]
    positive = (pair_index[:, None] == jnp.arange(pairs)[None, :]).astype(F32)
    logits = logit_scale * (mm_nt(src, tgt) - margin * positive)

    def soft(axis):
        powers = jnp.exp(logits - jnp.max(logits, axis, keepdims=True))
        return powers / jnp.sum(powers, axis, keepdims=True)

    dscore = (0.5 * logit_scale * (soft(1) + soft(0) - 2.0 * positive)).astype(BF)
    dunit = jnp.concatenate([mm(dscore, tgt), mm_tn(dscore, src)], 0)
    dy = radius * (dunit - unit * jnp.sum(dunit * unit, -1, keepdims=True))
    dg2, dc2 = colsum(dy * hat2), colsum(dy)
    dmixed = ln_back(dy, hat2, rstd2, gain[width:])
    dmixed_low = dmixed.astype(BF)
    dhidden = (mm_nt(dmixed_low, w_back) * slope).astype(BF)
    dnormed = dmixed + mm_nt(dhidden, w_in)
    dg1, dc1 = colsum(dnormed * hat1), colsum(dnormed)
    datt = ln_back(dnormed, hat1, rstd1, gain[:width])
    datt_low = datt.astype(BF)
    dctx = mm_nt(datt_low, w_out).astype(BF)
    grads = (mm_tn(normed_low, dhidden), mm_tn(activ, dmixed_low))
    vectors = dict(
        bv=colsum(dctx),
        b_resid=jnp.concatenate([colsum(datt), colsum(dmixed)]),
        gain=jnp.concatenate([dg1, dg2]),
        shift=jnp.concatenate([dc1, dc2]),
        b_in=colsum(dhidden),
    )
    return datt, dctx, grads, vectors


def per_device(short_tokens, long_tokens, short_len, long_len, pair_index, *params):
    n = lax.axis_size("stream") * lax.axis_size("dp")
    index = lax.axis_index("stream") * lax.axis_size("dp") + lax.axis_index("dp")
    width = short_tokens.shape[-1]
    spans = (short_tokens.shape[2], long_tokens.shape[2])
    counts = (short_tokens.shape[1], long_tokens.shape[1])
    sents = sum(counts)
    w_qkv, b_qv, w_out, b_resid, gain, shift, w_in, b_in, w_back = params
    w_qkv, b_qv, w_out, b_resid, gain, shift, w_in, b_in, w_back = (hbm(p) for p in (w_qkv, b_qv, w_out, b_resid, gain, shift, w_in, b_in, w_back))
    w = dict(qkv=w_qkv, b_qv=b_qv, out=w_out, b_resid=b_resid, gain=gain, shift=shift, b_in=b_in, back=w_back) | {"in": w_in}
    short, long = hbm(short_tokens.reshape(-1, width)), hbm(long_tokens.reshape(-1, width))
    lens = jnp.concatenate([short_len.reshape(-1), long_len.reshape(-1)])
    lens_wide = jnp.repeat(lens, HEADS)[:, None]

    outs = forward(short, long, lens, lens_wide, w, spans, counts[0], sents)
    y, qkv, prob, ctx, hat1, rstd1, act, slope, hat2, rstd2 = (hbm(a) for a in outs[:10])
    sent, *kept = outs[10:]
    one_kernel = n * sents <= 512
    if one_kernel:
        top_args = (index.reshape(1).astype(jnp.int32), *gather_near(sent, n), pair_index[None, :])
    else:
        datt, dctx, top_g, top_vec = top_rows(gather_rows(sent, n), pair_index, tuple(p[1] for p in params))
        top_args = tuple(lax.dynamic_slice_in_dim(v, index * sents, sents, 0) for v in (datt, dctx))
    bits = my_bits(n)
    bit = bits[0].reshape(1).astype(jnp.int32)

    keep, send, dlow, sums2, *top_kept = turn(top_args, y, [hbm(a) for a in kept], w, hat2, rstd2, act, spans, sents)
    lanes = {"1": Lane(sum_steps(keep, send, n, bits), n)}
    v = {}

    def ff():
        return (dlow, hat1, rstd1, slope, ctx), lambda *a: ff_back(*a, w)

    def attention():
        return (qkv, prob, v["dctx"], v["sums1"], sums2, v["sumin"]), lambda *a: attention_back(*a, short, long)

    def input_():
        return (v["dqkv"], v["datt"]), lambda *a: input_back(*a, w, counts[0] * spans[0])

    def top():
        if one_kernel:
            return [hbm(a) for a in top_kept], lambda *a: top_grads(*a, w)
        return (), None

    def unpack1():
        return (lanes["1"].result, v["gback"]), lambda *a: unpack_first(bit, *a)

    def unpack2():
        return (lanes["2"].result, v["gin"], v["gout"]), lambda *a: unpack_second(bit, *a)

    def unpack3():
        return (lanes["3"].ask[0], v["gqkv"]), lambda *a: third_half(bit, *a)

    work = dict(unpack3=unpack3, ff=ff, attention=attention, input=input_, top=top, unpack1=unpack1, unpack2=unpack2)
    gives = dict(
        ff=("keep", "send", "datt", "dctx", "sums1", "sumin"), attention=("dqkv", "keep", "send"), input=("dshort", "dlong"),
        top=("gin", "gback", "top_sums", "top_sumin"), unpack1=("gqkv", "gout", "gback"), unpack2=("gin", "gout"), unpack3=("gqkv", "vec"),
    )
    if not one_kernel:
        v["gin"], v["gback"] = (jnp.stack([g, g]) for g in top_g)
        rows_of = [top_vec[k].reshape(2, width) for k in ("b_resid", "gain", "shift")]
        v["top_sums"] = jnp.concatenate(rows_of + [top_vec["bv"][None], jnp.zeros((1, width), F32)], 0)
        v["top_sumin"] = top_vec["b_in"][None]
    for moved, piece in SCHEDULE:
        if piece[:6] == "unpack":
            while lanes[piece[6:]].left > (piece == "unpack3"):
                stage(lanes.values())
        args, body = work[piece]() if piece else ((), None)
        v.update(zip(gives.get(piece, ()), stage([lanes[k] for k in moved], body, args)))
        if piece in ("ff", "attention"):
            lanes["2" if piece == "ff" else "3"] = Lane(sum_steps(v["keep"], v["send"], n, bits), n)
    g_qkv, vec = third_half(1 - bit, lanes["3"].result[1], v["gqkv"])
    g_bqv, g_bresid, g_gain, g_shift, g_bin = unpack_vectors(bit, v["vec"], vec, v["top_sums"], v["top_sumin"])
    g_out, g_in, g_back, dshort, dlong = (v[k] for k in ("gout", "gin", "gback", "dshort", "dlong"))
    outs = (g_qkv, g_bqv, g_out, g_bresid, g_gain, g_shift, g_in, g_bin, g_back)
    return outs + (dshort.reshape((1, counts[0], spans[0], width)), dlong.reshape((1, counts[1], spans[1], width)))


def solution(mesh):
    split = P("stream", "dp", None, None)
    in_specs = (split, split, P("stream", "dp"), P("stream", "dp")) + (P(),) * 10
    out_specs = (P(),) * 9 + (split, split)
    return jax.shard_map(per_device, mesh=mesh, in_specs=in_specs, out_specs=out_specs, check_vma=False)
```
